512 devices in a mesh: dp: 16 (over z), expert: 32 (over x, y, core).
Axes of the slice: x: 4, y: 4, z: 16, core: 2. Of those that a mesh axis runs over, the one named last changes fastest.
Arguments:
- tokens: bfloat16 [65536, 1024], P(('dp', 'expert')), may hold values from -6 to 6
- upstream: bfloat16 [65536, 1024], P(('dp', 'expert')), may hold values from -6 to 6
- expert_ids: int32 [65536, 8], P(('dp', 'expert')), may hold values from 0 to 63, all different within a row; in each aligned block of 128 rows (0 to 127, 128 to 255, ...) at most 20 rows name the same one
- gates: float32 [65536, 8], P(('dp', 'expert')), may hold values from 0.02 to 0.5
- expert_weights: bfloat16 [64, 3, 1024, 384], P('expert', None, 'dp'), may hold values from -0.1875 to 0.1875
- router_weight: bfloat16 [1024, 64], replicated, may hold values from -0.1875 to 0.1875
Outputs:
- token_grad: bfloat16 [65536, 1024], P(('dp', 'expert'))
- router_grad: float32 [1024, 64], P('dp')
The draws below stay inside these ranges and needn't reach their ends.
Inputs may be any that keep to these rules, and one draw needn't show every extreme that they name: `expert_ids`: within each device's aligned block of 128 rows no expert is named by more than 20 rows.
All inputs are finite; a program needn't handle non-finite values.
Results may differ from the reference program's by a relative error of at most 0.023.
Values may be sent and summed in bfloat16 or wider, within the bound.
No kernel may reach another device: no remote copies, remote signals or barrier semaphores. Data moves between devices by JAX's collectives and lax.ppermute only.
A program may use at most 64 MiB of HBM per device.

```python
import math
import jax
import jax.numpy as jnp
import numpy as np
from jax import lax

D = 1024
FF = 384
TOP = 8
TOK_DEV = 128
EXPERTS = 64
CAP = 20
TOKENS = 65536


def shard_levels(stream_key, extent, pieces, smallest, largest):
    level, own = 1.0, jax.random.fold_in(stream_key, 6)
    for axis_at, parts in pieces:
        steps = jnp.exp(jax.random.uniform(jax.random.fold_in(own, axis_at), (parts,), jnp.float32, smallest / len(pieces), largest / len(pieces)))
        level = level * jnp.repeat(steps, extent[axis_at] // parts).reshape([-1 if axis == axis_at else 1 for axis in range(len(extent))])
    return level


def assign_block(rng, own, number, rows, amount, top, reach, skew):
    sequence = jax.random.permutation(rng, amount)
    crowded, common = portions_of(amount, rows * top, reach, skew, True), portions_of(amount, rows * top, reach, skew, False)
    places = jnp.arange(amount)

    def named(lengths, rotation):
        used = int((lengths > 0).sum())
        fixed = max(1, used // 4)
        passed = fixed + (places - fixed + rotation * (used - fixed)) % max(1, amount - fixed)
        return jnp.zeros((amount,), jnp.int32).at[sequence[jnp.where(places < fixed, places, passed)]].set(jnp.asarray(lengths, jnp.int32))

    lengths = jnp.where(number % 4 == 0, named(crowded, number // 4), named(common, number - number // 4 - 1))
    mixed = jax.random.permutation(jax.random.fold_in(own, 3), amount)
    source_of, taker = mixed[0:amount // 2 * 2:2], mixed[1:amount // 2 * 2:2]
    slack = jnp.minimum(lengths[source_of] - 1, reach - lengths[taker]) // 2
    slack = jnp.where((source_of == sequence[0]) | (taker == sequence[0]) | (lengths[taker] == 0), 0, jnp.maximum(slack, 0))
    passed = jax.random.randint(jax.random.fold_in(own, 4), (amount // 2,), 0, 1 << 20) % (slack + 1)
    lengths = lengths.at[source_of].add(-passed).at[taker].add(passed)
    labels = jnp.searchsorted(jnp.cumsum(lengths), jnp.arange(rows * top), side="right").astype(jnp.int32)
    grid = labels.reshape(top, rows).T
    grid = grid[jax.random.permutation(jax.random.fold_in(own, 1), rows)]
    rotation = jax.random.randint(jax.random.fold_in(own, 2), (rows, 1), 0, top)
    return jnp.take_along_axis(grid, (jnp.arange(top)[None, :] + rotation) % top, axis=1)


def portions_of(amount, total, bound, skew, full):
    weights = [(1 << 20) // math.isqrt(rank ** skew) + 1 for rank in range(1, amount + 1)]
    largest = bound if full else min(bound, max(-(-total // amount), total * weights[0] // sum(weights)))
    least = 1 if total - largest >= amount - 1 else 0
    given, rest = [largest] + [least] * (amount - 1), total - largest - least * (amount - 1)
    while rest > 0:
        candidates = [i for i in range(1, amount) if given[i] < largest] or [i for i in range(1, amount) if given[i] < bound]
        mass, left = sum([weights[i] for i in candidates]), rest
        for i in candidates:
            addition = min(bound - given[i], max(1, left * weights[i] // mass), rest)
            given[i] = given[i] + addition
            rest = rest - addition
    return np.array(given)


def normal_values(own_key, dims, spread, limit, cuts=(), kind=jnp.bfloat16):
    entries = jax.random.normal(own_key, dims, jnp.float32) * spread
    if len(cuts) > 0:
        entries = shard_levels(own_key, dims, cuts, -0.22, 0.18) * entries
    return jnp.clip(entries, min=-limit, max=limit).astype(kind)


def setup_inputs(seed: int = 0) -> dict:
    keys = jax.random.split(jax.random.key(seed), 7)
    tokens = normal_values(keys[0], (TOKENS, D), 1.0, 6.0, ((0, 512),))
    upstream = normal_values(keys[1], (TOKENS, D), 1.0, 6.0, ((0, 512),))
    expert_ids_keys = jax.random.split(jax.random.fold_in(keys[2], 1), TOKENS // TOK_DEV)
    expert_ids_turns = jax.random.permutation(jax.random.fold_in(keys[2], 3), TOKENS // TOK_DEV)
    expert_ids = jax.vmap(lambda own, number: assign_block(jax.random.fold_in(keys[2], 2), own, number, TOK_DEV, EXPERTS, TOP, CAP, 2))(expert_ids_keys, expert_ids_turns).reshape((TOKENS, TOP))
    gates = jnp.clip(jnp.exp(math.log(0.5) - 3.218876 * jax.random.uniform(keys[3], (TOKENS, TOP), jnp.float32) ** shard_levels(keys[3], (TOKENS, TOP), ((0, 512),), -0.2, 0.2)), 0.02, 0.5)
    expert_weights = normal_values(keys[4], (EXPERTS, 3, D, FF), D ** -0.5, 0.1875, ((0, 32), (2, 16)))
    router_weight = normal_values(keys[5], (D, EXPERTS), D ** -0.5, 0.1875)
    return dict(tokens=tokens, upstream=upstream, expert_ids=expert_ids, gates=gates, expert_weights=expert_weights, router_weight=router_weight)


block_rows = 1024


def expert_rows(inputs, grads, matrices):
    w_gate = matrices[0]
    w_up = matrices[1]
    w_down = matrices[2]
    pre_gate = jnp.dot(inputs, w_gate, preferred_element_type=jnp.float32)
    pre_up = jnp.dot(inputs, w_up, preferred_element_type=jnp.float32)
    sigma = jax.nn.sigmoid(pre_gate)
    active = pre_gate * sigma
    hidden = (active * pre_up).astype(jnp.bfloat16)
    hidden_grad = jnp.dot(grads, w_down, preferred_element_type=jnp.float32)
    gate_grad = jnp.sum(hidden_grad * hidden.astype(jnp.float32), axis=-1).astype(jnp.bfloat16)
    gate_pre = (hidden_grad * pre_up * sigma * (1.0 + pre_gate * (1.0 - sigma))).astype(jnp.bfloat16)
    up_pre = (hidden_grad * active).astype(jnp.bfloat16)
    row_grad = jnp.dot(gate_pre, w_gate.T, preferred_element_type=jnp.float32)
    row_grad = row_grad + jnp.dot(up_pre, w_up.T, preferred_element_type=jnp.float32)
    return row_grad.astype(jnp.bfloat16), gate_grad


def reference(tokens, upstream, expert_ids, gates, expert_weights, router_weight):
    total = TOKENS * TOP
    flat = expert_ids.reshape(-1).astype(jnp.int32)
    order = jnp.argsort(flat, stable=True).astype(jnp.int32)
    counts = jnp.bincount(flat, length=EXPERTS).astype(jnp.int32)
    starts = (jnp.cumsum(counts) - counts).astype(jnp.int32)
    zero_row = jnp.zeros((1, D), jnp.bfloat16)
    padded_x = jnp.concatenate([tokens, zero_row], axis=0)
    padded_dy = jnp.concatenate([upstream, zero_row], axis=0)
    padded_gate = jnp.concatenate([gates.reshape(-1), jnp.zeros((1,), jnp.float32)], axis=0)

    def per_expert(expert, carry):
        expert = jnp.asarray(expert).astype(jnp.int32)
        matrices = lax.dynamic_index_in_dim(expert_weights, expert, 0, keepdims=False)
        begin = starts[expert]
        count = counts[expert]

        def per_block(block_index, inner):
            combined, gate_grads = inner
            block_index = jnp.asarray(block_index).astype(jnp.int32)
            position = (begin + block_index * block_rows + jnp.arange(block_rows, dtype=jnp.int32)).astype(jnp.int32)
            valid = position < begin + count
            safe = jnp.minimum(position, total - 1).astype(jnp.int32)
            slot = jnp.where(valid, order[safe], total).astype(jnp.int32)
            owner = jnp.where(valid, slot // TOP, TOKENS).astype(jnp.int32)
            row_grad, gate_grad = expert_rows(padded_x[owner], padded_dy[owner], matrices)
            weight = padded_gate[slot]
            combined = combined.at[owner].add(weight[:, None] * row_grad.astype(jnp.float32), mode="drop")
            gate_grads = gate_grads.at[slot].set(gate_grad, mode="drop")
            return combined, gate_grads

        blocks = ((count + block_rows - 1) // block_rows).astype(jnp.int32)
        return lax.fori_loop(jnp.int32(0), blocks, per_block, carry)

    start_state = (jnp.zeros((TOKENS, D), jnp.float32), jnp.zeros((total,), jnp.bfloat16))
    combined, gate_grads = lax.fori_loop(0, EXPERTS, per_expert, start_state)
    gate_grad = gate_grads.reshape(TOKENS, TOP).astype(jnp.float32)
    weighted = jnp.sum(gates * gate_grad, axis=1, keepdims=True)
    logit_grad = (gates * (gate_grad - weighted)).astype(jnp.bfloat16)
    columns = jnp.arange(EXPERTS, dtype=jnp.int32)
    match = expert_ids[:, :, None] == columns[None, None, :]
    full_logit_grad = jnp.sum(jnp.where(match, logit_grad[:, :, None], jnp.zeros((), jnp.bfloat16)), axis=1).astype(jnp.bfloat16)
    token_grad = (combined + jnp.dot(full_logit_grad, router_weight.T, preferred_element_type=jnp.float32)).astype(jnp.bfloat16)
    router_grad = jnp.dot(tokens.T, full_logit_grad, preferred_element_type=jnp.float32)
    return token_grad, router_grad
```

```python
import functools

import jax
import jax.numpy as jnp
import numpy as np
from jax import lax
from jax.experimental import pallas as pl
from jax.experimental.pallas import tpu as pltpu
from jax.sharding import PartitionSpec as P

F32 = jnp.float32
BF = jnp.bfloat16
CAP = 20
SLOTS = 2 * CAP
HOSTS = 32
ROWS = HOSTS * SLOTS
VMEM_LIMIT = 56 * 1024 * 1024


def slot_table():
    which = [0] * 16 + [1] * 16 + [0] * 4 + [1] * 4
    rank = list(range(16)) + list(range(16)) + list(range(16, 20)) + list(range(16, 20))
    return np.array(which), np.array(rank)


WHICH, RANK = slot_table()


def strict(rows, cols, upper):
    a = lax.broadcasted_iota(jnp.int32, (rows, cols), 0)
    b = lax.broadcasted_iota(jnp.int32, (rows, cols), 1)
    return jnp.where((a < b) if upper else (a > b), 1.0, 0.0).astype(BF)


def host_block(first, second):
    width = first.shape[-1]
    row = lax.broadcasted_iota(jnp.int32, (16, width), 0).astype(F32) + 1.0
    row8 = lax.broadcasted_iota(jnp.int32, (8, width), 0)
    mixed = jnp.where(
        row8 < 4, jnp.broadcast_to(first, (8, width)), jnp.broadcast_to(second, (8, width))
    )
    late = (row8 + jnp.where(row8 < 4, 17, 13)).astype(F32)
    return jnp.concatenate(
        [
            jnp.where(jnp.broadcast_to(first, (16, width)) == row, 1.0, 0.0),
            jnp.where(jnp.broadcast_to(second, (16, width)) == row, 1.0, 0.0),
            jnp.where(mixed == late, 1.0, 0.0),
        ],
        axis=0,
    )


def dispatch_kernel(ids_ref, x_ref, out_ref, hot_ref):
    experts, tokens = 2 * HOSTS, x_ref.shape[0]
    column = lax.broadcasted_iota(jnp.int32, (experts, tokens), 0)
    member = jnp.zeros((experts, tokens), F32)
    for k in range(ids_ref.shape[0]):
        member += jnp.where(ids_ref[k : k + 1, :] == column, 1.0, 0.0)
    before = jnp.dot(member.astype(BF), strict(tokens, tokens, True), preferred_element_type=F32)
    order = jnp.where(member > 0.0, before + 1.0, 0.0)
    for pair in range(HOSTS // 2):
        blocks = [
            host_block(order[2 * h : 2 * h + 1], order[2 * h + 1 : 2 * h + 2])
            for h in (2 * pair, 2 * pair + 1)
        ]
        hot_ref[80 * pair : 80 * pair + 80, :] = jnp.concatenate(blocks, axis=0).astype(BF)

    def step(i, carry):
        at = pl.ds(pl.multiple_of(i * 320, 320), 320)
        out_ref[at, :] = jnp.dot(
            hot_ref[at, :], x_ref[...], preferred_element_type=F32
        ).astype(BF)
        return carry

    lax.fori_loop(0, ROWS // 320, step, 0)


def vmem():
    return pl.BlockSpec(memory_space=pltpu.VMEM)


def smem():
    return pl.BlockSpec(memory_space=pltpu.SMEM)


def dispatch(ids_t, values):
    return pl.pallas_call(
        dispatch_kernel,
        out_shape=jax.ShapeDtypeStruct((ROWS, values.shape[1]), BF),
        in_specs=[vmem(), vmem()],
        out_specs=vmem(),
        scratch_shapes=[pltpu.VMEM((ROWS, values.shape[0]), BF)],
        compiler_params=pltpu.CompilerParams(vmem_limit_bytes=VMEM_LIMIT),
        name="dispatch",
    )(ids_t, values)


def pieces(block):
    return tuple(
        jnp.concatenate(
            [
                block[16 * e : 16 * e + 16],
                block[40 + 16 * e : 56 + 16 * e],
                block[32:40],
                block[72:80],
            ],
            axis=0,
        )
        for e in (0, 1)
    )


def expert_kernel(
    host_ref, route_ref, x_ref, dy_ref, w_ref, rw_ref,
    out_ref, share_ref, gg_ref, gate_ref, order_ref,
    xe_ref, dye_ref, re_ref, hot_ref, gcol_ref,
):
    sources = route_ref.shape[0]
    pairs = sources // 2
    width = route_ref.shape[2]
    ff = w_ref.shape[2] // 3
    ids = route_ref[:, 0:8, :]
    gates = route_ref[:, 8:16, :]
    upper = strict(width, width, True)
    host = host_ref[0]
    row8 = lax.broadcasted_iota(jnp.int32, (8, width), 0)
    row16 = lax.broadcasted_iota(jnp.int32, (16, width), 0).astype(F32) + 1.0
    total = jnp.zeros((sources, width), F32)
    for p in range(pairs):
        xs = pieces(x_ref[80 * p : 80 * p + 80, :].astype(F32))
        ys = pieces(dy_ref[80 * p : 80 * p + 80, :].astype(F32))
        for e in (0, 1):
            xe_ref[e, 48 * p : 48 * p + 48, :] = xs[e].astype(BF)
            dye_ref[e, 48 * p : 48 * p + 48, :] = ys[e].astype(BF)
    for e in (0, 1):
        wanted = (2 * host + e).astype(F32)
        match = ids == wanted
        member = jnp.sum(jnp.where(match, 1.0, 0.0), axis=1)
        gate = jnp.sum(jnp.where(match, gates, 0.0), axis=1)
        before = jnp.dot(member.astype(BF), upper, preferred_element_type=F32)
        order = jnp.where(member > 0.0, before + 1.0, 0.0)
        gate_ref[e] = gate
        order_ref[e] = order
        if e == 0:
            late = jnp.where(row8 < 4, row8 + 17, -1).astype(F32)
        else:
            late = jnp.where(row8 < 4, -1, row8 + 13).astype(F32)
        for p in range(pairs):
            a, b = order[2 * p : 2 * p + 1], order[2 * p + 1 : 2 * p + 2]
            ga, gb = gate[2 * p : 2 * p + 1], gate[2 * p + 1 : 2 * p + 2]
            wide = lambda v, n: jnp.broadcast_to(v, (n, width))
            hot = jnp.concatenate(
                [
                    jnp.where(wide(a, 16) == row16, 1.0, 0.0),
                    jnp.where(wide(b, 16) == row16, 1.0, 0.0),
                    jnp.where(wide(a, 8) == late, 1.0, 0.0),
                    jnp.where(wide(b, 8) == late, 1.0, 0.0),
                ],
                axis=0,
            )
            weight = jnp.concatenate([wide(ga, 16), wide(gb, 16), wide(ga, 8), wide(gb, 8)], axis=0)
            hot_ref[48 * p : 48 * p + 48, :] = hot
            gcol_ref[48 * p : 48 * p + 48, :] = jnp.sum(hot * weight, axis=1, keepdims=True)
        pre = jnp.dot(xe_ref[e], w_ref[e, :, 0 : 2 * ff], preferred_element_type=F32)
        hidden_grad = jnp.dot(dye_ref[e], w_ref[e, :, 2 * ff :], preferred_element_type=F32)
        pre_gate, pre_up = pre[:, 0:ff], pre[:, ff:]
        sigma = jax.nn.sigmoid(pre_gate)
        active = pre_gate * sigma
        hidden = (active * pre_up).astype(BF).astype(F32)
        gg = jnp.sum(hidden_grad * hidden, axis=1, keepdims=True).astype(BF).astype(F32)
        gcol = gcol_ref[...]
        scaled = hidden_grad * gcol
        gate_pre = (scaled * pre_up * sigma * (1.0 + pre_gate * (1.0 - sigma))).astype(BF)
        up_pre = (scaled * active).astype(BF)
        row = lax.dot_general(
            jnp.concatenate([gate_pre, up_pre], axis=1),
            w_ref[e, :, 0 : 2 * ff],
            (((1,), (1,)), ((), ())),
            preferred_element_type=F32,
        )
        row = row + (gcol * gg) * rw_ref[e : e + 1, :]
        re_ref[e] = row.astype(BF)
        for p in range(pairs):
            hit = hot_ref[48 * p : 48 * p + 48, :] * gg[48 * p : 48 * p + 48]
            first = jnp.sum(hit[0:16], axis=0, keepdims=True) + jnp.sum(hit[32:40], axis=0, keepdims=True)
            second = jnp.sum(hit[16:32], axis=0, keepdims=True) + jnp.sum(hit[40:48], axis=0, keepdims=True)
            gg_ref[e, 2 * p : 2 * p + 1, :] = first
            gg_ref[e, 2 * p + 1 : 2 * p + 2, :] = second
        total = total + gate * gg_ref[e]
    share_ref[...] = total
    for p in range(pairs):
        r0 = re_ref[0, 48 * p : 48 * p + 48, :].astype(F32)
        r1 = re_ref[1, 48 * p : 48 * p + 48, :].astype(F32)
        out_ref[80 * p : 80 * p + 80, :] = jnp.concatenate(
            [
                r0[0:16], r1[0:16], r0[32:40] + r1[32:40],
                r0[16:32], r1[16:32], r0[40:48] + r1[40:48],
            ],
            axis=0,
        ).astype(BF)


def expert_rows(host, route, x_rows, dy_rows, weights, rw_rows):
    steps = 2
    sources = HOSTS // steps
    rows = ROWS // steps
    width = route.shape[2]
    model = x_rows.shape[1]
    compact = sources * 24
    dense = jax.ShapeDtypeStruct((2, HOSTS, width), F32)
    dense_spec = pl.BlockSpec((2, sources, width), lambda i: (0, i, 0))
    row_spec = pl.BlockSpec((rows, model), lambda i: (i, 0))
    return pl.pallas_call(
        expert_kernel,
        grid=(steps,),
        out_shape=(
            jax.ShapeDtypeStruct((ROWS, model), BF),
            jax.ShapeDtypeStruct((HOSTS, width), F32),
            dense, dense, dense,
        ),
        in_specs=[
            smem(),
            pl.BlockSpec((sources, 16, width), lambda i: (i, 0, 0)),
            row_spec, row_spec,
            pl.BlockSpec(weights.shape, lambda i: (0, 0, 0)),
            pl.BlockSpec(rw_rows.shape, lambda i: (0, 0)),
        ],
        out_specs=(
            row_spec,
            pl.BlockSpec((sources, width), lambda i: (i, 0)),
            dense_spec, dense_spec, dense_spec,
        ),
        scratch_shapes=[
            pltpu.VMEM((2, compact, model), BF),
            pltpu.VMEM((2, compact, model), BF),
            pltpu.VMEM((2, compact, model), BF),
            pltpu.VMEM((compact, width), F32),
            pltpu.VMEM((compact, 1), F32),
        ],
        compiler_params=pltpu.CompilerParams(vmem_limit_bytes=VMEM_LIMIT),
        name="expert_rows",
    )(host, route, x_rows, dy_rows, weights, rw_rows)


def router_kernel(shares_ref, gg_ref, gate_ref, order_ref, mask_ref, x_ref, part_ref, sum_ref, hot_ref):
    total = shares_ref[0:HOSTS, :]
    for h in range(1, HOSTS):
        total = total + shares_ref[HOSTS * h : HOSTS * h + HOSTS, :]
    sum_ref[...] = total
    logit = jnp.concatenate([gate_ref[e] * (gg_ref[e] - total) for e in (0, 1)], axis=0).astype(BF)
    for pair in range(HOSTS // 2):
        blocks = [
            host_block(order_ref[0, s : s + 1, :], order_ref[1, s : s + 1, :])
            for s in (2 * pair, 2 * pair + 1)
        ]
        hot_ref[80 * pair : 80 * pair + 80, :] = jnp.concatenate(blocks, axis=0).astype(BF)
    spread = lax.dot_general(
        logit, hot_ref[...], (((1,), (1,)), ((), ())), preferred_element_type=F32
    ) * mask_ref[...].astype(F32)
    lines = [jnp.sum(spread[32 * e : 32 * e + 32], axis=0, keepdims=True) for e in (0, 1)]
    lines = jnp.concatenate(lines + [jnp.zeros((6, ROWS), F32)], axis=0).astype(BF)
    part_ref[...] = jnp.dot(lines, x_ref[...], preferred_element_type=F32)


def router_part(shares, gg, gate, order, x_rows):
    slot = np.arange(ROWS)
    mask = np.concatenate(
        [
            (np.arange(HOSTS)[:, None] == slot[None, :] // SLOTS) & (WHICH[slot % SLOTS] == e)[None, :]
            for e in (0, 1)
        ],
        axis=0,
    )
    return pl.pallas_call(
        router_kernel,
        out_shape=(
            jax.ShapeDtypeStruct((8, x_rows.shape[1]), F32),
            jax.ShapeDtypeStruct((HOSTS, gg.shape[2]), F32),
        ),
        in_specs=[vmem()] * 6,
        out_specs=(vmem(), vmem()),
        scratch_shapes=[pltpu.VMEM((ROWS, gg.shape[2]), BF)],
        compiler_params=pltpu.CompilerParams(vmem_limit_bytes=VMEM_LIMIT),
        name="router_part",
    )(shares, gg, gate, order, jnp.asarray(mask.astype(np.float32), BF), x_rows)


def combine_kernel(host_ref, ids_ref, gates_ref, sum_ref, expand_ref, rank_ref, rw_ref, rows_ref, out_ref):
    tokens, top = ids_ref.shape
    experts = rw_ref.shape[0]
    column = lax.broadcasted_iota(jnp.int32, (tokens, experts), 1)
    member = jnp.zeros((tokens, experts), F32)
    dense = jnp.zeros((tokens, experts), F32)
    for k in range(top):
        match = ids_ref[:, k : k + 1] == column
        member += jnp.where(match, 1.0, 0.0)
        dense += jnp.where(match, gates_ref[:, k : k + 1], 0.0)
    before = jnp.dot(strict(tokens, tokens, False), member.astype(BF), preferred_element_type=F32)
    order = jnp.where(member > 0.0, before + 1.0, 0.0).astype(BF)
    wide = jnp.dot(order, expand_ref[...], preferred_element_type=F32)
    hot = jnp.where(wide == rank_ref[...], 1.0, 0.0).astype(BF)
    own = jnp.broadcast_to(sum_ref[pl.ds(host_ref[0], 1), :], (tokens, tokens))
    diagonal = lax.broadcasted_iota(jnp.int32, (tokens, tokens), 0) == lax.broadcasted_iota(
        jnp.int32, (tokens, tokens), 1
    )
    own = jnp.sum(jnp.where(diagonal, own, 0.0), axis=1, keepdims=True)
    lost = jnp.dot((dense * own).astype(BF), rw_ref[...], preferred_element_type=F32)
    out_ref[...] = (jnp.dot(hot, rows_ref[...], preferred_element_type=F32) - lost).astype(BF)


def combine(host, ids, gates, sums, rw_t, rows):
    slot = np.arange(ROWS)
    expert = 2 * (slot // SLOTS) + WHICH[slot % SLOTS]
    expand = (np.arange(2 * HOSTS)[:, None] == expert[None, :]).astype(np.float32)
    rank = (RANK[slot % SLOTS] + 1.0).astype(np.float32)[None, :]
    return pl.pallas_call(
        combine_kernel,
        out_shape=jax.ShapeDtypeStruct((ids.shape[0], rows.shape[1]), BF),
        in_specs=[smem()] + [vmem()] * 7,
        out_specs=vmem(),
        compiler_params=pltpu.CompilerParams(vmem_limit_bytes=VMEM_LIMIT),
        name="combine",
    )(host, ids, gates, sums, jnp.asarray(expand, BF), jnp.asarray(rank), rw_t, rows)


def exchange(rows):
    return lax.all_to_all(rows, "expert", split_axis=0, concat_axis=0, tiled=True)


def body(tokens, upstream, expert_ids, gates, expert_weights, router_weight):
    model = tokens.shape[1]
    per_host, _, part, ff = expert_weights.shape
    host = lax.axis_index("expert").astype(jnp.int32)
    group = lax.axis_index("dp").astype(jnp.int32)
    host_arr = host.reshape(1)
    ids_t = expert_ids.T
    shard = expert_weights.transpose(0, 2, 1, 3).reshape(per_host, part, 3 * ff)
    weights = lax.all_gather(shard, "dp", axis=1, tiled=True)
    x_rows = exchange(dispatch(ids_t, tokens))
    dy_rows = exchange(dispatch(ids_t, upstream))
    route = jnp.concatenate([ids_t.astype(F32), gates.T], axis=0)
    route = lax.all_gather(route, "expert", axis=0, tiled=False)
    rw_t = router_weight.T
    rw_rows = lax.dynamic_slice_in_dim(rw_t, per_host * host, per_host, 0).astype(F32)
    rows, share, gg, gate, order = expert_rows(host_arr, route, x_rows, dy_rows, weights, rw_rows)
    back = exchange(rows)
    shares = lax.all_gather(share, "expert", axis=0, tiled=True)
    piece, sums = router_part(shares, gg, gate, order, x_rows)
    everyone = lax.all_gather(piece[:per_host].reshape(-1, 128), "dp", axis=0, tiled=False)
    column = jnp.sum(everyone, axis=0).reshape(per_host, model)
    column = lax.dynamic_slice_in_dim(column, part * group, part, 1)
    columns = lax.all_gather(column.reshape(1, -1), "expert", axis=0, tiled=True)
    router_grad = columns.reshape(-1, part).T
    token_grad = combine(host_arr, expert_ids, gates, sums, rw_t, back)
    return (token_grad, router_grad)


def solution(mesh):
    in_specs = (
        P(("dp", "expert"), None),
        P(("dp", "expert"), None),
        P(("dp", "expert"), None),
        P(("dp", "expert"), None),
        P("expert", None, "dp", None),
        P(),
    )
    out_specs = (P(("dp", "expert"), None), P("dp", None))
    return jax.shard_map(body, mesh=mesh, in_specs=in_specs, out_specs=out_specs, check_vma=False)
```

```python
import functools

import jax
import jax.numpy as jnp
import numpy as np
from jax import lax
from jax.experimental import pallas as pl
from jax.experimental.pallas import tpu as pltpu
from jax.sharding import PartitionSpec as P

F32 = jnp.float32
BF = jnp.bfloat16
CAP = 20
SLOTS = 2 * CAP
HOSTS = 32
ROWS = HOSTS * SLOTS
BLOCK = 2 * SLOTS + 8
TOKENS = 128


def slot_table():
    which = [0] * 16 + [1] * 16 + [0] * 4 + [1] * 4
    rank = list(range(16)) + list(range(16)) + list(range(16, 20)) + list(range(16, 20))
    return np.array(which), np.array(rank)


WHICH, RANK = slot_table()


def strict(rows, cols, upper):
    a = lax.broadcasted_iota(jnp.int32, (rows, cols), 0)
    b = lax.broadcasted_iota(jnp.int32, (rows, cols), 1)
    return jnp.where((a < b) if upper else (a > b), 1.0, 0.0).astype(BF)


def host_block(first, second):
    width = first.shape[-1]
    row = lax.broadcasted_iota(jnp.int32, (16, width), 0).astype(F32) + 1.0
    row8 = lax.broadcasted_iota(jnp.int32, (8, width), 0)
    mixed = jnp.where(
        row8 < 4, jnp.broadcast_to(first, (8, width)), jnp.broadcast_to(second, (8, width))
    )
    late = (row8 + jnp.where(row8 < 4, 17, 13)).astype(F32)
    return jnp.concatenate(
        [
            jnp.where(jnp.broadcast_to(first, (16, width)) == row, 1.0, 0.0),
            jnp.where(jnp.broadcast_to(second, (16, width)) == row, 1.0, 0.0),
            jnp.where(mixed == late, 1.0, 0.0),
        ],
        axis=0,
    )


def dispatch_kernel(ids_ref, gates_ref, x_ref, dy_ref, out_ref, hot_ref):
    experts, tokens = 2 * HOSTS, x_ref.shape[0]
    top = ids_ref.shape[0]
    column = lax.broadcasted_iota(jnp.int32, (experts, tokens), 0)
    member = jnp.zeros((experts, tokens), F32)
    for k in range(top):
        member += jnp.where(ids_ref[k : k + 1, :] == column, 1.0, 0.0)
    before = jnp.dot(member.astype(BF), strict(tokens, tokens, True), preferred_element_type=F32)
    order = jnp.where(member > 0.0, before + 1.0, 0.0)
    for pair in range(HOSTS // 2):
        blocks = [
            host_block(order[2 * h : 2 * h + 1], order[2 * h + 1 : 2 * h + 2])
            for h in (2 * pair, 2 * pair + 1)
        ]
        hot_ref[80 * pair : 80 * pair + 80, :] = jnp.concatenate(blocks, axis=0).astype(BF)
    line = lambda ref: jnp.concatenate([ref[k : k + 1, :] for k in range(top)], axis=1)
    left = line(gates_ref)
    routes = [line(ids_ref).astype(F32)]
    for _ in range(3):
        high = left.astype(BF).astype(F32)
        routes.append(high)
        left = left - high
    routes = jnp.concatenate(routes + [jnp.zeros((4, top * tokens), F32)], axis=0)

    def step(i, carry):
        hot = hot_ref[pl.ds(pl.multiple_of(i * 320, 320), 320), :]
        xs = jnp.dot(hot, x_ref[...], preferred_element_type=F32)
        ys = jnp.dot(hot, dy_ref[...], preferred_element_type=F32)
        for j in range(8):
            block = jnp.concatenate(
                [xs[40 * j : 40 * j + 40], ys[40 * j : 40 * j + 40], routes], axis=0
            )
            out_ref[8 * i + j] = block.astype(BF)
        return carry

    lax.fori_loop(0, ROWS // 320, step, 0)


def vmem():
    return pl.BlockSpec(memory_space=pltpu.VMEM)


def smem():
    return pl.BlockSpec(memory_space=pltpu.SMEM)


def params(mib):
    return pltpu.CompilerParams(vmem_limit_bytes=mib * 1024 * 1024)


def cost(flops, moved):
    return pl.CostEstimate(flops=flops, bytes_accessed=moved, transcendentals=0)


def dispatch(ids_t, gates_t, tokens, upstream):
    return pl.pallas_call(
        dispatch_kernel,
        out_shape=jax.ShapeDtypeStruct((HOSTS, BLOCK, tokens.shape[1]), BF),
        in_specs=[vmem()] * 4,
        out_specs=vmem(),
        scratch_shapes=[pltpu.VMEM((ROWS, tokens.shape[0]), BF)],
        compiler_params=params(56),
        name="dispatch",
    )(ids_t, gates_t, tokens, upstream)


def pieces(a, b, start, e):
    at = start + 16 * e
    return jnp.concatenate(
        [a[at : at + 16], b[at : at + 16], a[start + 32 : start + 40], b[start + 32 : start + 40]],
        axis=0,
    ).astype(BF)


def forward_kernel(
    host_ref, rows_ref, w_ref,
    xe_ref, hot_ref, gu_ref, add_ref, gg_ref, gate_ref, share_ref,
    dye_ref, ids_ref, gates_ref, wide_ref, gcol_ref,
):
    sources = rows_ref.shape[0]
    pairs = sources // 2
    width = hot_ref.shape[3]
    top = ids_ref.shape[1] // width
    ff = w_ref.shape[2] // 3
    for p in range(pairs):
        a, b = rows_ref[2 * p].astype(F32), rows_ref[2 * p + 1].astype(F32)
        for e in (0, 1):
            xe_ref[0, e, 48 * p : 48 * p + 48, :] = pieces(a, b, 0, e)
            dye_ref[e, 48 * p : 48 * p + 48, :] = pieces(a, b, SLOTS, e)
        for n, block in ((2 * p, a), (2 * p + 1, b)):
            ids_ref[n : n + 1, :] = block[80:81]
            gates_ref[n : n + 1, :] = block[81:82] + block[82:83] + block[83:84]
    upper = strict(width, width, True)
    host = host_ref[0]
    row8 = lax.broadcasted_iota(jnp.int32, (8, width), 0)
    row16 = lax.broadcasted_iota(jnp.int32, (16, width), 0).astype(F32) + 1.0
    total = jnp.zeros((sources, width), F32)
    spread = lambda v, n: jnp.broadcast_to(v, (n, width))
    for e in (0, 1):
        wanted = (2 * host + e).astype(F32)
        member = jnp.zeros((sources, width), F32)
        gate = jnp.zeros((sources, width), F32)
        for k in range(top):
            match = ids_ref[:, width * k : width * k + width] == wanted
            member += jnp.where(match, 1.0, 0.0)
            gate += jnp.where(match, gates_ref[:, width * k : width * k + width], 0.0)
        before = jnp.dot(member.astype(BF), upper, preferred_element_type=F32)
        order = jnp.where(member > 0.0, before + 1.0, 0.0)
        gate_ref[e] = gate
        if e == 0:
            late = jnp.where(row8 < 4, row8 + 17, -1).astype(F32)
        else:
            late = jnp.where(row8 < 4, -1, row8 + 13).astype(F32)
        for p in range(pairs):
            a, b = order[2 * p : 2 * p + 1], order[2 * p + 1 : 2 * p + 2]
            ga, gb = gate[2 * p : 2 * p + 1], gate[2 * p + 1 : 2 * p + 2]
            hot = jnp.concatenate(
                [
                    jnp.where(spread(a, 16) == row16, 1.0, 0.0),
                    jnp.where(spread(b, 16) == row16, 1.0, 0.0),
                    jnp.where(spread(a, 8) == late, 1.0, 0.0),
                    jnp.where(spread(b, 8) == late, 1.0, 0.0),
                ],
                axis=0,
            )
            weight = jnp.concatenate(
                [spread(ga, 16), spread(gb, 16), spread(ga, 8), spread(gb, 8)], axis=0
            )
            wide_ref[48 * p : 48 * p + 48, :] = hot
            hot_ref[0, e, 48 * p : 48 * p + 48, :] = hot.astype(BF)
            gcol_ref[48 * p : 48 * p + 48, :] = jnp.sum(hot * weight, axis=1, keepdims=True)
        pre = jnp.dot(xe_ref[0, e], w_ref[e, :, 0 : 2 * ff], preferred_element_type=F32)
        hidden_grad = jnp.dot(dye_ref[e], w_ref[e, :, 2 * ff :], preferred_element_type=F32)
        pre_gate, pre_up = pre[:, 0:ff], pre[:, ff:]
        sigma = jax.nn.sigmoid(pre_gate)
        active = pre_gate * sigma
        hidden = (active * pre_up).astype(BF).astype(F32)
        gg = jnp.sum(hidden_grad * hidden, axis=1, keepdims=True).astype(BF).astype(F32)
        gcol = gcol_ref[...]
        scaled = hidden_grad * gcol
        gu_ref[0, e, :, 0:ff] = (
            scaled * pre_up * sigma * (1.0 + pre_gate * (1.0 - sigma))
        ).astype(BF)
        gu_ref[0, e, :, ff:] = (scaled * active).astype(BF)
        add_ref[0, e] = gcol * gg
        for p in range(pairs):
            hit = wide_ref[48 * p : 48 * p + 48, :] * gg[48 * p : 48 * p + 48]
            down = lambda v: jnp.sum(v, axis=0, keepdims=True)
            gg_ref[e, 2 * p : 2 * p + 1, :] = down(hit[0:16]) + down(hit[32:40])
            gg_ref[e, 2 * p + 1 : 2 * p + 2, :] = down(hit[16:32]) + down(hit[40:48])
        total = total + gate * gg_ref[e]
    for h in range(HOSTS):
        share_ref[h] = total


def forward(host, blocks, weights):
    halves, sources, width = 2, HOSTS // 2, TOKENS
    model = blocks.shape[2]
    ff = weights.shape[2] // 3
    compact = sources * 24
    shape = lambda last, kind: jax.ShapeDtypeStruct((halves, 2, compact, last), kind)
    spec = lambda last: pl.BlockSpec((1, 2, compact, last), lambda i: (i, 0, 0, 0))
    dense = jax.ShapeDtypeStruct((2, HOSTS, width), F32)
    dense_spec = pl.BlockSpec((2, sources, width), lambda i: (0, i, 0))
    return pl.pallas_call(
        forward_kernel,
        grid=(halves,),
        out_shape=(
            shape(model, BF), shape(width, BF), shape(2 * ff, BF), shape(1, F32),
            dense, dense,
            jax.ShapeDtypeStruct((HOSTS, HOSTS, width), F32),
        ),
        in_specs=[
            smem(),
            pl.BlockSpec((sources, BLOCK, model), lambda i: (i, 0, 0)),
            pl.BlockSpec(weights.shape, lambda i: (0, 0, 0)),
        ],
        out_specs=(
            spec(model), spec(width), spec(2 * ff), spec(1),
            dense_spec, dense_spec,
            pl.BlockSpec((HOSTS, sources, width), lambda i: (0, i, 0)),
        ),
        scratch_shapes=[
            pltpu.VMEM((2, compact, model), BF),
            pltpu.VMEM((sources, blocks.shape[2]), F32),
            pltpu.VMEM((sources, blocks.shape[2]), F32),
            pltpu.VMEM((compact, width), F32),
            pltpu.VMEM((compact, 1), F32),
        ],
        compiler_params=params(56),
        cost_estimate=cost(4 * halves * compact * model * 3 * ff, 20_000_000),
        name="forward",
    )(host, blocks, weights)


def backward_kernel(gu_ref, add_ref, w_ref, rw_ref, out_ref, re_ref):
    ff = w_ref.shape[2] // 3
    compact = gu_ref.shape[2]
    for e in (0, 1):
        row = lax.dot_general(
            gu_ref[0, e], w_ref[e, :, 0 : 2 * ff], (((1,), (1,)), ((), ())),
            preferred_element_type=F32,
        )
        re_ref[e] = (row + add_ref[0, e] * rw_ref[e : e + 1, :]).astype(BF)
    for p in range(compact // 48):
        r0 = re_ref[0, 48 * p : 48 * p + 48, :].astype(F32)
        r1 = re_ref[1, 48 * p : 48 * p + 48, :].astype(F32)
        out_ref[80 * p : 80 * p + 80, :] = jnp.concatenate(
            [
                r0[0:16], r1[0:16], r0[32:40] + r1[32:40],
                r0[16:32], r1[16:32], r0[40:48] + r1[40:48],
            ],
            axis=0,
        ).astype(BF)


def backward(gu, add, weights, rw_rows):
    halves, _, compact, double = gu.shape
    model = weights.shape[1]
    spec = lambda last: pl.BlockSpec((1, 2, compact, last), lambda i: (i, 0, 0, 0))
    return pl.pallas_call(
        backward_kernel,
        grid=(halves,),
        out_shape=jax.ShapeDtypeStruct((ROWS, model), BF),
        in_specs=[
            spec(double), spec(1),
            pl.BlockSpec(weights.shape, lambda i: (0, 0, 0)),
            pl.BlockSpec(rw_rows.shape, lambda i: (0, 0)),
        ],
        out_specs=pl.BlockSpec((ROWS // halves, model), lambda i: (i, 0)),
        scratch_shapes=[pltpu.VMEM((2, compact, model), BF)],
        compiler_params=params(56),
        cost_estimate=cost(4 * halves * compact * model * double, 10_000_000),
        name="backward",
    )(gu, add, weights, rw_rows)


def router_kernel(shares_ref, gg_ref, gate_ref, mask_ref, hot_ref, xe_ref, part_ref, sum_ref):
    total = shares_ref[0]
    for h in range(1, HOSTS):
        total = total + shares_ref[h]
    sum_ref[...] = total
    halves, _, compact, model = xe_ref.shape
    sources = HOSTS // halves
    for e in (0, 1):
        logit = (gate_ref[e] * (gg_ref[e] - total)).astype(BF)
        part = jnp.zeros((8, model), F32)
        for i in range(halves):
            near = lax.dot_general(
                logit[sources * i : sources * i + sources], hot_ref[i, e],
                (((1,), (1,)), ((), ())), preferred_element_type=F32,
            )
            line = jnp.sum(near * mask_ref[...], axis=0, keepdims=True)
            line = jnp.concatenate([line, jnp.zeros((7, compact), F32)], axis=0).astype(BF)
            part = part + jnp.dot(line, xe_ref[i, e], preferred_element_type=F32)
        part_ref[e : e + 1, :] = part[0:1]


def router_part(shares, gg, gate, hot, xe):
    slot = np.arange(xe.shape[2])
    inner = slot % 48
    second = ((inner >= 16) & (inner < 32)) | (inner >= 40)
    source = 2 * (slot // 48) + second
    mask = np.arange(HOSTS // 2)[:, None] == source[None, :]
    return pl.pallas_call(
        router_kernel,
        out_shape=(
            jax.ShapeDtypeStruct((2, xe.shape[3]), F32),
            jax.ShapeDtypeStruct((HOSTS, gg.shape[2]), F32),
        ),
        in_specs=[vmem()] * 6,
        out_specs=(vmem(), vmem()),
        compiler_params=params(16),
        cost_estimate=cost(64 * xe.size, 4_000_000),
        name="router_part",
    )(shares, gg, gate, jnp.asarray(mask.astype(np.float32)), hot, xe)


def combine_kernel(host_ref, ids_ref, gates_ref, sum_ref, expand_ref, rank_ref, rw_ref, rows_ref, out_ref):
    tokens, top = ids_ref.shape
    experts = rw_ref.shape[0]
    column = lax.broadcasted_iota(jnp.int32, (tokens, experts), 1)
    member = jnp.zeros((tokens, experts), F32)
    dense = jnp.zeros((tokens, experts), F32)
    for k in range(top):
        match = ids_ref[:, k : k + 1] == column
        member += jnp.where(match, 1.0, 0.0)
        dense += jnp.where(match, gates_ref[:, k : k + 1], 0.0)
    before = jnp.dot(strict(tokens, tokens, False), member.astype(BF), preferred_element_type=F32)
    order = jnp.where(member > 0.0, before + 1.0, 0.0).astype(BF)
    wide = jnp.dot(order, expand_ref[...], preferred_element_type=F32)
    hot = jnp.where(wide == rank_ref[...], 1.0, 0.0).astype(BF)
    own = jnp.broadcast_to(sum_ref[pl.ds(host_ref[0], 1), :], (tokens, tokens))
    diagonal = lax.broadcasted_iota(jnp.int32, (tokens, tokens), 0) == lax.broadcasted_iota(
        jnp.int32, (tokens, tokens), 1
    )
    own = jnp.sum(jnp.where(diagonal, own, 0.0), axis=1, keepdims=True)
    lost = jnp.dot((dense * own).astype(BF), rw_ref[...], preferred_element_type=F32)
    out_ref[...] = (jnp.dot(hot, rows_ref[...], preferred_element_type=F32) - lost).astype(BF)


def combine(host, ids, gates, sums, rw_t, rows):
    slot = np.arange(ROWS)
    expert = 2 * (slot // SLOTS) + WHICH[slot % SLOTS]
    expand = (np.arange(2 * HOSTS)[:, None] == expert[None, :]).astype(np.float32)
    rank = (RANK[slot % SLOTS] + 1.0).astype(np.float32)[None, :]
    return pl.pallas_call(
        combine_kernel,
        out_shape=jax.ShapeDtypeStruct((ids.shape[0], rows.shape[1]), BF),
        in_specs=[smem()] + [vmem()] * 7,
        out_specs=vmem(),
        compiler_params=params(20),
        name="combine",
    )(host, ids, gates, sums, jnp.asarray(expand, BF), jnp.asarray(rank), rw_t, rows)


def exchange(rows):
    return lax.all_to_all(rows, "expert", split_axis=0, concat_axis=0, tiled=True)


def body(tokens, upstream, expert_ids, gates, expert_weights, router_weight):
    model = tokens.shape[1]
    per_host, _, part, ff = expert_weights.shape
    host = lax.axis_index("expert").astype(jnp.int32)
    group = lax.axis_index("dp").astype(jnp.int32)
    host_arr = host.reshape(1)
    ids_t = expert_ids.T
    shard = expert_weights.transpose(0, 2, 1, 3).reshape(per_host, part, 3 * ff)
    weights = lax.all_gather(shard, "dp", axis=1, tiled=True)
    blocks = exchange(dispatch(ids_t, gates.T, tokens, upstream))
    rw_t = router_weight.T
    rw_rows = lax.dynamic_slice_in_dim(rw_t, per_host * host, per_host, 0).astype(F32)
    xe, hot, gu, add, gg, gate, share = forward(host_arr, blocks, weights)
    shares = exchange(share)
    back = exchange(backward(gu, add, weights, rw_rows))
    piece, sums = router_part(shares, gg, gate, hot, xe)
    everyone = lax.all_gather(piece.reshape(-1, 128), "dp", axis=0, tiled=False)
    column = jnp.sum(everyone, axis=0).reshape(per_host, model)
    column = lax.dynamic_slice_in_dim(column, part * group, part, 1)
    column, back = lax.optimization_barrier((column, back))
    columns = exchange(jnp.broadcast_to(column.reshape(1, -1), (HOSTS, per_host * part)))
    router_grad = columns.reshape(-1, part).T
    token_grad = combine(host_arr, expert_ids, gates, sums, rw_t, back)
    return (token_grad, router_grad)


def solution(mesh):
    in_specs = (
        P(("dp", "expert"), None),
        P(("dp", "expert"), None),
        P(("dp", "expert"), None),
        P(("dp", "expert"), None),
        P("expert", None, "dp", None),
        P(),
    )
    out_specs = (P(("dp", "expert"), None), P("dp", None))
    return jax.shard_map(body, mesh=mesh, in_specs=in_specs, out_specs=out_specs, check_vma=False)
```

```python
import functools

import jax
import jax.numpy as jnp
import numpy as np
from jax import lax
from jax.experimental import pallas as pl
from jax.experimental.pallas import tpu as pltpu
from jax.sharding import PartitionSpec as P

F32 = jnp.float32
BF = jnp.bfloat16
CAP = 20
SLOTS = 2 * CAP
HOSTS = 32
ROWS = HOSTS * SLOTS
BLOCK = 2 * SLOTS
TOKENS = 128


def slot_table():
    which = [0] * 16 + [1] * 16 + [0] * 4 + [1] * 4
    rank = list(range(16)) + list(range(16)) + list(range(16, 20)) + list(range(16, 20))
    return np.array(which), np.array(rank)


WHICH, RANK = slot_table()


def strict(rows, cols, upper):
    a = lax.broadcasted_iota(jnp.int32, (rows, cols), 0)
    b = lax.broadcasted_iota(jnp.int32, (rows, cols), 1)
    return jnp.where((a < b) if upper else (a > b), 1.0, 0.0).astype(BF)


def host_block(first, second):
    width = first.shape[-1]
    row = lax.broadcasted_iota(jnp.int32, (16, width), 0).astype(F32) + 1.0
    row8 = lax.broadcasted_iota(jnp.int32, (8, width), 0)
    mixed = jnp.where(
        row8 < 4, jnp.broadcast_to(first, (8, width)), jnp.broadcast_to(second, (8, width))
    )
    late = (row8 + jnp.where(row8 < 4, 17, 13)).astype(F32)
    return jnp.concatenate(
        [
            jnp.where(jnp.broadcast_to(first, (16, width)) == row, 1.0, 0.0),
            jnp.where(jnp.broadcast_to(second, (16, width)) == row, 1.0, 0.0),
            jnp.where(mixed == late, 1.0, 0.0),
        ],
        axis=0,
    )


def dispatch_kernel(ids_ref, x_ref, dy_ref, out_ref, hot_ref):
    experts, tokens = 2 * HOSTS, x_ref.shape[0]
    hosts = out_ref.shape[0]

    @pl.when(pl.program_id(0) == 0)
    def _():
        column = lax.broadcasted_iota(jnp.int32, (experts, tokens), 0)
        member = jnp.zeros((experts, tokens), F32)
        for k in range(ids_ref.shape[0]):
            member += jnp.where(ids_ref[k : k + 1, :] == column, 1.0, 0.0)
        before = jnp.dot(
            member.astype(BF), strict(tokens, tokens, True), preferred_element_type=F32
        )
        order = jnp.where(member > 0.0, before + 1.0, 0.0)
        for pair in range(HOSTS // 2):
            blocks = [
                host_block(order[2 * h : 2 * h + 1], order[2 * h + 1 : 2 * h + 2])
                for h in (2 * pair, 2 * pair + 1)
            ]
            hot_ref[80 * pair : 80 * pair + 80, :] = jnp.concatenate(blocks, axis=0).astype(BF)

    rows = SLOTS * hosts
    hot = hot_ref[pl.ds(pl.multiple_of(pl.program_id(0) * rows, rows), rows), :]
    xs = jnp.dot(hot, x_ref[...], preferred_element_type=F32)
    ys = jnp.dot(hot, dy_ref[...], preferred_element_type=F32)
    for j in range(hosts):
        at = slice(SLOTS * j, SLOTS * j + SLOTS)
        out_ref[j] = jnp.concatenate([xs[at], ys[at]], axis=0).astype(BF)


def vmem():
    return pl.BlockSpec(memory_space=pltpu.VMEM)


def smem():
    return pl.BlockSpec(memory_space=pltpu.SMEM)


def params(mib):
    return pltpu.CompilerParams(vmem_limit_bytes=mib * 1024 * 1024)


def cost(flops, moved):
    return pl.CostEstimate(flops=flops, bytes_accessed=moved, transcendentals=0)


def dispatch(ids_t, tokens, upstream):
    steps = 4
    whole = lambda v: pl.BlockSpec(v.shape, lambda i: (0, 0))
    return pl.pallas_call(
        dispatch_kernel,
        grid=(steps,),
        out_shape=jax.ShapeDtypeStruct((HOSTS, BLOCK, tokens.shape[1]), BF),
        in_specs=[whole(ids_t), whole(tokens), whole(upstream)],
        out_specs=pl.BlockSpec((HOSTS // steps, BLOCK, tokens.shape[1]), lambda i: (i, 0, 0)),
        scratch_shapes=[pltpu.VMEM((ROWS, tokens.shape[0]), BF)],
        compiler_params=params(56),
        name="dispatch",
    )(ids_t, tokens, upstream)


def pieces(a, b, start, e):
    at = start + 16 * e
    return jnp.concatenate(
        [a[at : at + 16], b[at : at + 16], a[start + 32 : start + 40], b[start + 32 : start + 40]],
        axis=0,
    ).astype(BF)


def load_weights(w_ref, held_ref, sems, count):
    ff = w_ref.shape[3]
    return [
        [
            pltpu.make_async_copy(
                w_ref.at[e, j], held_ref.at[e, :, pl.ds(ff * j, ff)], sems.at[e, j]
            )
            for j in range(count)
        ]
        for e in (0, 1)
    ]


def forward_kernel(
    host_ref, route_ref, rows_ref, w_hbm,
    xe_ref, hot_ref, gu_ref, add_ref, gg_ref, share_ref,
    dye_ref, wide_ref, gcol_ref, w_ref, sems,
):
    sources = rows_ref.shape[0]
    pairs = sources // 2
    width = hot_ref.shape[3]
    ff = w_ref.shape[2] // 3
    first = pl.program_id(0) == 0
    copies = load_weights(w_hbm, w_ref, sems, 3)

    @pl.when(first)
    def _():
        for group in copies:
            for copy in group:
                copy.start()

    for p in range(pairs):
        a, b = rows_ref[2 * p].astype(F32), rows_ref[2 * p + 1].astype(F32)
        for e in (0, 1):
            xe_ref[0, e, 48 * p : 48 * p + 48, :] = pieces(a, b, 0, e)
            dye_ref[e, 48 * p : 48 * p + 48, :] = pieces(a, b, SLOTS, e)
    ids = route_ref[:, 0:8, :]
    gates = route_ref[:, 8:16, :]
    upper = strict(width, width, True)
    host = host_ref[0]
    row8 = lax.broadcasted_iota(jnp.int32, (8, width), 0)
    row16 = lax.broadcasted_iota(jnp.int32, (16, width), 0).astype(F32) + 1.0
    total = jnp.zeros((sources, width), F32)
    spread = lambda v, n: jnp.broadcast_to(v, (n, width))
    for e in (0, 1):
        wanted = (2 * host + e).astype(F32)
        match = ids == wanted
        member = jnp.sum(jnp.where(match, 1.0, 0.0), axis=1)
        gate = jnp.sum(jnp.where(match, gates, 0.0), axis=1)
        before = jnp.dot(member.astype(BF), upper, preferred_element_type=F32)
        order = jnp.where(member > 0.0, before + 1.0, 0.0)
        gg_ref[2 + e] = gate
        if e == 0:
            late = jnp.where(row8 < 4, row8 + 17, -1).astype(F32)
        else:
            late = jnp.where(row8 < 4, -1, row8 + 13).astype(F32)
        for p in range(pairs):
            a, b = order[2 * p : 2 * p + 1], order[2 * p + 1 : 2 * p + 2]
            ga, gb = gate[2 * p : 2 * p + 1], gate[2 * p + 1 : 2 * p + 2]
            hot = jnp.concatenate(
                [
                    jnp.where(spread(a, 16) == row16, 1.0, 0.0),
                    jnp.where(spread(b, 16) == row16, 1.0, 0.0),
                    jnp.where(spread(a, 8) == late, 1.0, 0.0),
                    jnp.where(spread(b, 8) == late, 1.0, 0.0),
                ],
                axis=0,
            )
            weight = jnp.concatenate(
                [spread(ga, 16), spread(gb, 16), spread(ga, 8), spread(gb, 8)], axis=0
            )
            wide_ref[48 * p : 48 * p + 48, :] = hot
            hot_ref[0, e, 48 * p : 48 * p + 48, :] = hot.astype(BF)
            gcol_ref[48 * p : 48 * p + 48, :] = jnp.sum(hot * weight, axis=1, keepdims=True)

        @pl.when(first)
        def _(e=e):
            for copy in copies[e]:
                copy.wait()

        pre = jnp.dot(xe_ref[0, e], w_ref[e, :, 0 : 2 * ff], preferred_element_type=F32)
        hidden_grad = jnp.dot(dye_ref[e], w_ref[e, :, 2 * ff :], preferred_element_type=F32)
        pre_gate, pre_up = pre[:, 0:ff], pre[:, ff:]
        sigma = jax.nn.sigmoid(pre_gate)
        active = pre_gate * sigma
        hidden = (active * pre_up).astype(BF).astype(F32)
        gg = jnp.sum(hidden_grad * hidden, axis=1, keepdims=True).astype(BF).astype(F32)
        gcol = gcol_ref[...]
        scaled = hidden_grad * gcol
        gu_ref[0, e, :, 0:ff] = (
            scaled * pre_up * sigma * (1.0 + pre_gate * (1.0 - sigma))
        ).astype(BF)
        gu_ref[0, e, :, ff:] = (scaled * active).astype(BF)
        add_ref[0, e] = gcol * gg
        for p in range(pairs):
            hit = wide_ref[48 * p : 48 * p + 48, :] * gg[48 * p : 48 * p + 48]
            down = lambda v: jnp.sum(v, axis=0, keepdims=True)
            gg_ref[e, 2 * p : 2 * p + 1, :] = down(hit[0:16]) + down(hit[32:40])
            gg_ref[e, 2 * p + 1 : 2 * p + 2, :] = down(hit[16:32]) + down(hit[40:48])
        total = total + gate * gg_ref[e]
    for h in range(HOSTS):
        share_ref[h] = total


def forward(host, route, blocks, weights):
    halves, sources, width = 2, HOSTS // 2, TOKENS
    model, ff = weights.shape[2:]
    compact = sources * 24
    shape = lambda last, kind: jax.ShapeDtypeStruct((halves, 2, compact, last), kind)
    spec = lambda last: pl.BlockSpec((1, 2, compact, last), lambda i: (i, 0, 0, 0))
    return pl.pallas_call(
        forward_kernel,
        grid=(halves,),
        out_shape=(
            shape(model, BF), shape(width, BF), shape(2 * ff, BF), shape(1, F32),
            jax.ShapeDtypeStruct((4, HOSTS, width), F32),
            jax.ShapeDtypeStruct((HOSTS, HOSTS, width), F32),
        ),
        in_specs=[
            smem(),
            pl.BlockSpec((sources, 16, width), lambda i: (i, 0, 0)),
            pl.BlockSpec((sources, BLOCK, model), lambda i: (i, 0, 0)),
            pl.BlockSpec(memory_space=pl.ANY),
        ],
        out_specs=(
            spec(model), spec(width), spec(2 * ff), spec(1),
            pl.BlockSpec((4, sources, width), lambda i: (0, i, 0)),
            pl.BlockSpec((HOSTS, sources, width), lambda i: (0, i, 0)),
        ),
        scratch_shapes=[
            pltpu.VMEM((2, compact, model), BF),
            pltpu.VMEM((compact, width), F32),
            pltpu.VMEM((compact, 1), F32),
            pltpu.VMEM((2, model, 3 * ff), BF),
            pltpu.SemaphoreType.DMA((2, 3)),
        ],
        compiler_params=params(56),
        cost_estimate=cost(4 * halves * compact * model * 3 * ff, 20_000_000),
        name="forward",
    )(host, route, blocks, weights)


def backward_kernel(host_ref, gu_ref, add_ref, rw_ref, w_hbm, out_ref, re_ref, w_ref, sems):
    compact = gu_ref.shape[2]
    first = pl.program_id(0) == 0
    copies = load_weights(w_hbm, w_ref, sems, 2)

    @pl.when(first)
    def _():
        for group in copies:
            for copy in group:
                copy.start()

    experts = rw_ref.shape[0]
    mine = lax.broadcasted_iota(jnp.int32, (8, experts), 0) + 2 * host_ref[0]
    pick = jnp.where(lax.broadcasted_iota(jnp.int32, (8, experts), 1) == mine, 1.0, 0.0)
    router = jnp.dot(pick.astype(BF), rw_ref[...], preferred_element_type=F32)
    for e in (0, 1):

        @pl.when(first)
        def _(e=e):
            for copy in copies[e]:
                copy.wait()

        row = lax.dot_general(
            gu_ref[0, e], w_ref[e], (((1,), (1,)), ((), ())), preferred_element_type=F32
        )
        re_ref[e] = (row + add_ref[0, e] * router[e : e + 1]).astype(BF)
    for p in range(compact // 48):
        r0 = re_ref[0, 48 * p : 48 * p + 48, :].astype(F32)
        r1 = re_ref[1, 48 * p : 48 * p + 48, :].astype(F32)
        out_ref[80 * p : 80 * p + 80, :] = jnp.concatenate(
            [
                r0[0:16], r1[0:16], r0[32:40] + r1[32:40],
                r0[16:32], r1[16:32], r0[40:48] + r1[40:48],
            ],
            axis=0,
        ).astype(BF)


def backward(host, gu, add, rw_t, weights):
    halves, _, compact, double = gu.shape
    model = weights.shape[2]
    spec = lambda last: pl.BlockSpec((1, 2, compact, last), lambda i: (i, 0, 0, 0))
    return pl.pallas_call(
        backward_kernel,
        grid=(halves,),
        out_shape=jax.ShapeDtypeStruct((ROWS, model), BF),
        in_specs=[
            smem(), spec(double), spec(1),
            pl.BlockSpec(rw_t.shape, lambda i: (0, 0)),
            pl.BlockSpec(memory_space=pl.ANY),
        ],
        out_specs=pl.BlockSpec((ROWS // halves, model), lambda i: (i, 0)),
        scratch_shapes=[
            pltpu.VMEM((2, compact, model), BF),
            pltpu.VMEM((2, model, double), BF),
            pltpu.SemaphoreType.DMA((2, 2)),
        ],
        compiler_params=params(56),
        cost_estimate=cost(4 * halves * compact * model * double, 10_000_000),
        name="backward",
    )(host, gu, add, rw_t, weights)


def router_kernel(shares_ref, gg_ref, hot_hbm, xe_hbm, part_ref, sum_ref, hot_ref, xe_ref, sems):
    copies = [
        pltpu.make_async_copy(hot_hbm, hot_ref, sems.at[0]),
        pltpu.make_async_copy(xe_hbm, xe_ref, sems.at[1]),
    ]
    for copy in copies:
        copy.start()
    total = shares_ref[0]
    for h in range(1, HOSTS):
        total = total + shares_ref[h]
    sum_ref[...] = total
    halves, _, compact, model = xe_ref.shape
    sources = HOSTS // halves
    source = lax.broadcasted_iota(jnp.int32, (sources, compact), 0)
    slot = lax.broadcasted_iota(jnp.int32, (sources, compact), 1) - 48 * (source >> 1)
    even = ((slot >= 0) & (slot < 16)) | ((slot >= 32) & (slot < 40))
    odd = ((slot >= 16) & (slot < 32)) | ((slot >= 40) & (slot < 48))
    own = ((source & 1) == 0) & even | ((source & 1) == 1) & odd
    for copy in copies:
        copy.wait()
    for e in (0, 1):
        logit = (gg_ref[2 + e] * (gg_ref[e] - total)).astype(BF)
        part = jnp.zeros((8, model), F32)
        for i in range(halves):
            near = lax.dot_general(
                logit[sources * i : sources * i + sources], hot_ref[i, e],
                (((1,), (1,)), ((), ())), preferred_element_type=F32,
            )
            line = jnp.sum(jnp.where(own, near, 0.0), axis=0, keepdims=True)
            line = jnp.concatenate([line, jnp.zeros((7, compact), F32)], axis=0).astype(BF)
            part = part + jnp.dot(line, xe_ref[i, e], preferred_element_type=F32)
        part_ref[e : e + 1, :] = part[0:1]


def router_part(shares, gg, hot, xe):
    return pl.pallas_call(
        router_kernel,
        out_shape=(
            jax.ShapeDtypeStruct((2, xe.shape[3]), F32),
            jax.ShapeDtypeStruct((HOSTS, gg.shape[2]), F32),
        ),
        in_specs=[vmem(), vmem()] + [pl.BlockSpec(memory_space=pl.ANY)] * 2,
        out_specs=(vmem(), vmem()),
        scratch_shapes=[
            pltpu.VMEM(hot.shape, BF), pltpu.VMEM(xe.shape, BF), pltpu.SemaphoreType.DMA((2,)),
        ],
        compiler_params=params(16),
        cost_estimate=cost(64 * xe.size, 4_000_000),
        name="router_part",
    )(shares, gg, hot, xe)


def lookup_kernel(ids_ref, gates_ref, expand_ref, rank_ref, hot_ref, dense_ref):
    tokens, top = ids_ref.shape
    experts = expand_ref.shape[0]
    column = lax.broadcasted_iota(jnp.int32, (tokens, experts), 1)
    member = jnp.zeros((tokens, experts), F32)
    dense = jnp.zeros((tokens, experts), F32)
    for k in range(top):
        match = ids_ref[:, k : k + 1] == column
        member += jnp.where(match, 1.0, 0.0)
        dense += jnp.where(match, gates_ref[:, k : k + 1], 0.0)
    before = jnp.dot(strict(tokens, tokens, False), member.astype(BF), preferred_element_type=F32)
    order = jnp.where(member > 0.0, before + 1.0, 0.0).astype(BF)
    wide = jnp.dot(order, expand_ref[...], preferred_element_type=F32)
    hot_ref[...] = jnp.where(wide == rank_ref[...], 1.0, 0.0).astype(BF)
    dense_ref[...] = dense


def lookup(ids, gates):
    slot = np.arange(ROWS)
    expert = 2 * (slot // SLOTS) + WHICH[slot % SLOTS]
    expand = (np.arange(2 * HOSTS)[:, None] == expert[None, :]).astype(np.float32)
    rank = (RANK[slot % SLOTS] + 1.0).astype(np.float32)[None, :]
    return pl.pallas_call(
        lookup_kernel,
        out_shape=(
            jax.ShapeDtypeStruct((ids.shape[0], ROWS), BF),
            jax.ShapeDtypeStruct((ids.shape[0], 2 * HOSTS), F32),
        ),
        in_specs=[vmem()] * 4,
        out_specs=(vmem(), vmem()),
        compiler_params=params(56),
        name="lookup",
    )(ids, gates, jnp.asarray(expand, BF), jnp.asarray(rank))


def combine_kernel(host_ref, hot_ref, dense_ref, sum_ref, rw_ref, rows_ref, out_ref):
    tokens = hot_ref.shape[0]
    own = jnp.broadcast_to(sum_ref[pl.ds(host_ref[0], 1), :], (tokens, tokens))
    diagonal = lax.broadcasted_iota(jnp.int32, (tokens, tokens), 0) == lax.broadcasted_iota(
        jnp.int32, (tokens, tokens), 1
    )
    own = jnp.sum(jnp.where(diagonal, own, 0.0), axis=1, keepdims=True)
    lost = jnp.dot((dense_ref[...] * own).astype(BF), rw_ref[...], preferred_element_type=F32)
    out = jnp.dot(hot_ref[...], rows_ref[...], preferred_element_type=F32)
    out_ref[...] = (out - lost).astype(BF)


def combine(host, hot, dense, sums, rw_t, rows):
    return pl.pallas_call(
        combine_kernel,
        out_shape=jax.ShapeDtypeStruct((hot.shape[0], rows.shape[1]), BF),
        in_specs=[smem()] + [vmem()] * 5,
        out_specs=vmem(),
        compiler_params=params(20),
        name="combine",
    )(host, hot, dense, sums, rw_t, rows)


def exchange(rows):
    return lax.all_to_all(rows, "expert", split_axis=0, concat_axis=0, tiled=True)


def body(tokens, upstream, expert_ids, gates, expert_weights, router_weight):
    model = tokens.shape[1]
    per_host, _, part, ff = expert_weights.shape
    host = lax.axis_index("expert").astype(jnp.int32)
    group = lax.axis_index("dp").astype(jnp.int32)
    host_arr = host.reshape(1)
    ids_t = expert_ids.T
    weights = lax.all_gather(expert_weights, "dp", axis=2, tiled=True)
    blocks = exchange(dispatch(ids_t, tokens, upstream))
    route = jnp.concatenate([ids_t.astype(F32), gates.T], axis=0)
    route = lax.all_gather(route, "expert", axis=0, tiled=False)
    places, dense = lookup(expert_ids, gates)
    route, places, dense = lax.optimization_barrier((route, places, dense))
    rw_t = router_weight.T
    xe, hot, gu, add, gg, share = forward(host_arr, route, blocks, weights)
    shares = exchange(share)
    rows = backward(host_arr, gu, add, rw_t, weights)
    piece, sums = router_part(shares, gg, hot, xe)
    piece, rows = lax.optimization_barrier((piece, rows))
    back = exchange(rows)
    everyone = lax.all_gather(piece.reshape(-1, 128), "dp", axis=0, tiled=False)
    column = jnp.sum(everyone, axis=0).reshape(per_host, model)
    column = lax.dynamic_slice_in_dim(column, part * group, part, 1)
    column, back = lax.optimization_barrier((column, back))
    columns = exchange(jnp.broadcast_to(column.reshape(1, -1), (HOSTS, per_host * part)))
    router_grad = columns.reshape(-1, part).T
    token_grad = combine(host_arr, places, dense, sums, rw_t, back)
    return (token_grad, router_grad)


def solution(mesh):
    in_specs = (
        P(("dp", "expert"), None),
        P(("dp", "expert"), None),
        P(("dp", "expert"), None),
        P(("dp", "expert"), None),
        P("expert", None, "dp", None),
        P(),
    )
    out_specs = (P(("dp", "expert"), None), P("dp", None))
    return jax.shard_map(body, mesh=mesh, in_specs=in_specs, out_specs=out_specs, check_vma=False)
```

```python
import functools

import jax
import jax.numpy as jnp
import numpy as np
from jax import lax
from jax.experimental import pallas as pl
from jax.experimental.pallas import tpu as pltpu
from jax.sharding import PartitionSpec as P

F32 = jnp.float32
BF = jnp.bfloat16
CAP = 20
SLOTS = 2 * CAP
HOSTS = 32
ROWS = HOSTS * SLOTS
BLOCK = 2 * SLOTS
TOKENS = 128


def slot_table():
    which = [0] * 16 + [1] * 16 + [0] * 4 + [1] * 4
    rank = list(range(16)) + list(range(16)) + list(range(16, 20)) + list(range(16, 20))
    return np.array(which), np.array(rank)


WHICH, RANK = slot_table()


def strict(rows, cols, upper):
    a = lax.broadcasted_iota(jnp.int32, (rows, cols), 0)
    b = lax.broadcasted_iota(jnp.int32, (rows, cols), 1)
    return jnp.where((a < b) if upper else (a > b), 1.0, 0.0).astype(BF)


def host_block(first, second):
    width = first.shape[-1]
    row = lax.broadcasted_iota(jnp.int32, (16, width), 0).astype(F32) + 1.0
    row8 = lax.broadcasted_iota(jnp.int32, (8, width), 0)
    mixed = jnp.where(
        row8 < 4, jnp.broadcast_to(first, (8, width)), jnp.broadcast_to(second, (8, width))
    )
    late = (row8 + jnp.where(row8 < 4, 17, 13)).astype(F32)
    return jnp.concatenate(
        [
            jnp.where(jnp.broadcast_to(first, (16, width)) == row, 1.0, 0.0),
            jnp.where(jnp.broadcast_to(second, (16, width)) == row, 1.0, 0.0),
            jnp.where(mixed == late, 1.0, 0.0),
        ],
        axis=0,
    )


def dispatch_kernel(ids_ref, x_ref, dy_ref, out_ref, hot_ref):
    experts, tokens = 2 * HOSTS, x_ref.shape[0]
    hosts = out_ref.shape[0]

    @pl.when(pl.program_id(0) == 0)
    def _():
        column = lax.broadcasted_iota(jnp.int32, (experts, tokens), 0)
        member = jnp.zeros((experts, tokens), F32)
        for k in range(ids_ref.shape[0]):
            member += jnp.where(ids_ref[k : k + 1, :] == column, 1.0, 0.0)
        before = jnp.dot(
            member.astype(BF), strict(tokens, tokens, True), preferred_element_type=F32
        )
        order = jnp.where(member > 0.0, before + 1.0, 0.0)
        for pair in range(HOSTS // 2):
            blocks = [
                host_block(order[2 * h : 2 * h + 1], order[2 * h + 1 : 2 * h + 2])
                for h in (2 * pair, 2 * pair + 1)
            ]
            hot_ref[80 * pair : 80 * pair + 80, :] = jnp.concatenate(blocks, axis=0).astype(BF)

    rows = SLOTS * hosts
    hot = hot_ref[pl.ds(pl.multiple_of(pl.program_id(0) * rows, rows), rows), :]
    xs = jnp.dot(hot, x_ref[...], preferred_element_type=F32)
    ys = jnp.dot(hot, dy_ref[...], preferred_element_type=F32)
    for j in range(hosts):
        at = slice(SLOTS * j, SLOTS * j + SLOTS)
        out_ref[j] = jnp.concatenate([xs[at], ys[at]], axis=0).astype(BF)


def vmem():
    return pl.BlockSpec(memory_space=pltpu.VMEM)


def smem():
    return pl.BlockSpec(memory_space=pltpu.SMEM)


def params(mib):
    return pltpu.CompilerParams(vmem_limit_bytes=mib * 1024 * 1024)


def cost(flops, moved):
    return pl.CostEstimate(flops=flops, bytes_accessed=moved, transcendentals=0)


def dispatch(ids_t, tokens, upstream):
    steps = 4
    whole = lambda v: pl.BlockSpec(v.shape, lambda i: (0, 0))
    return pl.pallas_call(
        dispatch_kernel,
        grid=(steps,),
        out_shape=jax.ShapeDtypeStruct((HOSTS, BLOCK, tokens.shape[1]), BF),
        in_specs=[whole(ids_t), whole(tokens), whole(upstream)],
        out_specs=pl.BlockSpec((HOSTS // steps, BLOCK, tokens.shape[1]), lambda i: (i, 0, 0)),
        scratch_shapes=[pltpu.VMEM((ROWS, tokens.shape[0]), BF)],
        compiler_params=params(56),
        name="dispatch",
    )(ids_t, tokens, upstream)


def route_kernel(ids_ref, gates_ref, out_ref):
    route = jnp.concatenate([ids_ref[...].astype(F32), gates_ref[...]], axis=0)
    for h in range(out_ref.shape[0]):
        out_ref[h] = route


def routes(ids_t, gates_t):
    top, tokens = ids_t.shape
    return pl.pallas_call(
        route_kernel,
        out_shape=jax.ShapeDtypeStruct((HOSTS, 2 * top, tokens), F32),
        in_specs=[vmem(), vmem()],
        out_specs=vmem(),
        compiler_params=params(56),
        name="routes",
    )(ids_t, gates_t)


def pieces(a, b, start, e):
    at = start + 16 * e
    return jnp.concatenate(
        [a[at : at + 16], b[at : at + 16], a[start + 32 : start + 40], b[start + 32 : start + 40]],
        axis=0,
    ).astype(BF)


def prep_kernel(host_ref, route_ref, rows_ref, xe_ref, dye_ref, hot_ref, gcol_ref, gate_ref):
    sources = rows_ref.shape[0]
    pairs = sources // 2
    width = hot_ref.shape[3]
    for p in range(pairs):
        a, b = rows_ref[2 * p].astype(F32), rows_ref[2 * p + 1].astype(F32)
        for e in (0, 1):
            xe_ref[0, e, 48 * p : 48 * p + 48, :] = pieces(a, b, 0, e)
            dye_ref[0, e, 48 * p : 48 * p + 48, :] = pieces(a, b, SLOTS, e)
    ids = route_ref[:, 0:8, :]
    gates = route_ref[:, 8:16, :]
    upper = strict(width, width, True)
    host = host_ref[0]
    row8 = lax.broadcasted_iota(jnp.int32, (8, width), 0)
    row16 = lax.broadcasted_iota(jnp.int32, (16, width), 0).astype(F32) + 1.0
    spread = lambda v, n: jnp.broadcast_to(v, (n, width))
    for e in (0, 1):
        match = ids == (2 * host + e).astype(F32)
        member = jnp.sum(jnp.where(match, 1.0, 0.0), axis=1)
        gate = jnp.sum(jnp.where(match, gates, 0.0), axis=1)
        before = jnp.dot(member.astype(BF), upper, preferred_element_type=F32)
        order = jnp.where(member > 0.0, before + 1.0, 0.0)
        gate_ref[e] = gate
        if e == 0:
            late = jnp.where(row8 < 4, row8 + 17, -1).astype(F32)
        else:
            late = jnp.where(row8 < 4, -1, row8 + 13).astype(F32)
        for p in range(pairs):
            a, b = order[2 * p : 2 * p + 1], order[2 * p + 1 : 2 * p + 2]
            ga, gb = gate[2 * p : 2 * p + 1], gate[2 * p + 1 : 2 * p + 2]
            hot = jnp.concatenate(
                [
                    jnp.where(spread(a, 16) == row16, 1.0, 0.0),
                    jnp.where(spread(b, 16) == row16, 1.0, 0.0),
                    jnp.where(spread(a, 8) == late, 1.0, 0.0),
                    jnp.where(spread(b, 8) == late, 1.0, 0.0),
                ],
                axis=0,
            )
            weight = jnp.concatenate(
                [spread(ga, 16), spread(gb, 16), spread(ga, 8), spread(gb, 8)], axis=0
            )
            hot_ref[0, e, 48 * p : 48 * p + 48, :] = hot.astype(BF)
            gcol_ref[0, e, 48 * p : 48 * p + 48, :] = jnp.sum(hot * weight, axis=1, keepdims=True)


HALVES = 2
SOURCES = HOSTS // HALVES
COMPACT = SOURCES * 24


def compact_shape(last, kind):
    return jax.ShapeDtypeStruct((HALVES, 2, COMPACT, last), kind)


def compact_spec(last):
    return pl.BlockSpec((1, 2, COMPACT, last), lambda i: (i, 0, 0, 0))


def dense_shape():
    return jax.ShapeDtypeStruct((2, HOSTS, TOKENS), F32)


def dense_spec():
    return pl.BlockSpec((2, SOURCES, TOKENS), lambda i: (0, i, 0))


def prep(host, route, blocks):
    model = blocks.shape[2]
    return pl.pallas_call(
        prep_kernel,
        grid=(HALVES,),
        out_shape=(
            compact_shape(model, BF), compact_shape(model, BF), compact_shape(TOKENS, BF),
            compact_shape(1, F32), dense_shape(),
        ),
        in_specs=[
            smem(),
            pl.BlockSpec((SOURCES, 16, TOKENS), lambda i: (i, 0, 0)),
            pl.BlockSpec((SOURCES, BLOCK, model), lambda i: (i, 0, 0)),
        ],
        out_specs=(
            compact_spec(model), compact_spec(model), compact_spec(TOKENS),
            compact_spec(1), dense_spec(),
        ),
        compiler_params=params(56),
        cost_estimate=cost(1_000_000, 14_000_000),
        name="prep",
    )(host, route, blocks)


def forward_kernel(
    xe_ref, dye_ref, hot_ref, gcol_ref, gate_ref, w_ref, gu_ref, add_ref, gg_ref, share_ref,
):
    pairs = COMPACT // 48
    ff = w_ref.shape[2] // 3
    total = jnp.zeros(share_ref.shape[1:], F32)
    down = lambda v: jnp.sum(v, axis=0, keepdims=True)
    for e in (0, 1):
        pre = jnp.dot(xe_ref[0, e], w_ref[e, :, 0 : 2 * ff], preferred_element_type=F32)
        hidden_grad = jnp.dot(dye_ref[0, e], w_ref[e, :, 2 * ff :], preferred_element_type=F32)
        pre_gate, pre_up = pre[:, 0:ff], pre[:, ff:]
        sigma = jax.nn.sigmoid(pre_gate)
        active = pre_gate * sigma
        hidden = (active * pre_up).astype(BF).astype(F32)
        gg = jnp.sum(hidden_grad * hidden, axis=1, keepdims=True).astype(BF).astype(F32)
        gcol = gcol_ref[0, e]
        scaled = hidden_grad * gcol
        gu_ref[0, e, :, 0:ff] = (
            scaled * pre_up * sigma * (1.0 + pre_gate * (1.0 - sigma))
        ).astype(BF)
        gu_ref[0, e, :, ff:] = (scaled * active).astype(BF)
        add_ref[0, e] = gcol * gg
        for p in range(pairs):
            hit = hot_ref[0, e, 48 * p : 48 * p + 48, :].astype(F32) * gg[48 * p : 48 * p + 48]
            gg_ref[e, 2 * p : 2 * p + 1, :] = down(hit[0:16]) + down(hit[32:40])
            gg_ref[e, 2 * p + 1 : 2 * p + 2, :] = down(hit[16:32]) + down(hit[40:48])
        total = total + gate_ref[e] * gg_ref[e]
    total = total.astype(BF)
    for h in range(HOSTS):
        share_ref[h] = total


def forward(xe, dye, hot, gcol, gate, weights):
    _, model, triple = weights.shape
    return pl.pallas_call(
        forward_kernel,
        grid=(HALVES,),
        out_shape=(
            compact_shape(triple // 3 * 2, BF), compact_shape(1, F32), dense_shape(),
            jax.ShapeDtypeStruct((HOSTS, HOSTS, TOKENS), BF),
        ),
        in_specs=[
            compact_spec(model), compact_spec(model), compact_spec(TOKENS),
            compact_spec(1), dense_spec(),
            pl.BlockSpec(weights.shape, lambda i: (0, 0, 0)),
        ],
        out_specs=(
            compact_spec(triple // 3 * 2), compact_spec(1), dense_spec(),
            pl.BlockSpec((HOSTS, SOURCES, TOKENS), lambda i: (0, i, 0)),
        ),
        compiler_params=params(56),
        cost_estimate=cost(4 * HALVES * COMPACT * model * triple, 20_000_000),
        name="forward",
    )(xe, dye, hot, gcol, gate, weights)


def backward_kernel(host_ref, gu_ref, add_ref, rw_ref, w_ref, out_ref, re_ref):
    experts = rw_ref.shape[0]
    mine = lax.broadcasted_iota(jnp.int32, (8, experts), 0) + 2 * host_ref[0]
    pick = jnp.where(lax.broadcasted_iota(jnp.int32, (8, experts), 1) == mine, 1.0, 0.0)
    router = jnp.dot(pick.astype(BF), rw_ref[...], preferred_element_type=F32)
    for e in (0, 1):
        row = lax.dot_general(
            gu_ref[0, e], w_ref[e], (((1,), (1,)), ((), ())), preferred_element_type=F32
        )
        re_ref[e] = (row + add_ref[0, e] * router[e : e + 1]).astype(BF)
    for p in range(COMPACT // 48):
        r0 = re_ref[0, 48 * p : 48 * p + 48, :].astype(F32)
        r1 = re_ref[1, 48 * p : 48 * p + 48, :].astype(F32)
        out_ref[80 * p : 80 * p + 80, :] = jnp.concatenate(
            [
                r0[0:16], r1[0:16], r0[32:40] + r1[32:40],
                r0[16:32], r1[16:32], r0[40:48] + r1[40:48],
            ],
            axis=0,
        ).astype(BF)


def backward(host, gu, add, rw_t, weights):
    double = gu.shape[3]
    model = weights.shape[1]
    return pl.pallas_call(
        backward_kernel,
        grid=(HALVES,),
        out_shape=jax.ShapeDtypeStruct((ROWS, model), BF),
        in_specs=[
            smem(), compact_spec(double), compact_spec(1),
            pl.BlockSpec(rw_t.shape, lambda i: (0, 0)),
            pl.BlockSpec((2, model, double), lambda i: (0, 0, 0)),
        ],
        out_specs=pl.BlockSpec((ROWS // HALVES, model), lambda i: (i, 0)),
        scratch_shapes=[pltpu.VMEM((2, COMPACT, model), BF)],
        compiler_params=params(56),
        cost_estimate=cost(4 * HALVES * COMPACT * model * double, 10_000_000),
        name="backward",
    )(host, gu, add, rw_t, weights)


def router_kernel(shares_ref, gg_ref, gate_ref, hot_hbm, xe_hbm, part_ref, sum_ref, hot_ref, xe_ref, sems):
    copies = [
        pltpu.make_async_copy(hot_hbm, hot_ref, sems.at[0]),
        pltpu.make_async_copy(xe_hbm, xe_ref, sems.at[1]),
    ]
    for copy in copies:
        copy.start()
    total = shares_ref[0].astype(F32)
    for h in range(1, HOSTS):
        total = total + shares_ref[h].astype(F32)
    sum_ref[...] = total
    halves, _, compact, model = xe_ref.shape
    sources = HOSTS // halves
    source = lax.broadcasted_iota(jnp.int32, (sources, compact), 0)
    slot = lax.broadcasted_iota(jnp.int32, (sources, compact), 1) - 48 * (source >> 1)
    even = ((slot >= 0) & (slot < 16)) | ((slot >= 32) & (slot < 40))
    odd = ((slot >= 16) & (slot < 32)) | ((slot >= 40) & (slot < 48))
    own = ((source & 1) == 0) & even | ((source & 1) == 1) & odd
    for copy in copies:
        copy.wait()
    for e in (0, 1):
        logit = (gate_ref[e] * (gg_ref[e] - total)).astype(BF)
        part = jnp.zeros((8, model), F32)
        for i in range(halves):
            near = lax.dot_general(
                logit[sources * i : sources * i + sources], hot_ref[i, e],
                (((1,), (1,)), ((), ())), preferred_element_type=F32,
            )
            line = jnp.sum(jnp.where(own, near, 0.0), axis=0, keepdims=True)
            line = jnp.concatenate([line, jnp.zeros((7, compact), F32)], axis=0).astype(BF)
            part = part + jnp.dot(line, xe_ref[i, e], preferred_element_type=F32)
        part_ref[e : e + 1, :] = part[0:1]


def router_part(shares, gg, gate, hot, xe):
    return pl.pallas_call(
        router_kernel,
        out_shape=(
            jax.ShapeDtypeStruct((2, xe.shape[3]), F32),
            jax.ShapeDtypeStruct((HOSTS, gg.shape[2]), F32),
        ),
        in_specs=[vmem()] * 3 + [pl.BlockSpec(memory_space=pl.ANY)] * 2,
        out_specs=(vmem(), vmem()),
        scratch_shapes=[
            pltpu.VMEM(hot.shape, BF), pltpu.VMEM(xe.shape, BF), pltpu.SemaphoreType.DMA((2,)),
        ],
        compiler_params=params(16),
        cost_estimate=cost(64 * xe.size, 4_000_000),
        name="router_part",
    )(shares, gg, gate, hot, xe)


def lookup_kernel(ids_ref, gates_ref, expand_ref, rank_ref, hot_ref, dense_ref):
    tokens, top = ids_ref.shape
    experts = expand_ref.shape[0]
    column = lax.broadcasted_iota(jnp.int32, (tokens, experts), 1)
    member = jnp.zeros((tokens, experts), F32)
    dense = jnp.zeros((tokens, experts), F32)
    for k in range(top):
        match = ids_ref[:, k : k + 1] == column
        member += jnp.where(match, 1.0, 0.0)
        dense += jnp.where(match, gates_ref[:, k : k + 1], 0.0)
    before = jnp.dot(strict(tokens, tokens, False), member.astype(BF), preferred_element_type=F32)
    order = jnp.where(member > 0.0, before + 1.0, 0.0).astype(BF)
    wide = jnp.dot(order, expand_ref[...], preferred_element_type=F32)
    hot_ref[...] = jnp.where(wide == rank_ref[...], 1.0, 0.0).astype(BF)
    dense_ref[...] = dense


def lookup(ids, gates):
    slot = np.arange(ROWS)
    expert = 2 * (slot // SLOTS) + WHICH[slot % SLOTS]
    expand = (np.arange(2 * HOSTS)[:, None] == expert[None, :]).astype(np.float32)
    rank = (RANK[slot % SLOTS] + 1.0).astype(np.float32)[None, :]
    return pl.pallas_call(
        lookup_kernel,
        out_shape=(
            jax.ShapeDtypeStruct((ids.shape[0], ROWS), BF),
            jax.ShapeDtypeStruct((ids.shape[0], 2 * HOSTS), F32),
        ),
        in_specs=[vmem()] * 4,
        out_specs=(vmem(), vmem()),
        compiler_params=params(56),
        name="lookup",
    )(ids, gates, jnp.asarray(expand, BF), jnp.asarray(rank))


def combine_kernel(host_ref, hot_ref, dense_ref, sum_ref, rw_ref, rows_ref, out_ref):
    tokens = hot_ref.shape[0]
    own = jnp.broadcast_to(sum_ref[pl.ds(host_ref[0], 1), :], (tokens, tokens))
    diagonal = lax.broadcasted_iota(jnp.int32, (tokens, tokens), 0) == lax.broadcasted_iota(
        jnp.int32, (tokens, tokens), 1
    )
    own = jnp.sum(jnp.where(diagonal, own, 0.0), axis=1, keepdims=True)
    lost = jnp.dot((dense_ref[...] * own).astype(BF), rw_ref[...], preferred_element_type=F32)
    out = jnp.dot(hot_ref[...], rows_ref[...], preferred_element_type=F32)
    out_ref[...] = (out - lost).astype(BF)


def combine(host, hot, dense, sums, rw_t, rows):
    return pl.pallas_call(
        combine_kernel,
        out_shape=jax.ShapeDtypeStruct((hot.shape[0], rows.shape[1]), BF),
        in_specs=[smem()] + [vmem()] * 5,
        out_specs=vmem(),
        compiler_params=params(20),
        name="combine",
    )(host, hot, dense, sums, rw_t, rows)


def exchange(rows):
    return lax.all_to_all(rows, "expert", split_axis=0, concat_axis=0, tiled=True)


def body(tokens, upstream, expert_ids, gates, expert_weights, router_weight):
    model = tokens.shape[1]
    per_host, _, part, ff = expert_weights.shape
    host = lax.axis_index("expert").astype(jnp.int32)
    group = lax.axis_index("dp").astype(jnp.int32)
    host_arr = host.reshape(1)
    ids_t = expert_ids.T
    shard = expert_weights.transpose(0, 2, 1, 3).reshape(per_host, part, 3 * ff)
    weights = lax.all_gather(shard, "dp", axis=1, tiled=True)
    route = exchange(routes(ids_t, gates.T))
    sent = dispatch(ids_t, tokens, upstream)
    route, sent = lax.optimization_barrier((route, sent))
    blocks = exchange(sent)
    places, dense = lookup(expert_ids, gates)
    blocks, places, dense = lax.optimization_barrier((blocks, places, dense))
    rw_t = router_weight.T
    xe, dye, hot, gcol, gate = prep(host_arr, route, blocks)
    gu, add, gg, share = forward(xe, dye, hot, gcol, gate, weights)
    shares = exchange(share)
    rows = backward(host_arr, gu, add, rw_t, weights)
    piece, sums = router_part(shares, gg, gate, hot, xe)
    piece, rows = lax.optimization_barrier((piece, rows))
    back = exchange(rows)
    everyone = lax.all_gather(piece.reshape(-1, 128), "dp", axis=0, tiled=False)
    column = jnp.sum(everyone, axis=0).reshape(per_host, model)
    column = lax.dynamic_slice_in_dim(column, part * group, part, 1)
    column, back = lax.optimization_barrier((column, back))
    columns = exchange(jnp.broadcast_to(column.reshape(1, -1), (HOSTS, per_host * part)))
    router_grad = columns.reshape(-1, part).T
    token_grad = combine(host_arr, places, dense, sums, rw_t, back)
    return (token_grad, router_grad)


def solution(mesh):
    in_specs = (
        P(("dp", "expert"), None),
        P(("dp", "expert"), None),
        P(("dp", "expert"), None),
        P(("dp", "expert"), None),
        P("expert", None, "dp", None),
        P(),
    )
    out_specs = (P(("dp", "expert"), None), P("dp", None))
    return jax.shard_map(body, mesh=mesh, in_specs=in_specs, out_specs=out_specs, check_vma=False)
```

```python
import functools

import jax
import jax.numpy as jnp
import numpy as np
from jax import lax
from jax.experimental import pallas as pl
from jax.experimental.pallas import tpu as pltpu
from jax.sharding import PartitionSpec as P

F32 = jnp.float32
BF = jnp.bfloat16
CAP = 20
SLOTS = 2 * CAP
HOSTS = 32
ROWS = HOSTS * SLOTS
TILES = 8
SPAN = SLOTS * TILES
BLOCK = 2 * SPAN + 32
TOKENS = 128


def slot_table():
    which = [0] * 16 + [1] * 16 + [0] * 4 + [1] * 4
    rank = list(range(16)) + list(range(16)) + list(range(16, 20)) + list(range(16, 20))
    return np.array(which), np.array(rank)


WHICH, RANK = slot_table()


def strict(rows, cols, upper):
    a = lax.broadcasted_iota(jnp.int32, (rows, cols), 0)
    b = lax.broadcasted_iota(jnp.int32, (rows, cols), 1)
    return jnp.where((a < b) if upper else (a > b), 1.0, 0.0).astype(BF)


def host_block(first, second):
    width = first.shape[-1]
    row = lax.broadcasted_iota(jnp.int32, (16, width), 0).astype(F32) + 1.0
    row8 = lax.broadcasted_iota(jnp.int32, (8, width), 0)
    mixed = jnp.where(
        row8 < 4, jnp.broadcast_to(first, (8, width)), jnp.broadcast_to(second, (8, width))
    )
    late = (row8 + jnp.where(row8 < 4, 17, 13)).astype(F32)
    return jnp.concatenate(
        [
            jnp.where(jnp.broadcast_to(first, (16, width)) == row, 1.0, 0.0),
            jnp.where(jnp.broadcast_to(second, (16, width)) == row, 1.0, 0.0),
            jnp.where(mixed == late, 1.0, 0.0),
        ],
        axis=0,
    )


def to_tiles(rows):
    return [
        rows[8 * i : 8 * i + 8, 128 * j : 128 * j + 128]
        for i in range(rows.shape[0] // 8)
        for j in range(TILES)
    ]


def from_tiles(block, start, i):
    at = start + 64 * i
    return jnp.concatenate([block[at + 8 * j : at + 8 * j + 8] for j in range(TILES)], axis=1)


def dispatch_kernel(ids_ref, gates_ref, x_ref, dy_ref, out_ref, hot_ref):
    experts, tokens = 2 * HOSTS, x_ref.shape[0]
    hosts = out_ref.shape[0]

    @pl.when(pl.program_id(0) == 0)
    def _():
        column = lax.broadcasted_iota(jnp.int32, (experts, tokens), 0)
        member = jnp.zeros((experts, tokens), F32)
        for k in range(ids_ref.shape[0]):
            member += jnp.where(ids_ref[k : k + 1, :] == column, 1.0, 0.0)
        before = jnp.dot(
            member.astype(BF), strict(tokens, tokens, True), preferred_element_type=F32
        )
        order = jnp.where(member > 0.0, before + 1.0, 0.0)
        for pair in range(HOSTS // 2):
            blocks = [
                host_block(order[2 * h : 2 * h + 1], order[2 * h + 1 : 2 * h + 2])
                for h in (2 * pair, 2 * pair + 1)
            ]
            hot_ref[80 * pair : 80 * pair + 80, :] = jnp.concatenate(blocks, axis=0).astype(BF)

    rows = SLOTS * hosts
    hot = hot_ref[pl.ds(pl.multiple_of(pl.program_id(0) * rows, rows), rows), :]
    xs = jnp.dot(hot, x_ref[...], preferred_element_type=F32)
    ys = jnp.dot(hot, dy_ref[...], preferred_element_type=F32)
    left = gates_ref[...]
    route = [ids_ref[...].astype(F32)]
    for _ in range(3):
        high = left.astype(BF).astype(F32)
        route.append(high)
        left = left - high
    for j in range(hosts):
        at = slice(SLOTS * j, SLOTS * j + SLOTS)
        out_ref[j] = jnp.concatenate(to_tiles(xs[at]) + to_tiles(ys[at]) + route, axis=0).astype(BF)


def vmem():
    return pl.BlockSpec(memory_space=pltpu.VMEM)


def smem():
    return pl.BlockSpec(memory_space=pltpu.SMEM)


def params(mib):
    return pltpu.CompilerParams(vmem_limit_bytes=mib * 1024 * 1024)


def cost(flops, moved):
    return pl.CostEstimate(flops=flops, bytes_accessed=moved, transcendentals=0)


def dispatch(ids_t, gates_t, tokens, upstream):
    steps = 4
    whole = lambda v: pl.BlockSpec(v.shape, lambda i: (0, 0))
    return pl.pallas_call(
        dispatch_kernel,
        grid=(steps,),
        out_shape=jax.ShapeDtypeStruct((HOSTS, BLOCK, 128), BF),
        in_specs=[whole(ids_t), whole(gates_t), whole(tokens), whole(upstream)],
        out_specs=pl.BlockSpec((HOSTS // steps, BLOCK, 128), lambda i: (i, 0, 0)),
        scratch_shapes=[pltpu.VMEM((ROWS, tokens.shape[0]), BF)],
        compiler_params=params(56),
        name="dispatch",
    )(ids_t, gates_t, tokens, upstream)


def pieces(a, b, start, e):
    rows = [from_tiles(v, start, i) for v in (a, b) for i in (2 * e, 2 * e + 1)]
    rows += [from_tiles(v, start, 4) for v in (a, b)]
    return jnp.concatenate(rows, axis=0).astype(BF)


HALVES = 2
SOURCES = HOSTS // HALVES
COMPACT = SOURCES * 24


def compact_shape(last, kind):
    return jax.ShapeDtypeStruct((HALVES, 2, COMPACT, last), kind)


def compact_spec(last):
    return pl.BlockSpec((1, 2, COMPACT, last), lambda i: (i, 0, 0, 0))


def dense_shape():
    return jax.ShapeDtypeStruct((2, HOSTS, TOKENS), F32)


def dense_spec():
    return pl.BlockSpec((2, SOURCES, TOKENS), lambda i: (0, i, 0))


def forward_kernel(
    host_ref, rows_ref, w_ref,
    xe_ref, hot_ref, gu_ref, add_ref, gg_ref, gate_ref, share_ref,
    dye_ref, ids_ref, gates_ref, gcol_ref,
):
    sources = rows_ref.shape[0]
    pairs = sources // 2
    width = hot_ref.shape[3]
    ff = w_ref.shape[2] // 3
    for p in range(pairs):
        a, b = rows_ref[2 * p].astype(F32), rows_ref[2 * p + 1].astype(F32)
        for e in (0, 1):
            xe_ref[0, e, 48 * p : 48 * p + 48, :] = pieces(a, b, 0, e)
            dye_ref[e, 48 * p : 48 * p + 48, :] = pieces(a, b, SPAN, e)
        for n, v in ((2 * p, a), (2 * p + 1, b)):
            at = 2 * SPAN
            ids_ref[n] = v[at : at + 8]
            gates_ref[n] = v[at + 8 : at + 16] + v[at + 16 : at + 24] + v[at + 24 : at + 32]
    ids, gates = ids_ref[...], gates_ref[...]
    upper = strict(width, width, True)
    host = host_ref[0]
    row8 = lax.broadcasted_iota(jnp.int32, (8, width), 0)
    row16 = lax.broadcasted_iota(jnp.int32, (16, width), 0).astype(F32) + 1.0
    spread = lambda v, n: jnp.broadcast_to(v, (n, width))
    down = lambda v: jnp.sum(v, axis=0, keepdims=True)
    total = jnp.zeros((sources, width), F32)
    for e in (0, 1):
        match = ids == (2 * host + e).astype(F32)
        member = jnp.sum(jnp.where(match, 1.0, 0.0), axis=1)
        gate = jnp.sum(jnp.where(match, gates, 0.0), axis=1)
        before = jnp.dot(member.astype(BF), upper, preferred_element_type=F32)
        order = jnp.where(member > 0.0, before + 1.0, 0.0)
        gate_ref[e] = gate
        if e == 0:
            late = jnp.where(row8 < 4, row8 + 17, -1).astype(F32)
        else:
            late = jnp.where(row8 < 4, -1, row8 + 13).astype(F32)
        for p in range(pairs):
            a, b = order[2 * p : 2 * p + 1], order[2 * p + 1 : 2 * p + 2]
            ga, gb = gate[2 * p : 2 * p + 1], gate[2 * p + 1 : 2 * p + 2]
            hot = jnp.concatenate(
                [
                    jnp.where(spread(a, 16) == row16, 1.0, 0.0),
                    jnp.where(spread(b, 16) == row16, 1.0, 0.0),
                    jnp.where(spread(a, 8) == late, 1.0, 0.0),
                    jnp.where(spread(b, 8) == late, 1.0, 0.0),
                ],
                axis=0,
            )
            weight = jnp.concatenate(
                [spread(ga, 16), spread(gb, 16), spread(ga, 8), spread(gb, 8)], axis=0
            )
            hot_ref[0, e, 48 * p : 48 * p + 48, :] = hot.astype(BF)
            gcol_ref[e, 48 * p : 48 * p + 48, :] = jnp.sum(hot * weight, axis=1, keepdims=True)
        pre = jnp.dot(xe_ref[0, e], w_ref[e, :, 0 : 2 * ff], preferred_element_type=F32)
        hidden_grad = jnp.dot(dye_ref[e], w_ref[e, :, 2 * ff :], preferred_element_type=F32)
        pre_gate, pre_up = pre[:, 0:ff], pre[:, ff:]
        sigma = jax.nn.sigmoid(pre_gate)
        active = pre_gate * sigma
        hidden = (active * pre_up).astype(BF).astype(F32)
        gg = jnp.sum(hidden_grad * hidden, axis=1, keepdims=True).astype(BF).astype(F32)
        gcol = gcol_ref[e]
        scaled = hidden_grad * gcol
        gu_ref[0, e, :, 0:ff] = (
            scaled * pre_up * sigma * (1.0 + pre_gate * (1.0 - sigma))
        ).astype(BF)
        gu_ref[0, e, :, ff:] = (scaled * active).astype(BF)
        add_ref[0, e] = gcol * gg
        for p in range(pairs):
            hit = hot_ref[0, e, 48 * p : 48 * p + 48, :].astype(F32) * gg[48 * p : 48 * p + 48]
            gg_ref[e, 2 * p : 2 * p + 1, :] = down(hit[0:16]) + down(hit[32:40])
            gg_ref[e, 2 * p + 1 : 2 * p + 2, :] = down(hit[16:32]) + down(hit[40:48])
        total = total + gate * gg_ref[e]
    total = total.astype(BF)
    for h in range(HOSTS):
        share_ref[h] = total


def forward(host, blocks, weights):
    _, model, triple = weights.shape
    double = triple // 3 * 2
    return pl.pallas_call(
        forward_kernel,
        grid=(HALVES,),
        out_shape=(
            compact_shape(model, BF), compact_shape(TOKENS, BF), compact_shape(double, BF),
            compact_shape(1, F32), dense_shape(), dense_shape(),
            jax.ShapeDtypeStruct((HOSTS, HOSTS, TOKENS), BF),
        ),
        in_specs=[
            smem(),
            pl.BlockSpec((SOURCES, BLOCK, 128), lambda i: (i, 0, 0)),
            pl.BlockSpec(weights.shape, lambda i: (0, 0, 0)),
        ],
        out_specs=(
            compact_spec(model), compact_spec(TOKENS), compact_spec(double),
            compact_spec(1), dense_spec(), dense_spec(),
            pl.BlockSpec((HOSTS, SOURCES, TOKENS), lambda i: (0, i, 0)),
        ),
        scratch_shapes=[
            pltpu.VMEM((2, COMPACT, model), BF),
            pltpu.VMEM((SOURCES, 8, TOKENS), F32),
            pltpu.VMEM((SOURCES, 8, TOKENS), F32),
            pltpu.VMEM((2, COMPACT, 1), F32),
        ],
        compiler_params=params(56),
        cost_estimate=cost(4 * HALVES * COMPACT * model * triple, 20_000_000),
        name="forward",
    )(host, blocks, weights)


def backward_kernel(host_ref, gu_ref, add_ref, rw_ref, w_ref, out_ref, re_ref):
    experts = rw_ref.shape[0]
    mine = lax.broadcasted_iota(jnp.int32, (8, experts), 0) + 2 * host_ref[0]
    pick = jnp.where(lax.broadcasted_iota(jnp.int32, (8, experts), 1) == mine, 1.0, 0.0)
    router = jnp.dot(pick.astype(BF), rw_ref[...], preferred_element_type=F32)
    for e in (0, 1):
        row = lax.dot_general(
            gu_ref[0, e], w_ref[e], (((1,), (1,)), ((), ())), preferred_element_type=F32
        )
        re_ref[e] = (row + add_ref[0, e] * router[e : e + 1]).astype(BF)
    for p in range(COMPACT // 48):
        r0 = re_ref[0, 48 * p : 48 * p + 48, :].astype(F32)
        r1 = re_ref[1, 48 * p : 48 * p + 48, :].astype(F32)
        out_ref[80 * p : 80 * p + 80, :] = jnp.concatenate(
            [
                r0[0:16], r1[0:16], r0[32:40] + r1[32:40],
                r0[16:32], r1[16:32], r0[40:48] + r1[40:48],
            ],
            axis=0,
        ).astype(BF)


def backward(host, gu, add, rw_t, weights):
    double = gu.shape[3]
    model = weights.shape[1]
    return pl.pallas_call(
        backward_kernel,
        grid=(HALVES,),
        out_shape=jax.ShapeDtypeStruct((ROWS, model), BF),
        in_specs=[
            smem(), compact_spec(double), compact_spec(1),
            pl.BlockSpec(rw_t.shape, lambda i: (0, 0)),
            pl.BlockSpec((2, model, double), lambda i: (0, 0, 0)),
        ],
        out_specs=pl.BlockSpec((ROWS // HALVES, model), lambda i: (i, 0)),
        scratch_shapes=[pltpu.VMEM((2, COMPACT, model), BF)],
        compiler_params=params(56),
        cost_estimate=cost(4 * HALVES * COMPACT * model * double, 10_000_000),
        name="backward",
    )(host, gu, add, rw_t, weights)


def router_kernel(shares_ref, gg_ref, gate_ref, hot_hbm, xe_hbm, part_ref, sum_ref, hot_ref, xe_ref, sems):
    copies = [
        pltpu.make_async_copy(hot_hbm, hot_ref, sems.at[0]),
        pltpu.make_async_copy(xe_hbm, xe_ref, sems.at[1]),
    ]
    for copy in copies:
        copy.start()
    total = shares_ref[0].astype(F32)
    for h in range(1, HOSTS):
        total = total + shares_ref[h].astype(F32)
    sum_ref[...] = total
    halves, _, compact, model = xe_ref.shape
    sources = HOSTS // halves
    source = lax.broadcasted_iota(jnp.int32, (sources, compact), 0)
    slot = lax.broadcasted_iota(jnp.int32, (sources, compact), 1) - 48 * (source >> 1)
    even = ((slot >= 0) & (slot < 16)) | ((slot >= 32) & (slot < 40))
    odd = ((slot >= 16) & (slot < 32)) | ((slot >= 40) & (slot < 48))
    own = ((source & 1) == 0) & even | ((source & 1) == 1) & odd
    for copy in copies:
        copy.wait()
    for e in (0, 1):
        logit = (gate_ref[e] * (gg_ref[e] - total)).astype(BF)
        part = jnp.zeros((8, model), F32)
        for i in range(halves):
            near = lax.dot_general(
                logit[sources * i : sources * i + sources], hot_ref[i, e],
                (((1,), (1,)), ((), ())), preferred_element_type=F32,
            )
            line = jnp.sum(jnp.where(own, near, 0.0), axis=0, keepdims=True)
            line = jnp.concatenate([line, jnp.zeros((7, compact), F32)], axis=0).astype(BF)
            part = part + jnp.dot(line, xe_ref[i, e], preferred_element_type=F32)
        part_ref[e : e + 1, :] = part[0:1]


def router_part(shares, gg, gate, hot, xe):
    return pl.pallas_call(
        router_kernel,
        out_shape=(
            jax.ShapeDtypeStruct((2, xe.shape[3]), F32),
            jax.ShapeDtypeStruct((HOSTS, gg.shape[2]), F32),
        ),
        in_specs=[vmem()] * 3 + [pl.BlockSpec(memory_space=pl.ANY)] * 2,
        out_specs=(vmem(), vmem()),
        scratch_shapes=[
            pltpu.VMEM(hot.shape, BF), pltpu.VMEM(xe.shape, BF), pltpu.SemaphoreType.DMA((2,)),
        ],
        compiler_params=params(16),
        cost_estimate=cost(64 * xe.size, 4_000_000),
        name="router_part",
    )(shares, gg, gate, hot, xe)


def lookup_kernel(ids_ref, gates_ref, expand_ref, rank_ref, hot_ref, dense_ref):
    tokens, top = ids_ref.shape
    experts = expand_ref.shape[0]
    column = lax.broadcasted_iota(jnp.int32, (tokens, experts), 1)
    member = jnp.zeros((tokens, experts), F32)
    dense = jnp.zeros((tokens, experts), F32)
    for k in range(top):
        match = ids_ref[:, k : k + 1] == column
        member += jnp.where(match, 1.0, 0.0)
        dense += jnp.where(match, gates_ref[:, k : k + 1], 0.0)
    before = jnp.dot(strict(tokens, tokens, False), member.astype(BF), preferred_element_type=F32)
    order = jnp.where(member > 0.0, before + 1.0, 0.0).astype(BF)
    wide = jnp.dot(order, expand_ref[...], preferred_element_type=F32)
    hot_ref[...] = jnp.where(wide == rank_ref[...], 1.0, 0.0).astype(BF)
    dense_ref[...] = dense


def lookup(ids, gates):
    slot = np.arange(ROWS)
    expert = 2 * (slot // SLOTS) + WHICH[slot % SLOTS]
    expand = (np.arange(2 * HOSTS)[:, None] == expert[None, :]).astype(np.float32)
    rank = (RANK[slot % SLOTS] + 1.0).astype(np.float32)[None, :]
    return pl.pallas_call(
        lookup_kernel,
        out_shape=(
            jax.ShapeDtypeStruct((ids.shape[0], ROWS), BF),
            jax.ShapeDtypeStruct((ids.shape[0], 2 * HOSTS), F32),
        ),
        in_specs=[vmem()] * 4,
        out_specs=(vmem(), vmem()),
        compiler_params=params(56),
        name="lookup",
    )(ids, gates, jnp.asarray(expand, BF), jnp.asarray(rank))


def combine_kernel(host_ref, hot_ref, dense_ref, sum_ref, rw_ref, rows_ref, out_ref):
    tokens = hot_ref.shape[0]
    own = jnp.broadcast_to(sum_ref[pl.ds(host_ref[0], 1), :], (tokens, tokens))
    diagonal = lax.broadcasted_iota(jnp.int32, (tokens, tokens), 0) == lax.broadcasted_iota(
        jnp.int32, (tokens, tokens), 1
    )
    own = jnp.sum(jnp.where(diagonal, own, 0.0), axis=1, keepdims=True)
    lost = jnp.dot((dense_ref[...] * own).astype(BF), rw_ref[...], preferred_element_type=F32)
    out = jnp.dot(hot_ref[...], rows_ref[...], preferred_element_type=F32)
    out_ref[...] = (out - lost).astype(BF)


def combine(host, hot, dense, sums, rw_t, rows):
    return pl.pallas_call(
        combine_kernel,
        out_shape=jax.ShapeDtypeStruct((hot.shape[0], rows.shape[1]), BF),
        in_specs=[smem()] + [vmem()] * 5,
        out_specs=vmem(),
        compiler_params=params(20),
        name="combine",
    )(host, hot, dense, sums, rw_t, rows)


def exchange(rows):
    return lax.all_to_all(rows, "expert", split_axis=0, concat_axis=0, tiled=True)


def body(tokens, upstream, expert_ids, gates, expert_weights, router_weight):
    model = tokens.shape[1]
    per_host, _, part, ff = expert_weights.shape
    host = lax.axis_index("expert").astype(jnp.int32)
    group = lax.axis_index("dp").astype(jnp.int32)
    host_arr = host.reshape(1)
    ids_t = expert_ids.T
    shard = expert_weights.transpose(0, 2, 1, 3).reshape(per_host, part, 3 * ff)
    weights = lax.all_gather(shard, "dp", axis=1, tiled=True)
    blocks = exchange(dispatch(ids_t, gates.T, tokens, upstream))
    places, dense = lookup(expert_ids, gates)
    blocks, places, dense = lax.optimization_barrier((blocks, places, dense))
    rw_t = router_weight.T
    xe, hot, gu, add, gg, gate, share = forward(host_arr, blocks, weights)
    shares = exchange(share)
    rows = backward(host_arr, gu, add, rw_t, weights)
    piece, sums = router_part(shares, gg, gate, hot, xe)
    piece, rows = lax.optimization_barrier((piece, rows))
    back = exchange(rows)
    everyone = lax.all_gather(piece.reshape(-1, 128), "dp", axis=0, tiled=False)
    column = jnp.sum(everyone, axis=0).reshape(per_host, model)
    column = lax.dynamic_slice_in_dim(column, part * group, part, 1)
    column, back = lax.optimization_barrier((column, back))
    columns = exchange(jnp.broadcast_to(column.reshape(1, -1), (HOSTS, per_host * part)))
    router_grad = columns.reshape(-1, part).T
    token_grad = combine(host_arr, places, dense, sums, rw_t, back)
    return (token_grad, router_grad)


def solution(mesh):
    in_specs = (
        P(("dp", "expert"), None),
        P(("dp", "expert"), None),
        P(("dp", "expert"), None),
        P(("dp", "expert"), None),
        P("expert", None, "dp", None),
        P(),
    )
    out_specs = (P(("dp", "expert"), None), P("dp", None))
    return jax.shard_map(body, mesh=mesh, in_specs=in_specs, out_specs=out_specs, check_vma=False)
```

```python
import math

import jax
import jax.numpy as jnp
import numpy as np
from jax import lax
from jax.experimental import pallas as pl
from jax.experimental.pallas import tpu as pltpu
from jax.sharding import PartitionSpec as P

F32 = jnp.float32
BF = jnp.bfloat16
CAP = 20
SLOTS = 2 * CAP
HOSTS = 32
ROWS = HOSTS * SLOTS
TILES = 8
SPAN = SLOTS * TILES
BLOCK = 2 * SPAN + 32
TOKENS = 128


def slot_table():
    which = [0] * 16 + [1] * 16 + [0] * 4 + [1] * 4
    rank = list(range(16)) + list(range(16)) + list(range(16, 20)) + list(range(16, 20))
    return np.array(which), np.array(rank)


WHICH, RANK = slot_table()


def strict(rows, cols, upper):
    a = lax.broadcasted_iota(jnp.int32, (rows, cols), 0)
    b = lax.broadcasted_iota(jnp.int32, (rows, cols), 1)
    return jnp.where((a < b) if upper else (a > b), 1.0, 0.0).astype(BF)


def host_block(first, second):
    width = first.shape[-1]
    row = lax.broadcasted_iota(jnp.int32, (16, width), 0).astype(F32) + 1.0
    row8 = lax.broadcasted_iota(jnp.int32, (8, width), 0)
    mixed = jnp.where(
        row8 < 4, jnp.broadcast_to(first, (8, width)), jnp.broadcast_to(second, (8, width))
    )
    late = (row8 + jnp.where(row8 < 4, 17, 13)).astype(F32)
    return jnp.concatenate(
        [
            jnp.where(jnp.broadcast_to(first, (16, width)) == row, 1.0, 0.0),
            jnp.where(jnp.broadcast_to(second, (16, width)) == row, 1.0, 0.0),
            jnp.where(mixed == late, 1.0, 0.0),
        ],
        axis=0,
    )


def to_tiles(rows):
    return [
        rows[8 * i : 8 * i + 8, 128 * j : 128 * j + 128]
        for i in range(rows.shape[0] // 8)
        for j in range(TILES)
    ]


def from_tiles(block, start, i):
    at = start + 64 * i
    return jnp.concatenate([block[at + 8 * j : at + 8 * j + 8] for j in range(TILES)], axis=1)


def dispatch_kernel(ids_ref, gates_ref, x_ref, dy_ref, out_ref, hot_ref):
    experts, tokens = 2 * HOSTS, x_ref.shape[0]
    hosts = out_ref.shape[0]

    @pl.when(pl.program_id(0) == 0)
    def _():
        column = lax.broadcasted_iota(jnp.int32, (experts, tokens), 0)
        member = jnp.zeros((experts, tokens), F32)
        for k in range(ids_ref.shape[0]):
            member += jnp.where(ids_ref[k : k + 1, :] == column, 1.0, 0.0)
        before = jnp.dot(
            member.astype(BF), strict(tokens, tokens, True), preferred_element_type=F32
        )
        order = jnp.where(member > 0.0, before + 1.0, 0.0)
        for pair in range(HOSTS // 2):
            blocks = [
                host_block(order[2 * h : 2 * h + 1], order[2 * h + 1 : 2 * h + 2])
                for h in (2 * pair, 2 * pair + 1)
            ]
            hot_ref[80 * pair : 80 * pair + 80, :] = jnp.concatenate(blocks, axis=0).astype(BF)

    rows = SLOTS * hosts
    hot = hot_ref[pl.ds(pl.multiple_of(pl.program_id(0) * rows, rows), rows), :]
    xs = jnp.dot(hot, x_ref[...], preferred_element_type=F32)
    ys = jnp.dot(hot, dy_ref[...], preferred_element_type=F32)
    left = gates_ref[...]
    route = [ids_ref[...].astype(F32)]
    for _ in range(3):
        high = left.astype(BF).astype(F32)
        route.append(high)
        left = left - high
    for j in range(hosts):
        at = slice(SLOTS * j, SLOTS * j + SLOTS)
        out_ref[j] = jnp.concatenate(to_tiles(xs[at]) + to_tiles(ys[at]) + route, axis=0).astype(BF)


def vmem():
    return pl.BlockSpec(memory_space=pltpu.VMEM)


def smem():
    return pl.BlockSpec(memory_space=pltpu.SMEM)


def params(mib):
    return pltpu.CompilerParams(vmem_limit_bytes=mib * 1024 * 1024)


def cost(flops, moved):
    return pl.CostEstimate(flops=flops, bytes_accessed=moved, transcendentals=0)


def dispatch(ids_t, gates_t, tokens, upstream):
    steps = 4
    whole = lambda v: pl.BlockSpec(v.shape, lambda i: (0, 0))
    return pl.pallas_call(
        dispatch_kernel,
        grid=(steps,),
        out_shape=jax.ShapeDtypeStruct((HOSTS, BLOCK, 128), BF),
        in_specs=[whole(ids_t), whole(gates_t), whole(tokens), whole(upstream)],
        out_specs=pl.BlockSpec((HOSTS // steps, BLOCK, 128), lambda i: (i, 0, 0)),
        scratch_shapes=[pltpu.VMEM((ROWS, tokens.shape[0]), BF)],
        compiler_params=params(56),
        name="dispatch",
    )(ids_t, gates_t, tokens, upstream)


def pieces(a, b, start, e):
    rows = [from_tiles(v, start, i) for v in (a, b) for i in (2 * e, 2 * e + 1)]
    rows += [from_tiles(v, start, 4) for v in (a, b)]
    return jnp.concatenate(rows, axis=0).astype(BF)


HALVES = 2
SOURCES = HOSTS // HALVES
COMPACT = SOURCES * 24


def compact_shape(last, kind):
    return jax.ShapeDtypeStruct((HALVES, 2, COMPACT, last), kind)


def compact_spec(last):
    return pl.BlockSpec((1, 2, COMPACT, last), lambda i: (i, 0, 0, 0))


def dense_shape():
    return jax.ShapeDtypeStruct((2, HOSTS, TOKENS), F32)


def dense_spec():
    return pl.BlockSpec((2, SOURCES, TOKENS), lambda i: (0, i, 0))


def forward_kernel(
    host_ref, rows_ref, w_ref,
    xe_ref, hot_ref, gu_ref, add_ref, gg_ref, gate_ref, share_ref,
    dye_ref, ids_ref, gates_ref, gcol_ref,
):
    sources = rows_ref.shape[0]
    pairs = sources // 2
    width = hot_ref.shape[3]
    ff = w_ref.shape[2] // 3
    for p in range(pairs):
        a, b = rows_ref[2 * p].astype(F32), rows_ref[2 * p + 1].astype(F32)
        for e in (0, 1):
            xe_ref[0, e, 48 * p : 48 * p + 48, :] = pieces(a, b, 0, e)
            dye_ref[e, 48 * p : 48 * p + 48, :] = pieces(a, b, SPAN, e)
        for n, v in ((2 * p, a), (2 * p + 1, b)):
            at = 2 * SPAN
            ids_ref[n] = v[at : at + 8]
            gates_ref[n] = v[at + 8 : at + 16] + v[at + 16 : at + 24] + v[at + 24 : at + 32]
    ids, gates = ids_ref[...], gates_ref[...]
    upper = strict(width, width, True)
    host = host_ref[0]
    row8 = lax.broadcasted_iota(jnp.int32, (8, width), 0)
    row16 = lax.broadcasted_iota(jnp.int32, (16, width), 0).astype(F32) + 1.0
    spread = lambda v, n: jnp.broadcast_to(v, (n, width))
    down = lambda v: jnp.sum(v, axis=0, keepdims=True)
    total = jnp.zeros((sources, width), F32)
    for e in (0, 1):
        match = ids == (2 * host + e).astype(F32)
        member = jnp.sum(jnp.where(match, 1.0, 0.0), axis=1)
        gate = jnp.sum(jnp.where(match, gates, 0.0), axis=1)
        before = jnp.dot(member.astype(BF), upper, preferred_element_type=F32)
        order = jnp.where(member > 0.0, before + 1.0, 0.0)
        gate_ref[e] = gate
        if e == 0:
            late = jnp.where(row8 < 4, row8 + 17, -1).astype(F32)
        else:
            late = jnp.where(row8 < 4, -1, row8 + 13).astype(F32)
        for p in range(pairs):
            a, b = order[2 * p : 2 * p + 1], order[2 * p + 1 : 2 * p + 2]
            ga, gb = gate[2 * p : 2 * p + 1], gate[2 * p + 1 : 2 * p + 2]
            hot = jnp.concatenate(
                [
                    jnp.where(spread(a, 16) == row16, 1.0, 0.0),
                    jnp.where(spread(b, 16) == row16, 1.0, 0.0),
                    jnp.where(spread(a, 8) == late, 1.0, 0.0),
                    jnp.where(spread(b, 8) == late, 1.0, 0.0),
                ],
                axis=0,
            )
            weight = jnp.concatenate(
                [spread(ga, 16), spread(gb, 16), spread(ga, 8), spread(gb, 8)], axis=0
            )
            hot_ref[0, e, 48 * p : 48 * p + 48, :] = hot.astype(BF)
            gcol_ref[e, 48 * p : 48 * p + 48, :] = jnp.sum(hot * weight, axis=1, keepdims=True)
        pre = jnp.dot(xe_ref[0, e], w_ref[e, :, 0 : 2 * ff], preferred_element_type=F32)
        hidden_grad = jnp.dot(dye_ref[e], w_ref[e, :, 2 * ff :], preferred_element_type=F32)
        pre_gate, pre_up = pre[:, 0:ff], pre[:, ff:]
        sigma = jax.nn.sigmoid(pre_gate)
        active = pre_gate * sigma
        hidden = (active * pre_up).astype(BF).astype(F32)
        gg = jnp.sum(hidden_grad * hidden, axis=1, keepdims=True).astype(BF).astype(F32)
        gcol = gcol_ref[e]
        scaled = hidden_grad * gcol
        gu_ref[0, e, :, 0:ff] = (
            scaled * pre_up * sigma * (1.0 + pre_gate * (1.0 - sigma))
        ).astype(BF)
        gu_ref[0, e, :, ff:] = (scaled * active).astype(BF)
        add_ref[0, e] = gcol * gg
        for p in range(pairs):
            hit = hot_ref[0, e, 48 * p : 48 * p + 48, :].astype(F32) * gg[48 * p : 48 * p + 48]
            gg_ref[e, 2 * p : 2 * p + 1, :] = down(hit[0:16]) + down(hit[32:40])
            gg_ref[e, 2 * p + 1 : 2 * p + 2, :] = down(hit[16:32]) + down(hit[40:48])
        total = total + gate * gg_ref[e]
    total = total.astype(BF)
    for h in range(HOSTS):
        share_ref[h] = total


def forward(host, blocks, weights):
    _, model, triple = weights.shape
    double = triple // 3 * 2
    return pl.pallas_call(
        forward_kernel,
        grid=(HALVES,),
        out_shape=(
            compact_shape(model, BF), compact_shape(TOKENS, BF), compact_shape(double, BF),
            compact_shape(1, F32), dense_shape(), dense_shape(),
            jax.ShapeDtypeStruct((HOSTS, HOSTS, TOKENS), BF),
        ),
        in_specs=[
            smem(),
            pl.BlockSpec((SOURCES, BLOCK, 128), lambda i: (i, 0, 0)),
            pl.BlockSpec(weights.shape, lambda i: (0, 0, 0)),
        ],
        out_specs=(
            compact_spec(model), compact_spec(TOKENS), compact_spec(double),
            compact_spec(1), dense_spec(), dense_spec(),
            pl.BlockSpec((HOSTS, SOURCES, TOKENS), lambda i: (0, i, 0)),
        ),
        scratch_shapes=[
            pltpu.VMEM((2, COMPACT, model), BF),
            pltpu.VMEM((SOURCES, 8, TOKENS), F32),
            pltpu.VMEM((SOURCES, 8, TOKENS), F32),
            pltpu.VMEM((2, COMPACT, 1), F32),
        ],
        compiler_params=params(56),
        cost_estimate=cost(4 * HALVES * COMPACT * model * triple, 20_000_000),
        name="forward",
    )(host, blocks, weights)


def backward_kernel(host_ref, gu_ref, add_ref, rw_ref, w_ref, out_ref, re_ref):
    experts = rw_ref.shape[0]
    mine = lax.broadcasted_iota(jnp.int32, (8, experts), 0) + 2 * host_ref[0]
    pick = jnp.where(lax.broadcasted_iota(jnp.int32, (8, experts), 1) == mine, 1.0, 0.0)
    router = jnp.dot(pick.astype(BF), rw_ref[...], preferred_element_type=F32)
    for e in (0, 1):
        row = lax.dot_general(
            gu_ref[0, e], w_ref[e], (((1,), (1,)), ((), ())), preferred_element_type=F32
        )
        re_ref[e] = (row + add_ref[0, e] * router[e : e + 1]).astype(BF)
    for p in range(COMPACT // 48):
        r0 = re_ref[0, 48 * p : 48 * p + 48, :].astype(F32)
        r1 = re_ref[1, 48 * p : 48 * p + 48, :].astype(F32)
        out_ref[80 * p : 80 * p + 80, :] = jnp.concatenate(
            [
                r0[0:16], r1[0:16], r0[32:40] + r1[32:40],
                r0[16:32], r1[16:32], r0[40:48] + r1[40:48],
            ],
            axis=0,
        ).astype(BF)


def backward(host, gu, add, rw_t, weights):
    double = gu.shape[3]
    model = weights.shape[1]
    return pl.pallas_call(
        backward_kernel,
        grid=(HALVES,),
        out_shape=jax.ShapeDtypeStruct((ROWS, model), BF),
        in_specs=[
            smem(), compact_spec(double), compact_spec(1),
            pl.BlockSpec(rw_t.shape, lambda i: (0, 0)),
            pl.BlockSpec((2, model, double), lambda i: (0, 0, 0)),
        ],
        out_specs=pl.BlockSpec((ROWS // HALVES, model), lambda i: (i, 0)),
        scratch_shapes=[pltpu.VMEM((2, COMPACT, model), BF)],
        compiler_params=params(56),
        cost_estimate=cost(4 * HALVES * COMPACT * model * double, 10_000_000),
        name="backward",
    )(host, gu, add, rw_t, weights)


def router_kernel(shares_ref, gg_ref, gate_ref, hot_hbm, xe_hbm, part_ref, sum_ref, hot_ref, xe_ref, sems):
    copies = [
        pltpu.make_async_copy(hot_hbm, hot_ref, sems.at[0]),
        pltpu.make_async_copy(xe_hbm, xe_ref, sems.at[1]),
    ]
    for copy in copies:
        copy.start()
    total = shares_ref[0].astype(F32)
    for h in range(1, HOSTS):
        total = total + shares_ref[h].astype(F32)
    sum_ref[...] = total
    halves, _, compact, model = xe_ref.shape
    sources = HOSTS // halves
    source = lax.broadcasted_iota(jnp.int32, (sources, compact), 0)
    slot = lax.broadcasted_iota(jnp.int32, (sources, compact), 1) - 48 * (source >> 1)
    even = ((slot >= 0) & (slot < 16)) | ((slot >= 32) & (slot < 40))
    odd = ((slot >= 16) & (slot < 32)) | ((slot >= 40) & (slot < 48))
    own = ((source & 1) == 0) & even | ((source & 1) == 1) & odd
    for copy in copies:
        copy.wait()
    for e in (0, 1):
        logit = (gate_ref[e] * (gg_ref[e] - total)).astype(BF)
        part = jnp.zeros((8, model), F32)
        for i in range(halves):
            near = lax.dot_general(
                logit[sources * i : sources * i + sources], hot_ref[i, e],
                (((1,), (1,)), ((), ())), preferred_element_type=F32,
            )
            line = jnp.sum(jnp.where(own, near, 0.0), axis=0, keepdims=True)
            line = jnp.concatenate([line, jnp.zeros((7, compact), F32)], axis=0).astype(BF)
            part = part + jnp.dot(line, xe_ref[i, e], preferred_element_type=F32)
        part_ref[e : e + 1, :] = part[0:1]


def router_part(shares, gg, gate, hot, xe):
    return pl.pallas_call(
        router_kernel,
        out_shape=(
            jax.ShapeDtypeStruct((2, xe.shape[3]), F32),
            jax.ShapeDtypeStruct((HOSTS, gg.shape[2]), F32),
        ),
        in_specs=[vmem()] * 3 + [pl.BlockSpec(memory_space=pl.ANY)] * 2,
        out_specs=(vmem(), vmem()),
        scratch_shapes=[
            pltpu.VMEM(hot.shape, BF), pltpu.VMEM(xe.shape, BF), pltpu.SemaphoreType.DMA((2,)),
        ],
        compiler_params=params(16),
        cost_estimate=cost(64 * xe.size, 4_000_000),
        name="router_part",
    )(shares, gg, gate, hot, xe)


def lookup_kernel(ids_ref, gates_ref, expand_ref, rank_ref, hot_ref, dense_ref):
    tokens, top = ids_ref.shape
    experts = expand_ref.shape[0]
    column = lax.broadcasted_iota(jnp.int32, (tokens, experts), 1)
    member = jnp.zeros((tokens, experts), F32)
    dense = jnp.zeros((tokens, experts), F32)
    for k in range(top):
        match = ids_ref[:, k : k + 1] == column
        member += jnp.where(match, 1.0, 0.0)
        dense += jnp.where(match, gates_ref[:, k : k + 1], 0.0)
    before = jnp.dot(strict(tokens, tokens, False), member.astype(BF), preferred_element_type=F32)
    order = jnp.where(member > 0.0, before + 1.0, 0.0).astype(BF)
    wide = jnp.dot(order, expand_ref[...], preferred_element_type=F32)
    hot_ref[...] = jnp.where(wide == rank_ref[...], 1.0, 0.0).astype(BF)
    dense_ref[...] = dense


def lookup(ids, gates):
    slot = np.arange(ROWS)
    expert = 2 * (slot // SLOTS) + WHICH[slot % SLOTS]
    expand = (np.arange(2 * HOSTS)[:, None] == expert[None, :]).astype(np.float32)
    rank = (RANK[slot % SLOTS] + 1.0).astype(np.float32)[None, :]
    return pl.pallas_call(
        lookup_kernel,
        out_shape=(
            jax.ShapeDtypeStruct((ids.shape[0], ROWS), BF),
            jax.ShapeDtypeStruct((ids.shape[0], 2 * HOSTS), F32),
        ),
        in_specs=[vmem()] * 4,
        out_specs=(vmem(), vmem()),
        compiler_params=params(56),
        name="lookup",
    )(ids, gates, jnp.asarray(expand, BF), jnp.asarray(rank))


def combine_kernel(host_ref, hot_ref, dense_ref, sum_ref, rw_ref, rows_ref, out_ref):
    tokens = hot_ref.shape[0]
    own = jnp.broadcast_to(sum_ref[pl.ds(host_ref[0], 1), :], (tokens, tokens))
    diagonal = lax.broadcasted_iota(jnp.int32, (tokens, tokens), 0) == lax.broadcasted_iota(
        jnp.int32, (tokens, tokens), 1
    )
    own = jnp.sum(jnp.where(diagonal, own, 0.0), axis=1, keepdims=True)
    lost = jnp.dot((dense_ref[...] * own).astype(BF), rw_ref[...], preferred_element_type=F32)
    out = jnp.dot(hot_ref[...], rows_ref[...], preferred_element_type=F32)
    out_ref[...] = (out - lost).astype(BF)


def combine(host, hot, dense, sums, rw_t, rows):
    return pl.pallas_call(
        combine_kernel,
        out_shape=jax.ShapeDtypeStruct((hot.shape[0], rows.shape[1]), BF),
        in_specs=[smem()] + [vmem()] * 5,
        out_specs=vmem(),
        compiler_params=params(20),
        name="combine",
    )(host, hot, dense, sums, rw_t, rows)


def exchange(rows):
    return lax.all_to_all(rows, "expert", split_axis=0, concat_axis=0, tiled=True)


def body(tokens, upstream, expert_ids, gates, expert_weights, router_weight):
    model = tokens.shape[1]
    per_host, _, part, ff = expert_weights.shape
    host = lax.axis_index("expert").astype(jnp.int32)
    group = lax.axis_index("dp").astype(jnp.int32)
    host_arr = host.reshape(1)
    ids_t = expert_ids.T
    shard = expert_weights.transpose(0, 2, 1, 3).reshape(per_host, part, 3 * ff)
    weights = lax.all_gather(shard, "dp", axis=1, tiled=True)
    blocks = exchange(dispatch(ids_t, gates.T, tokens, upstream))
    places, dense = lookup(expert_ids, gates)
    blocks, places, dense = lax.optimization_barrier((blocks, places, dense))
    rw_t = router_weight.T
    xe, hot, gu, add, gg, gate, share = forward(host_arr, blocks, weights)
    shares = exchange(share)
    rows = backward(host_arr, gu, add, rw_t, weights)
    piece, sums = router_part(shares, gg, gate, hot, xe)
    back = exchange(rows)
    side = math.isqrt(lax.axis_size("dp"))
    near = [[side * h + l for l in range(side)] for h in range(side)]
    far = [[side * h + l for h in range(side)] for l in range(side)]
    column = lax.psum(piece.reshape(-1, 128), "dp", axis_index_groups=near)
    column = lax.psum(column, "dp", axis_index_groups=far).reshape(per_host, model)
    column = lax.dynamic_slice_in_dim(column, part * group, part, 1)
    column, back = lax.optimization_barrier((column, back))
    columns = exchange(jnp.broadcast_to(column.reshape(1, -1), (HOSTS, per_host * part)))
    router_grad = columns.reshape(-1, part).T
    token_grad = combine(host_arr, places, dense, sums, rw_t, back)
    return (token_grad, router_grad)


def solution(mesh):
    in_specs = (
        P(("dp", "expert"), None),
        P(("dp", "expert"), None),
        P(("dp", "expert"), None),
        P(("dp", "expert"), None),
        P("expert", None, "dp", None),
        P(),
    )
    out_specs = (P(("dp", "expert"), None), P("dp", None))
    return jax.shard_map(body, mesh=mesh, in_specs=in_specs, out_specs=out_specs, check_vma=False)
```

```python
import math

import jax
import jax.numpy as jnp
import numpy as np
from jax import lax
from jax.experimental import pallas as pl
from jax.experimental.pallas import tpu as pltpu
from jax.sharding import PartitionSpec as P

F32 = jnp.float32
BF = jnp.bfloat16
CAP = 20
SLOTS = 2 * CAP
HOSTS = 32
ROWS = HOSTS * SLOTS
TILES = 8
SPAN = SLOTS * TILES
BLOCK = 2 * SPAN + 16
TOKENS = 128


def slot_table():
    which = [0] * 16 + [1] * 16 + [0] * 4 + [1] * 4
    rank = list(range(16)) + list(range(16)) + list(range(16, 20)) + list(range(16, 20))
    return np.array(which), np.array(rank)


WHICH, RANK = slot_table()


def strict(rows, cols, upper):
    a = lax.broadcasted_iota(jnp.int32, (rows, cols), 0)
    b = lax.broadcasted_iota(jnp.int32, (rows, cols), 1)
    return jnp.where((a < b) if upper else (a > b), 1.0, 0.0).astype(BF)


def host_block(first, second):
    width = first.shape[-1]
    row = lax.broadcasted_iota(jnp.int32, (16, width), 0).astype(F32) + 1.0
    row8 = lax.broadcasted_iota(jnp.int32, (8, width), 0)
    mixed = jnp.where(
        row8 < 4, jnp.broadcast_to(first, (8, width)), jnp.broadcast_to(second, (8, width))
    )
    late = (row8 + jnp.where(row8 < 4, 17, 13)).astype(F32)
    return jnp.concatenate(
        [
            jnp.where(jnp.broadcast_to(first, (16, width)) == row, 1.0, 0.0),
            jnp.where(jnp.broadcast_to(second, (16, width)) == row, 1.0, 0.0),
            jnp.where(mixed == late, 1.0, 0.0),
        ],
        axis=0,
    )


def to_tiles(rows):
    return [
        rows[8 * i : 8 * i + 8, 128 * j : 128 * j + 128]
        for i in range(rows.shape[0] // 8)
        for j in range(TILES)
    ]


def from_tiles(block, start, i):
    at = start + 64 * i
    return jnp.concatenate([block[at + 8 * j : at + 8 * j + 8] for j in range(TILES)], axis=1)


def dispatch_kernel(ids_ref, gates_ref, x_ref, dy_ref, out_ref, hot_ref):
    experts, tokens = 2 * HOSTS, x_ref.shape[0]
    hosts = out_ref.shape[0]

    @pl.when(pl.program_id(0) == 0)
    def _():
        column = lax.broadcasted_iota(jnp.int32, (experts, tokens), 0)
        member = jnp.zeros((experts, tokens), F32)
        for k in range(ids_ref.shape[0]):
            member += jnp.where(ids_ref[k : k + 1, :] == column, 1.0, 0.0)
        before = jnp.dot(
            member.astype(BF), strict(tokens, tokens, True), preferred_element_type=F32
        )
        order = jnp.where(member > 0.0, before + 1.0, 0.0)
        for pair in range(HOSTS // 2):
            blocks = [
                host_block(order[2 * h : 2 * h + 1], order[2 * h + 1 : 2 * h + 2])
                for h in (2 * pair, 2 * pair + 1)
            ]
            hot_ref[80 * pair : 80 * pair + 80, :] = jnp.concatenate(blocks, axis=0).astype(BF)

    rows = SLOTS * hosts
    hot = hot_ref[pl.ds(pl.multiple_of(pl.program_id(0) * rows, rows), rows), :]
    xs = jnp.dot(hot, x_ref[...], preferred_element_type=F32)
    ys = jnp.dot(hot, dy_ref[...], preferred_element_type=F32)
    route = [ids_ref[...].astype(F32), gates_ref[...]]
    for j in range(hosts):
        at = slice(SLOTS * j, SLOTS * j + SLOTS)
        out_ref[j] = jnp.concatenate(to_tiles(xs[at]) + to_tiles(ys[at]) + route, axis=0).astype(BF)


def vmem():
    return pl.BlockSpec(memory_space=pltpu.VMEM)


def smem():
    return pl.BlockSpec(memory_space=pltpu.SMEM)


def params(mib):
    return pltpu.CompilerParams(vmem_limit_bytes=mib * 1024 * 1024)


def cost(flops, moved):
    return pl.CostEstimate(flops=flops, bytes_accessed=moved, transcendentals=0)


def dispatch(ids_t, gates_t, tokens, upstream):
    steps = 4
    whole = lambda v: pl.BlockSpec(v.shape, lambda i: (0, 0))
    return pl.pallas_call(
        dispatch_kernel,
        grid=(steps,),
        out_shape=jax.ShapeDtypeStruct((HOSTS, BLOCK, 128), BF),
        in_specs=[whole(ids_t), whole(gates_t), whole(tokens), whole(upstream)],
        out_specs=pl.BlockSpec((HOSTS // steps, BLOCK, 128), lambda i: (i, 0, 0)),
        scratch_shapes=[pltpu.VMEM((ROWS, tokens.shape[0]), BF)],
        compiler_params=params(56),
        name="dispatch",
    )(ids_t, gates_t, tokens, upstream)


def pieces(a, b, start, e):
    rows = [from_tiles(v, start, i) for v in (a, b) for i in (2 * e, 2 * e + 1)]
    rows += [from_tiles(v, start, 4) for v in (a, b)]
    return jnp.concatenate(rows, axis=0).astype(BF)


HALVES = 2
SOURCES = HOSTS // HALVES
COMPACT = SOURCES * 24


def compact_shape(last, kind):
    return jax.ShapeDtypeStruct((HALVES, 2, COMPACT, last), kind)


def compact_spec(last):
    return pl.BlockSpec((1, 2, COMPACT, last), lambda i: (i, 0, 0, 0))


def dense_shape():
    return jax.ShapeDtypeStruct((2, HOSTS, TOKENS), F32)


def dense_spec():
    return pl.BlockSpec((2, SOURCES, TOKENS), lambda i: (0, i, 0))


def forward_kernel(
    host_ref, rows_ref, w_ref,
    xe_ref, hot_ref, gu_ref, add_ref, gg_ref, gate_ref, share_ref,
    dye_ref, ids_ref, gates_ref, gcol_ref,
):
    sources = rows_ref.shape[0]
    pairs = sources // 2
    width = hot_ref.shape[3]
    ff = w_ref.shape[2] // 3
    for p in range(pairs):
        a, b = rows_ref[2 * p].astype(F32), rows_ref[2 * p + 1].astype(F32)
        for e in (0, 1):
            xe_ref[0, e, 48 * p : 48 * p + 48, :] = pieces(a, b, 0, e)
            dye_ref[e, 48 * p : 48 * p + 48, :] = pieces(a, b, SPAN, e)
        for n, v in ((2 * p, a), (2 * p + 1, b)):
            at = 2 * SPAN
            ids_ref[n] = v[at : at + 8]
            gates_ref[n] = v[at + 8 : at + 16]
    ids, gates = ids_ref[...], gates_ref[...]
    upper = strict(width, width, True)
    host = host_ref[0]
    row8 = lax.broadcasted_iota(jnp.int32, (8, width), 0)
    row16 = lax.broadcasted_iota(jnp.int32, (16, width), 0).astype(F32) + 1.0
    spread = lambda v, n: jnp.broadcast_to(v, (n, width))
    down = lambda v: jnp.sum(v, axis=0, keepdims=True)
    total = jnp.zeros((sources, width), F32)
    for e in (0, 1):
        match = ids == (2 * host + e).astype(F32)
        member = jnp.sum(jnp.where(match, 1.0, 0.0), axis=1)
        gate = jnp.sum(jnp.where(match, gates, 0.0), axis=1)
        before = jnp.dot(member.astype(BF), upper, preferred_element_type=F32)
        order = jnp.where(member > 0.0, before + 1.0, 0.0)
        gate_ref[e] = gate
        if e == 0:
            late = jnp.where(row8 < 4, row8 + 17, -1).astype(F32)
        else:
            late = jnp.where(row8 < 4, -1, row8 + 13).astype(F32)
        for p in range(pairs):
            a, b = order[2 * p : 2 * p + 1], order[2 * p + 1 : 2 * p + 2]
            ga, gb = gate[2 * p : 2 * p + 1], gate[2 * p + 1 : 2 * p + 2]
            hot = jnp.concatenate(
                [
                    jnp.where(spread(a, 16) == row16, 1.0, 0.0),
                    jnp.where(spread(b, 16) == row16, 1.0, 0.0),
                    jnp.where(spread(a, 8) == late, 1.0, 0.0),
                    jnp.where(spread(b, 8) == late, 1.0, 0.0),
                ],
                axis=0,
            )
            weight = jnp.concatenate(
                [spread(ga, 16), spread(gb, 16), spread(ga, 8), spread(gb, 8)], axis=0
            )
            hot_ref[0, e, 48 * p : 48 * p + 48, :] = hot.astype(BF)
            gcol_ref[e, 48 * p : 48 * p + 48, :] = jnp.sum(hot * weight, axis=1, keepdims=True)
        pre = jnp.dot(xe_ref[0, e], w_ref[e, :, 0 : 2 * ff], preferred_element_type=F32)
        hidden_grad = jnp.dot(dye_ref[e], w_ref[e, :, 2 * ff :], preferred_element_type=F32)
        pre_gate, pre_up = pre[:, 0:ff], pre[:, ff:]
        sigma = jax.nn.sigmoid(pre_gate)
        active = pre_gate * sigma
        hidden = (active * pre_up).astype(BF).astype(F32)
        gg = jnp.sum(hidden_grad * hidden, axis=1, keepdims=True).astype(BF).astype(F32)
        gcol = gcol_ref[e]
        scaled = hidden_grad * gcol
        gu_ref[0, e, :, 0:ff] = (
            scaled * pre_up * sigma * (1.0 + pre_gate * (1.0 - sigma))
        ).astype(BF)
        gu_ref[0, e, :, ff:] = (scaled * active).astype(BF)
        add_ref[0, e] = gcol * gg
        for p in range(pairs):
            hit = hot_ref[0, e, 48 * p : 48 * p + 48, :].astype(F32) * gg[48 * p : 48 * p + 48]
            gg_ref[e, 2 * p : 2 * p + 1, :] = down(hit[0:16]) + down(hit[32:40])
            gg_ref[e, 2 * p + 1 : 2 * p + 2, :] = down(hit[16:32]) + down(hit[40:48])
        total = total + gate * gg_ref[e]
    total = total.astype(BF)
    for h in range(HOSTS):
        share_ref[h] = total


def forward(host, blocks, weights):
    _, model, triple = weights.shape
    double = triple // 3 * 2
    return pl.pallas_call(
        forward_kernel,
        grid=(HALVES,),
        out_shape=(
            compact_shape(model, BF), compact_shape(TOKENS, BF), compact_shape(double, BF),
            compact_shape(1, F32), dense_shape(), dense_shape(),
            jax.ShapeDtypeStruct((HOSTS, HOSTS, TOKENS), BF),
        ),
        in_specs=[
            smem(),
            pl.BlockSpec((SOURCES, BLOCK, 128), lambda i: (i, 0, 0)),
            pl.BlockSpec(weights.shape, lambda i: (0, 0, 0)),
        ],
        out_specs=(
            compact_spec(model), compact_spec(TOKENS), compact_spec(double),
            compact_spec(1), dense_spec(), dense_spec(),
            pl.BlockSpec((HOSTS, SOURCES, TOKENS), lambda i: (0, i, 0)),
        ),
        scratch_shapes=[
            pltpu.VMEM((2, COMPACT, model), BF),
            pltpu.VMEM((SOURCES, 8, TOKENS), F32),
            pltpu.VMEM((SOURCES, 8, TOKENS), F32),
            pltpu.VMEM((2, COMPACT, 1), F32),
        ],
        compiler_params=params(56),
        cost_estimate=cost(4 * HALVES * COMPACT * model * triple, 20_000_000),
        name="forward",
    )(host, blocks, weights)


def backward_kernel(host_ref, gu_ref, add_ref, rw_ref, w_ref, out_ref, re_ref):
    experts = rw_ref.shape[0]
    mine = lax.broadcasted_iota(jnp.int32, (8, experts), 0) + 2 * host_ref[0]
    pick = jnp.where(lax.broadcasted_iota(jnp.int32, (8, experts), 1) == mine, 1.0, 0.0)
    router = jnp.dot(pick.astype(BF), rw_ref[...], preferred_element_type=F32)
    for e in (0, 1):
        row = lax.dot_general(
            gu_ref[0, e], w_ref[e], (((1,), (1,)), ((), ())), preferred_element_type=F32
        )
        re_ref[e] = (row + add_ref[0, e] * router[e : e + 1]).astype(BF)
    for p in range(COMPACT // 48):
        r0 = re_ref[0, 48 * p : 48 * p + 48, :].astype(F32)
        r1 = re_ref[1, 48 * p : 48 * p + 48, :].astype(F32)
        out_ref[80 * p : 80 * p + 80, :] = jnp.concatenate(
            [
                r0[0:16], r1[0:16], r0[32:40] + r1[32:40],
                r0[16:32], r1[16:32], r0[40:48] + r1[40:48],
            ],
            axis=0,
        ).astype(BF)


def backward(host, gu, add, rw_t, weights):
    double = gu.shape[3]
    model = weights.shape[1]
    return pl.pallas_call(
        backward_kernel,
        grid=(HALVES,),
        out_shape=jax.ShapeDtypeStruct((ROWS, model), BF),
        in_specs=[
            smem(), compact_spec(double), compact_spec(1),
            pl.BlockSpec(rw_t.shape, lambda i: (0, 0)),
            pl.BlockSpec((2, model, double), lambda i: (0, 0, 0)),
        ],
        out_specs=pl.BlockSpec((ROWS // HALVES, model), lambda i: (i, 0)),
        scratch_shapes=[pltpu.VMEM((2, COMPACT, model), BF)],
        compiler_params=params(56),
        cost_estimate=cost(4 * HALVES * COMPACT * model * double, 10_000_000),
        name="backward",
    )(host, gu, add, rw_t, weights)


def router_kernel(shares_ref, gg_ref, gate_ref, hot_hbm, xe_hbm, part_ref, sum_ref, hot_ref, xe_ref, sems):
    copies = [
        pltpu.make_async_copy(hot_hbm, hot_ref, sems.at[0]),
        pltpu.make_async_copy(xe_hbm, xe_ref, sems.at[1]),
    ]
    for copy in copies:
        copy.start()
    total = shares_ref[0].astype(F32)
    for h in range(1, HOSTS):
        total = total + shares_ref[h].astype(F32)
    sum_ref[...] = total
    halves, _, compact, model = xe_ref.shape
    sources = HOSTS // halves
    source = lax.broadcasted_iota(jnp.int32, (sources, compact), 0)
    slot = lax.broadcasted_iota(jnp.int32, (sources, compact), 1) - 48 * (source >> 1)
    even = ((slot >= 0) & (slot < 16)) | ((slot >= 32) & (slot < 40))
    odd = ((slot >= 16) & (slot < 32)) | ((slot >= 40) & (slot < 48))
    own = ((source & 1) == 0) & even | ((source & 1) == 1) & odd
    for copy in copies:
        copy.wait()
    for e in (0, 1):
        logit = (gate_ref[e] * (gg_ref[e] - total)).astype(BF)
        part = jnp.zeros((8, model), F32)
        for i in range(halves):
            near = lax.dot_general(
                logit[sources * i : sources * i + sources], hot_ref[i, e],
                (((1,), (1,)), ((), ())), preferred_element_type=F32,
            )
            line = jnp.sum(jnp.where(own, near, 0.0), axis=0, keepdims=True)
            line = jnp.concatenate([line, jnp.zeros((7, compact), F32)], axis=0).astype(BF)
            part = part + jnp.dot(line, xe_ref[i, e], preferred_element_type=F32)
        part_ref[e : e + 1, :] = part[0:1]


def router_part(shares, gg, gate, hot, xe):
    return pl.pallas_call(
        router_kernel,
        out_shape=(
            jax.ShapeDtypeStruct((2, xe.shape[3]), F32),
            jax.ShapeDtypeStruct((HOSTS, gg.shape[2]), F32),
        ),
        in_specs=[vmem()] * 3 + [pl.BlockSpec(memory_space=pl.ANY)] * 2,
        out_specs=(vmem(), vmem()),
        scratch_shapes=[
            pltpu.VMEM(hot.shape, BF), pltpu.VMEM(xe.shape, BF), pltpu.SemaphoreType.DMA((2,)),
        ],
        compiler_params=params(16),
        cost_estimate=cost(64 * xe.size, 4_000_000),
        name="router_part",
    )(shares, gg, gate, hot, xe)


def lookup_kernel(ids_ref, gates_ref, expand_ref, rank_ref, hot_ref, dense_ref):
    tokens, top = ids_ref.shape
    experts = expand_ref.shape[0]
    column = lax.broadcasted_iota(jnp.int32, (tokens, experts), 1)
    member = jnp.zeros((tokens, experts), F32)
    dense = jnp.zeros((tokens, experts), F32)
    for k in range(top):
        match = ids_ref[:, k : k + 1] == column
        member += jnp.where(match, 1.0, 0.0)
        dense += jnp.where(match, gates_ref[:, k : k + 1], 0.0)
    before = jnp.dot(strict(tokens, tokens, False), member.astype(BF), preferred_element_type=F32)
    order = jnp.where(member > 0.0, before + 1.0, 0.0).astype(BF)
    wide = jnp.dot(order, expand_ref[...], preferred_element_type=F32)
    hot_ref[...] = jnp.where(wide == rank_ref[...], 1.0, 0.0).astype(BF)
    dense_ref[...] = dense


def lookup(ids, gates):
    slot = np.arange(ROWS)
    expert = 2 * (slot // SLOTS) + WHICH[slot % SLOTS]
    expand = (np.arange(2 * HOSTS)[:, None] == expert[None, :]).astype(np.float32)
    rank = (RANK[slot % SLOTS] + 1.0).astype(np.float32)[None, :]
    return pl.pallas_call(
        lookup_kernel,
        out_shape=(
            jax.ShapeDtypeStruct((ids.shape[0], ROWS), BF),
            jax.ShapeDtypeStruct((ids.shape[0], 2 * HOSTS), F32),
        ),
        in_specs=[vmem()] * 4,
        out_specs=(vmem(), vmem()),
        compiler_params=params(56),
        name="lookup",
    )(ids, gates, jnp.asarray(expand, BF), jnp.asarray(rank))


def combine_kernel(host_ref, hot_ref, dense_ref, sum_ref, rw_ref, rows_ref, out_ref):
    tokens = hot_ref.shape[0]
    own = jnp.broadcast_to(sum_ref[pl.ds(host_ref[0], 1), :], (tokens, tokens))
    diagonal = lax.broadcasted_iota(jnp.int32, (tokens, tokens), 0) == lax.broadcasted_iota(
        jnp.int32, (tokens, tokens), 1
    )
    own = jnp.sum(jnp.where(diagonal, own, 0.0), axis=1, keepdims=True)
    lost = jnp.dot((dense_ref[...] * own).astype(BF), rw_ref[...], preferred_element_type=F32)
    out = jnp.dot(hot_ref[...], rows_ref[...], preferred_element_type=F32)
    out_ref[...] = (out - lost).astype(BF)


def combine(host, hot, dense, sums, rw_t, rows):
    return pl.pallas_call(
        combine_kernel,
        out_shape=jax.ShapeDtypeStruct((hot.shape[0], rows.shape[1]), BF),
        in_specs=[smem()] + [vmem()] * 5,
        out_specs=vmem(),
        compiler_params=params(20),
        name="combine",
    )(host, hot, dense, sums, rw_t, rows)


def layout_kernel(columns_ref, out_ref):
    hosts, both = columns_ref.shape
    part = both // 2
    turned = columns_ref[...].T
    row = lax.broadcasted_iota(jnp.int32, (hosts, 2 * hosts), 0)
    column = lax.broadcasted_iota(jnp.int32, (hosts, 2 * hosts), 1)
    out = jnp.zeros(out_ref.shape, F32)
    for e in (0, 1):
        out = out + jnp.dot(
            turned[part * e : part * e + part],
            jnp.where(column == 2 * row + e, 1.0, 0.0),
            precision=lax.Precision.HIGHEST,
            preferred_element_type=F32,
        )
    out_ref[...] = out


def layout(columns):
    hosts, both = columns.shape
    return pl.pallas_call(
        layout_kernel,
        out_shape=jax.ShapeDtypeStruct((both // 2, 2 * hosts), F32),
        in_specs=[vmem()],
        out_specs=vmem(),
        compiler_params=params(16),
        name="layout",
    )(columns)


def exchange(rows):
    return lax.all_to_all(rows, "expert", split_axis=0, concat_axis=0, tiled=True)


def body(tokens, upstream, expert_ids, gates, expert_weights, router_weight):
    model = tokens.shape[1]
    per_host, _, part, ff = expert_weights.shape
    host = lax.axis_index("expert").astype(jnp.int32)
    group = lax.axis_index("dp").astype(jnp.int32)
    host_arr = host.reshape(1)
    ids_t = expert_ids.T
    shard = expert_weights.transpose(0, 2, 1, 3).reshape(per_host, part, 3 * ff)
    weights = lax.all_gather(shard, "dp", axis=1, tiled=True)
    blocks = exchange(dispatch(ids_t, gates.T, tokens, upstream))
    places, dense = lookup(expert_ids, gates)
    blocks, places, dense = lax.optimization_barrier((blocks, places, dense))
    rw_t = router_weight.T
    xe, hot, gu, add, gg, gate, share = forward(host_arr, blocks, weights)
    shares = exchange(share)
    rows = backward(host_arr, gu, add, rw_t, weights)
    piece, sums = router_part(shares, gg, gate, hot, xe)
    back = exchange(rows)
    side = math.isqrt(lax.axis_size("dp"))
    near = [[side * h + l for l in range(side)] for h in range(side)]
    far = [[side * h + l for h in range(side)] for l in range(side)]
    column = lax.psum(piece.reshape(-1, 128), "dp", axis_index_groups=near)
    column = lax.psum(column, "dp", axis_index_groups=far).reshape(per_host, model)
    column = lax.dynamic_slice_in_dim(column, part * group, part, 1)
    column, back = lax.optimization_barrier((column, back))
    columns = exchange(jnp.broadcast_to(column.reshape(1, -1), (HOSTS, per_host * part)))
    router_grad = layout(columns)
    token_grad = combine(host_arr, places, dense, sums, rw_t, back)
    return (token_grad, router_grad)


def solution(mesh):
    in_specs = (
        P(("dp", "expert"), None),
        P(("dp", "expert"), None),
        P(("dp", "expert"), None),
        P(("dp", "expert"), None),
        P("expert", None, "dp", None),
        P(),
    )
    out_specs = (P(("dp", "expert"), None), P("dp", None))
    return jax.shard_map(body, mesh=mesh, in_specs=in_specs, out_specs=out_specs, check_vma=False)
```

```python
import math

import jax
import jax.numpy as jnp
import numpy as np
from jax import lax
from jax.experimental import pallas as pl
from jax.experimental.pallas import tpu as pltpu
from jax.sharding import PartitionSpec as P

F32 = jnp.float32
BF = jnp.bfloat16
CAP = 20
SLOTS = 2 * CAP
HOSTS = 32
ROWS = HOSTS * SLOTS
TILES = 8
SPAN = SLOTS * TILES
BLOCK = 2 * SPAN + 16
TOKENS = 128


def slot_table():
    which = [0] * 16 + [1] * 16 + [0] * 4 + [1] * 4
    rank = list(range(16)) + list(range(16)) + list(range(16, 20)) + list(range(16, 20))
    return np.array(which), np.array(rank)


WHICH, RANK = slot_table()


def strict(rows, cols, upper):
    a = lax.broadcasted_iota(jnp.int32, (rows, cols), 0)
    b = lax.broadcasted_iota(jnp.int32, (rows, cols), 1)
    return jnp.where((a < b) if upper else (a > b), 1.0, 0.0).astype(BF)


def host_block(first, second):
    width = first.shape[-1]
    row = lax.broadcasted_iota(jnp.int32, (16, width), 0).astype(F32) + 1.0
    row8 = lax.broadcasted_iota(jnp.int32, (8, width), 0)
    mixed = jnp.where(
        row8 < 4, jnp.broadcast_to(first, (8, width)), jnp.broadcast_to(second, (8, width))
    )
    late = (row8 + jnp.where(row8 < 4, 17, 13)).astype(F32)
    return jnp.concatenate(
        [
            jnp.where(jnp.broadcast_to(first, (16, width)) == row, 1.0, 0.0),
            jnp.where(jnp.broadcast_to(second, (16, width)) == row, 1.0, 0.0),
            jnp.where(mixed == late, 1.0, 0.0),
        ],
        axis=0,
    )


def to_tiles(rows):
    return [
        rows[8 * i : 8 * i + 8, 128 * j : 128 * j + 128]
        for i in range(rows.shape[0] // 8)
        for j in range(TILES)
    ]


def from_tiles(block, start, i):
    at = start + 64 * i
    return jnp.concatenate([block[at + 8 * j : at + 8 * j + 8] for j in range(TILES)], axis=1)


def dispatch_kernel(ids_ref, gates_ref, x_ref, dy_ref, out_ref, hot_ref):
    experts, tokens = 2 * HOSTS, x_ref.shape[0]
    hosts = out_ref.shape[0]

    @pl.when(pl.program_id(0) == 0)
    def _():
        column = lax.broadcasted_iota(jnp.int32, (experts, tokens), 0)
        member = jnp.zeros((experts, tokens), F32)
        for k in range(ids_ref.shape[0]):
            member += jnp.where(ids_ref[k : k + 1, :] == column, 1.0, 0.0)
        before = jnp.dot(
            member.astype(BF), strict(tokens, tokens, True), preferred_element_type=F32
        )
        order = jnp.where(member > 0.0, before + 1.0, 0.0)
        for pair in range(HOSTS // 2):
            blocks = [
                host_block(order[2 * h : 2 * h + 1], order[2 * h + 1 : 2 * h + 2])
                for h in (2 * pair, 2 * pair + 1)
            ]
            hot_ref[80 * pair : 80 * pair + 80, :] = jnp.concatenate(blocks, axis=0).astype(BF)

    rows = SLOTS * hosts
    hot = hot_ref[pl.ds(pl.multiple_of(pl.program_id(0) * rows, rows), rows), :]
    xs = jnp.dot(hot, x_ref[...], preferred_element_type=F32)
    ys = jnp.dot(hot, dy_ref[...], preferred_element_type=F32)
    route = [ids_ref[...].astype(F32), gates_ref[...]]
    for j in range(hosts):
        at = slice(SLOTS * j, SLOTS * j + SLOTS)
        out_ref[j] = jnp.concatenate(to_tiles(xs[at]) + to_tiles(ys[at]) + route, axis=0).astype(BF)


def vmem():
    return pl.BlockSpec(memory_space=pltpu.VMEM)


def smem():
    return pl.BlockSpec(memory_space=pltpu.SMEM)


def params(mib):
    return pltpu.CompilerParams(vmem_limit_bytes=mib * 1024 * 1024)


def cost(flops, moved):
    return pl.CostEstimate(flops=flops, bytes_accessed=moved, transcendentals=0)


def dispatch(ids_t, gates_t, tokens, upstream):
    steps = 4
    whole = lambda v: pl.BlockSpec(v.shape, lambda i: (0, 0))
    return pl.pallas_call(
        dispatch_kernel,
        grid=(steps,),
        out_shape=jax.ShapeDtypeStruct((HOSTS, BLOCK, 128), BF),
        in_specs=[whole(ids_t), whole(gates_t), whole(tokens), whole(upstream)],
        out_specs=pl.BlockSpec((HOSTS // steps, BLOCK, 128), lambda i: (i, 0, 0)),
        scratch_shapes=[pltpu.VMEM((ROWS, tokens.shape[0]), BF)],
        compiler_params=params(56),
        name="dispatch",
    )(ids_t, gates_t, tokens, upstream)


def pieces(a, b, start, e):
    rows = [from_tiles(v, start, i) for v in (a, b) for i in (2 * e, 2 * e + 1)]
    rows += [from_tiles(v, start, 4) for v in (a, b)]
    return jnp.concatenate(rows, axis=0).astype(BF)


HALVES = 2
SOURCES = HOSTS // HALVES
COMPACT = SOURCES * 24


def compact_shape(last, kind):
    return jax.ShapeDtypeStruct((HALVES, 2, COMPACT, last), kind)


def compact_spec(last):
    return pl.BlockSpec((1, 2, COMPACT, last), lambda i: (i, 0, 0, 0))


def dense_shape():
    return jax.ShapeDtypeStruct((2, HOSTS, TOKENS), F32)


def dense_spec():
    return pl.BlockSpec((2, SOURCES, TOKENS), lambda i: (0, i, 0))


def forward_kernel(
    host_ref, rows_ref, w_ref,
    xe_ref, hot_ref, gu_ref, add_ref, gg_ref, gate_ref, share_ref,
    dye_ref, ids_ref, gates_ref, gcol_ref,
):
    sources = rows_ref.shape[0]
    pairs = sources // 2
    width = hot_ref.shape[3]
    ff = w_ref.shape[2] // 3
    for p in range(pairs):
        a, b = rows_ref[2 * p].astype(F32), rows_ref[2 * p + 1].astype(F32)
        for e in (0, 1):
            xe_ref[0, e, 48 * p : 48 * p + 48, :] = pieces(a, b, 0, e)
            dye_ref[e, 48 * p : 48 * p + 48, :] = pieces(a, b, SPAN, e)
        for n, v in ((2 * p, a), (2 * p + 1, b)):
            at = 2 * SPAN
            ids_ref[n] = v[at : at + 8]
            gates_ref[n] = v[at + 8 : at + 16]
    ids, gates = ids_ref[...], gates_ref[...]
    upper = strict(width, width, True)
    host = host_ref[0]
    row8 = lax.broadcasted_iota(jnp.int32, (8, width), 0)
    row16 = lax.broadcasted_iota(jnp.int32, (16, width), 0).astype(F32) + 1.0
    spread = lambda v, n: jnp.broadcast_to(v, (n, width))
    down = lambda v: jnp.sum(v, axis=0, keepdims=True)
    total = jnp.zeros((sources, width), F32)
    for e in (0, 1):
        match = ids == (2 * host + e).astype(F32)
        member = jnp.sum(jnp.where(match, 1.0, 0.0), axis=1)
        gate = jnp.sum(jnp.where(match, gates, 0.0), axis=1)
        before = jnp.dot(member.astype(BF), upper, preferred_element_type=F32)
        order = jnp.where(member > 0.0, before + 1.0, 0.0)
        gate_ref[e] = gate
        if e == 0:
            late = jnp.where(row8 < 4, row8 + 17, -1).astype(F32)
        else:
            late = jnp.where(row8 < 4, -1, row8 + 13).astype(F32)
        for p in range(pairs):
            a, b = order[2 * p : 2 * p + 1], order[2 * p + 1 : 2 * p + 2]
            ga, gb = gate[2 * p : 2 * p + 1], gate[2 * p + 1 : 2 * p + 2]
            hot = jnp.concatenate(
                [
                    jnp.where(spread(a, 16) == row16, 1.0, 0.0),
                    jnp.where(spread(b, 16) == row16, 1.0, 0.0),
                    jnp.where(spread(a, 8) == late, 1.0, 0.0),
                    jnp.where(spread(b, 8) == late, 1.0, 0.0),
                ],
                axis=0,
            )
            weight = jnp.concatenate(
                [spread(ga, 16), spread(gb, 16), spread(ga, 8), spread(gb, 8)], axis=0
            )
            hot_ref[0, e, 48 * p : 48 * p + 48, :] = hot.astype(BF)
            gcol_ref[e, 48 * p : 48 * p + 48, :] = jnp.sum(hot * weight, axis=1, keepdims=True)
        pre = jnp.dot(xe_ref[0, e], w_ref[e, :, 0 : 2 * ff], preferred_element_type=F32)
        hidden_grad = jnp.dot(dye_ref[e], w_ref[e, :, 2 * ff :], preferred_element_type=F32)
        pre_gate, pre_up = pre[:, 0:ff], pre[:, ff:]
        sigma = jax.nn.sigmoid(pre_gate)
        active = pre_gate * sigma
        hidden = (active * pre_up).astype(BF).astype(F32)
        gg = jnp.sum(hidden_grad * hidden, axis=1, keepdims=True).astype(BF).astype(F32)
        gcol = gcol_ref[e]
        scaled = hidden_grad * gcol
        gu_ref[0, e, :, 0:ff] = (
            scaled * pre_up * sigma * (1.0 + pre_gate * (1.0 - sigma))
        ).astype(BF)
        gu_ref[0, e, :, ff:] = (scaled * active).astype(BF)
        add_ref[0, e] = gcol * gg
        for p in range(pairs):
            hit = hot_ref[0, e, 48 * p : 48 * p + 48, :].astype(F32) * gg[48 * p : 48 * p + 48]
            gg_ref[e, 2 * p : 2 * p + 1, :] = down(hit[0:16]) + down(hit[32:40])
            gg_ref[e, 2 * p + 1 : 2 * p + 2, :] = down(hit[16:32]) + down(hit[40:48])
        total = total + gate * gg_ref[e]
    total = total.astype(BF)
    for h in range(HOSTS):
        share_ref[h] = total


def forward(host, blocks, weights):
    _, model, triple = weights.shape
    double = triple // 3 * 2
    return pl.pallas_call(
        forward_kernel,
        grid=(HALVES,),
        out_shape=(
            compact_shape(model, BF), compact_shape(TOKENS, BF), compact_shape(double, BF),
            compact_shape(1, F32), dense_shape(), dense_shape(),
            jax.ShapeDtypeStruct((HOSTS, HOSTS, TOKENS), BF),
        ),
        in_specs=[
            smem(),
            pl.BlockSpec((SOURCES, BLOCK, 128), lambda i: (i, 0, 0)),
            pl.BlockSpec(weights.shape, lambda i: (0, 0, 0)),
        ],
        out_specs=(
            compact_spec(model), compact_spec(TOKENS), compact_spec(double),
            compact_spec(1), dense_spec(), dense_spec(),
            pl.BlockSpec((HOSTS, SOURCES, TOKENS), lambda i: (0, i, 0)),
        ),
        scratch_shapes=[
            pltpu.VMEM((2, COMPACT, model), BF),
            pltpu.VMEM((SOURCES, 8, TOKENS), F32),
            pltpu.VMEM((SOURCES, 8, TOKENS), F32),
            pltpu.VMEM((2, COMPACT, 1), F32),
        ],
        compiler_params=params(56),
        cost_estimate=cost(4 * HALVES * COMPACT * model * triple, 20_000_000),
        name="forward",
    )(host, blocks, weights)


def backward_kernel(host_ref, gu_ref, add_ref, rw_ref, w_ref, out_hbm, re_ref, out_ref, sems):
    expert = pl.program_id(0)
    experts = rw_ref.shape[0]
    mine = 2 * host_ref[0] + expert
    pick = jnp.where(lax.broadcasted_iota(jnp.int32, (8, experts), 1) == mine, 1.0, 0.0)
    router = jnp.dot(pick.astype(BF), rw_ref[...], preferred_element_type=F32)
    row = lax.dot_general(
        jnp.concatenate([gu_ref[0, 0], gu_ref[1, 0]], axis=0), w_ref[0],
        (((1,), (1,)), ((), ())), preferred_element_type=F32,
    )
    add = jnp.concatenate([add_ref[0, 0], add_ref[1, 0]], axis=0)
    re_ref[expert] = (row + add * router[0:1]).astype(BF)

    @pl.when(expert == 1)
    def _():
        chunks = sems.shape[0]
        pairs = HOSTS // 2 // chunks
        copies = []
        for c in range(chunks):
            for p in range(pairs * c, pairs * c + pairs):
                r0 = re_ref[0, 48 * p : 48 * p + 48, :].astype(F32)
                r1 = re_ref[1, 48 * p : 48 * p + 48, :].astype(F32)
                out_ref[80 * p : 80 * p + 80, :] = jnp.concatenate(
                    [
                        r0[0:16], r1[0:16], r0[32:40] + r1[32:40],
                        r0[16:32], r1[16:32], r0[40:48] + r1[40:48],
                    ],
                    axis=0,
                ).astype(BF)
            at = pl.ds(80 * pairs * c, 80 * pairs)
            copies.append(pltpu.make_async_copy(out_ref.at[at], out_hbm.at[at], sems.at[c]))
            copies[c].start()
        for copy in copies:
            copy.wait()


def backward(host, gu, add, rw_t, weights):
    double = gu.shape[3]
    model = weights.shape[1]
    one = lambda last: pl.BlockSpec((HALVES, 1, COMPACT, last), lambda e: (0, e, 0, 0))
    return pl.pallas_call(
        backward_kernel,
        grid=(2,),
        out_shape=jax.ShapeDtypeStruct((ROWS, model), BF),
        in_specs=[
            smem(), one(double), one(1),
            pl.BlockSpec(rw_t.shape, lambda e: (0, 0)),
            pl.BlockSpec((1, model, double), lambda e: (e, 0, 0)),
        ],
        out_specs=pl.BlockSpec(memory_space=pl.ANY),
        scratch_shapes=[
            pltpu.VMEM((2, HALVES * COMPACT, model), BF),
            pltpu.VMEM((ROWS, model), BF),
            pltpu.SemaphoreType.DMA((4,)),
        ],
        compiler_params=params(56),
        cost_estimate=cost(4 * HALVES * COMPACT * model * double, 10_000_000),
        name="backward",
    )(host, gu, add, rw_t, weights)


def router_kernel(shares_ref, gg_ref, gate_ref, hot_hbm, xe_hbm, part_ref, sum_ref, hot_ref, xe_ref, sems):
    copies = [
        pltpu.make_async_copy(hot_hbm, hot_ref, sems.at[0]),
        pltpu.make_async_copy(xe_hbm, xe_ref, sems.at[1]),
    ]
    for copy in copies:
        copy.start()
    total = shares_ref[0].astype(F32)
    for h in range(1, HOSTS):
        total = total + shares_ref[h].astype(F32)
    sum_ref[...] = total
    halves, _, compact, model = xe_ref.shape
    sources = HOSTS // halves
    source = lax.broadcasted_iota(jnp.int32, (sources, compact), 0)
    slot = lax.broadcasted_iota(jnp.int32, (sources, compact), 1) - 48 * (source >> 1)
    even = ((slot >= 0) & (slot < 16)) | ((slot >= 32) & (slot < 40))
    odd = ((slot >= 16) & (slot < 32)) | ((slot >= 40) & (slot < 48))
    own = ((source & 1) == 0) & even | ((source & 1) == 1) & odd
    for copy in copies:
        copy.wait()
    for e in (0, 1):
        logit = (gate_ref[e] * (gg_ref[e] - total)).astype(BF)
        part = jnp.zeros((8, model), F32)
        for i in range(halves):
            near = lax.dot_general(
                logit[sources * i : sources * i + sources], hot_ref[i, e],
                (((1,), (1,)), ((), ())), preferred_element_type=F32,
            )
            line = jnp.sum(jnp.where(own, near, 0.0), axis=0, keepdims=True)
            line = jnp.concatenate([line, jnp.zeros((7, compact), F32)], axis=0).astype(BF)
            part = part + jnp.dot(line, xe_ref[i, e], preferred_element_type=F32)
        part_ref[e : e + 1, :] = part[0:1]


def router_part(shares, gg, gate, hot, xe):
    return pl.pallas_call(
        router_kernel,
        out_shape=(
            jax.ShapeDtypeStruct((2, xe.shape[3]), F32),
            jax.ShapeDtypeStruct((HOSTS, gg.shape[2]), F32),
        ),
        in_specs=[vmem()] * 3 + [pl.BlockSpec(memory_space=pl.ANY)] * 2,
        out_specs=(vmem(), vmem()),
        scratch_shapes=[
            pltpu.VMEM(hot.shape, BF), pltpu.VMEM(xe.shape, BF), pltpu.SemaphoreType.DMA((2,)),
        ],
        compiler_params=params(16),
        cost_estimate=cost(64 * xe.size, 4_000_000),
        name="router_part",
    )(shares, gg, gate, hot, xe)


def lookup_kernel(ids_ref, gates_ref, expand_ref, rank_ref, hot_ref, dense_ref):
    tokens, top = ids_ref.shape
    experts = expand_ref.shape[0]
    column = lax.broadcasted_iota(jnp.int32, (tokens, experts), 1)
    member = jnp.zeros((tokens, experts), F32)
    dense = jnp.zeros((tokens, experts), F32)
    for k in range(top):
        match = ids_ref[:, k : k + 1] == column
        member += jnp.where(match, 1.0, 0.0)
        dense += jnp.where(match, gates_ref[:, k : k + 1], 0.0)
    before = jnp.dot(strict(tokens, tokens, False), member.astype(BF), preferred_element_type=F32)
    order = jnp.where(member > 0.0, before + 1.0, 0.0).astype(BF)
    wide = jnp.dot(order, expand_ref[...], preferred_element_type=F32)
    hot_ref[...] = jnp.where(wide == rank_ref[...], 1.0, 0.0).astype(BF)
    dense_ref[...] = dense


def lookup(ids, gates):
    slot = np.arange(ROWS)
    expert = 2 * (slot // SLOTS) + WHICH[slot % SLOTS]
    expand = (np.arange(2 * HOSTS)[:, None] == expert[None, :]).astype(np.float32)
    rank = (RANK[slot % SLOTS] + 1.0).astype(np.float32)[None, :]
    return pl.pallas_call(
        lookup_kernel,
        out_shape=(
            jax.ShapeDtypeStruct((ids.shape[0], ROWS), BF),
            jax.ShapeDtypeStruct((ids.shape[0], 2 * HOSTS), F32),
        ),
        in_specs=[vmem()] * 4,
        out_specs=(vmem(), vmem()),
        compiler_params=params(56),
        name="lookup",
    )(ids, gates, jnp.asarray(expand, BF), jnp.asarray(rank))


def combine_kernel(host_ref, hot_ref, dense_ref, sum_ref, rw_ref, rows_ref, out_ref):
    tokens = hot_ref.shape[0]
    own = jnp.broadcast_to(sum_ref[pl.ds(host_ref[0], 1), :], (tokens, tokens))
    diagonal = lax.broadcasted_iota(jnp.int32, (tokens, tokens), 0) == lax.broadcasted_iota(
        jnp.int32, (tokens, tokens), 1
    )
    own = jnp.sum(jnp.where(diagonal, own, 0.0), axis=1, keepdims=True)
    lost = jnp.dot((dense_ref[...] * own).astype(BF), rw_ref[...], preferred_element_type=F32)
    out = jnp.dot(hot_ref[...], rows_ref[...], preferred_element_type=F32)
    out_ref[...] = (out - lost).astype(BF)


def combine(host, hot, dense, sums, rw_t, rows):
    return pl.pallas_call(
        combine_kernel,
        out_shape=jax.ShapeDtypeStruct((hot.shape[0], rows.shape[1]), BF),
        in_specs=[smem()] + [vmem()] * 5,
        out_specs=vmem(),
        compiler_params=params(20),
        name="combine",
    )(host, hot, dense, sums, rw_t, rows)


def layout_kernel(columns_ref, out_ref):
    hosts, both = columns_ref.shape
    part = both // 2
    turned = columns_ref[...].T
    row = lax.broadcasted_iota(jnp.int32, (hosts, 2 * hosts), 0)
    column = lax.broadcasted_iota(jnp.int32, (hosts, 2 * hosts), 1)
    out = jnp.zeros(out_ref.shape, F32)
    for e in (0, 1):
        out = out + jnp.dot(
            turned[part * e : part * e + part],
            jnp.where(column == 2 * row + e, 1.0, 0.0),
            precision=lax.Precision.HIGHEST,
            preferred_element_type=F32,
        )
    out_ref[...] = out


def layout(columns):
    hosts, both = columns.shape
    return pl.pallas_call(
        layout_kernel,
        out_shape=jax.ShapeDtypeStruct((both // 2, 2 * hosts), F32),
        in_specs=[vmem()],
        out_specs=vmem(),
        compiler_params=params(16),
        name="layout",
    )(columns)


def exchange(rows):
    return lax.all_to_all(rows, "expert", split_axis=0, concat_axis=0, tiled=True)


def body(tokens, upstream, expert_ids, gates, expert_weights, router_weight):
    model = tokens.shape[1]
    per_host, _, part, ff = expert_weights.shape
    host = lax.axis_index("expert").astype(jnp.int32)
    group = lax.axis_index("dp").astype(jnp.int32)
    host_arr = host.reshape(1)
    ids_t = expert_ids.T
    shard = expert_weights.transpose(0, 2, 1, 3).reshape(per_host, part, 3 * ff)
    weights = lax.all_gather(shard, "dp", axis=1, tiled=True)
    blocks = exchange(dispatch(ids_t, gates.T, tokens, upstream))
    places, dense = lookup(expert_ids, gates)
    blocks, places, dense = lax.optimization_barrier((blocks, places, dense))
    rw_t = router_weight.T
    xe, hot, gu, add, gg, gate, share = forward(host_arr, blocks, weights)
    shares = exchange(share)
    rows = backward(host_arr, gu, add, rw_t, weights)
    piece, sums = router_part(shares, gg, gate, hot, xe)
    back = exchange(rows)
    side = math.isqrt(lax.axis_size("dp"))
    near = [[side * h + l for l in range(side)] for h in range(side)]
    far = [[side * h + l for h in range(side)] for l in range(side)]
    column = lax.psum(piece.reshape(-1, 128), "dp", axis_index_groups=near)
    column = lax.psum(column, "dp", axis_index_groups=far).reshape(per_host, model)
    column = lax.dynamic_slice_in_dim(column, part * group, part, 1)
    column, back = lax.optimization_barrier((column, back))
    columns = exchange(jnp.broadcast_to(column.reshape(1, -1), (HOSTS, per_host * part)))
    router_grad = layout(columns)
    token_grad = combine(host_arr, places, dense, sums, rw_t, back)
    return (token_grad, router_grad)


def solution(mesh):
    in_specs = (
        P(("dp", "expert"), None),
        P(("dp", "expert"), None),
        P(("dp", "expert"), None),
        P(("dp", "expert"), None),
        P("expert", None, "dp", None),
        P(),
    )
    out_specs = (P(("dp", "expert"), None), P("dp", None))
    return jax.shard_map(body, mesh=mesh, in_specs=in_specs, out_specs=out_specs, check_vma=False)
```

```python
import math

import jax
import jax.numpy as jnp
import numpy as np
from jax import lax
from jax.experimental import pallas as pl
from jax.experimental.pallas import tpu as pltpu
from jax.sharding import PartitionSpec as P

F32 = jnp.float32
BF = jnp.bfloat16
CAP = 20
SLOTS = 2 * CAP
HOSTS = 32
ROWS = HOSTS * SLOTS
TILES = 8
SPAN = SLOTS * TILES
BLOCK = 2 * SPAN + 16
TOKENS = 128


def slot_table():
    which = [0] * 16 + [1] * 16 + [0] * 4 + [1] * 4
    rank = list(range(16)) + list(range(16)) + list(range(16, 20)) + list(range(16, 20))
    return np.array(which), np.array(rank)


WHICH, RANK = slot_table()


def strict(rows, cols, upper):
    a = lax.broadcasted_iota(jnp.int32, (rows, cols), 0)
    b = lax.broadcasted_iota(jnp.int32, (rows, cols), 1)
    return jnp.where((a < b) if upper else (a > b), 1.0, 0.0).astype(BF)


def host_block(first, second):
    width = first.shape[-1]
    row = lax.broadcasted_iota(jnp.int32, (16, width), 0).astype(F32) + 1.0
    row8 = lax.broadcasted_iota(jnp.int32, (8, width), 0)
    mixed = jnp.where(
        row8 < 4, jnp.broadcast_to(first, (8, width)), jnp.broadcast_to(second, (8, width))
    )
    late = (row8 + jnp.where(row8 < 4, 17, 13)).astype(F32)
    return jnp.concatenate(
        [
            jnp.where(jnp.broadcast_to(first, (16, width)) == row, 1.0, 0.0),
            jnp.where(jnp.broadcast_to(second, (16, width)) == row, 1.0, 0.0),
            jnp.where(mixed == late, 1.0, 0.0),
        ],
        axis=0,
    )


def to_tiles(rows):
    return [
        rows[8 * i : 8 * i + 8, 128 * j : 128 * j + 128]
        for i in range(rows.shape[0] // 8)
        for j in range(TILES)
    ]


def from_tiles(block, start, i):
    at = start + 64 * i
    return jnp.concatenate([block[at + 8 * j : at + 8 * j + 8] for j in range(TILES)], axis=1)


def dispatch_kernel(ids_ref, gates_ref, x_ref, dy_ref, out_ref, hot_ref):
    experts, tokens = 2 * HOSTS, x_ref.shape[0]
    hosts = out_ref.shape[0]

    @pl.when(pl.program_id(0) == 0)
    def _():
        column = lax.broadcasted_iota(jnp.int32, (experts, tokens), 0)
        member = jnp.zeros((experts, tokens), F32)
        for k in range(ids_ref.shape[0]):
            member += jnp.where(ids_ref[k : k + 1, :] == column, 1.0, 0.0)
        before = jnp.dot(
            member.astype(BF), strict(tokens, tokens, True), preferred_element_type=F32
        )
        order = jnp.where(member > 0.0, before + 1.0, 0.0)
        for pair in range(HOSTS // 2):
            blocks = [
                host_block(order[2 * h : 2 * h + 1], order[2 * h + 1 : 2 * h + 2])
                for h in (2 * pair, 2 * pair + 1)
            ]
            hot_ref[80 * pair : 80 * pair + 80, :] = jnp.concatenate(blocks, axis=0).astype(BF)

    rows = SLOTS * hosts
    hot = hot_ref[pl.ds(pl.multiple_of(pl.program_id(0) * rows, rows), rows), :]
    xs = jnp.dot(hot, x_ref[...], preferred_element_type=F32)
    ys = jnp.dot(hot, dy_ref[...], preferred_element_type=F32)
    route = [ids_ref[...].astype(F32), gates_ref[...]]
    for j in range(hosts):
        at = slice(SLOTS * j, SLOTS * j + SLOTS)
        out_ref[j] = jnp.concatenate(to_tiles(xs[at]) + to_tiles(ys[at]) + route, axis=0).astype(BF)


def vmem():
    return pl.BlockSpec(memory_space=pltpu.VMEM)


def smem():
    return pl.BlockSpec(memory_space=pltpu.SMEM)


def params(mib):
    return pltpu.CompilerParams(vmem_limit_bytes=mib * 1024 * 1024)


def cost(flops, moved):
    return pl.CostEstimate(flops=flops, bytes_accessed=moved, transcendentals=0)


def dispatch(ids_t, gates_t, tokens, upstream):
    steps = 4
    whole = lambda v: pl.BlockSpec(v.shape, lambda i: (0, 0))
    return pl.pallas_call(
        dispatch_kernel,
        grid=(steps,),
        out_shape=jax.ShapeDtypeStruct((HOSTS, BLOCK, 128), BF),
        in_specs=[whole(ids_t), whole(gates_t), whole(tokens), whole(upstream)],
        out_specs=pl.BlockSpec((HOSTS // steps, BLOCK, 128), lambda i: (i, 0, 0)),
        scratch_shapes=[pltpu.VMEM((ROWS, tokens.shape[0]), BF)],
        compiler_params=params(56),
        name="dispatch",
    )(ids_t, gates_t, tokens, upstream)


def pieces(a, b, start, e):
    rows = [from_tiles(v, start, i) for v in (a, b) for i in (2 * e, 2 * e + 1)]
    rows += [from_tiles(v, start, 4) for v in (a, b)]
    return jnp.concatenate(rows, axis=0).astype(BF)


HALVES = 2
SOURCES = HOSTS // HALVES
COMPACT = SOURCES * 24


def compact_shape(last, kind):
    return jax.ShapeDtypeStruct((HALVES, 2, COMPACT, last), kind)


def compact_spec(last):
    return pl.BlockSpec((1, 2, COMPACT, last), lambda i: (i, 0, 0, 0))


def dense_shape():
    return jax.ShapeDtypeStruct((2, HOSTS, TOKENS), F32)


def dense_spec():
    return pl.BlockSpec((2, SOURCES, TOKENS), lambda i: (0, i, 0))


def forward_kernel(
    host_ref, rows_ref, w_ref,
    xe_ref, hot_ref, gu_ref, add_ref, gg_ref, gate_ref, share_ref,
    dye_ref, ids_ref, gates_ref, gcol_ref,
):
    sources = rows_ref.shape[0]
    pairs = sources // 2
    width = hot_ref.shape[3]
    ff = w_ref.shape[2] // 3
    for p in range(pairs):
        a, b = rows_ref[2 * p].astype(F32), rows_ref[2 * p + 1].astype(F32)
        for e in (0, 1):
            xe_ref[0, e, 48 * p : 48 * p + 48, :] = pieces(a, b, 0, e)
            dye_ref[e, 48 * p : 48 * p + 48, :] = pieces(a, b, SPAN, e)
        for n, v in ((2 * p, a), (2 * p + 1, b)):
            at = 2 * SPAN
            ids_ref[n] = v[at : at + 8]
            gates_ref[n] = v[at + 8 : at + 16]
    ids, gates = ids_ref[...], gates_ref[...]
    upper = strict(width, width, True)
    host = host_ref[0]
    row8 = lax.broadcasted_iota(jnp.int32, (8, width), 0)
    row16 = lax.broadcasted_iota(jnp.int32, (16, width), 0).astype(F32) + 1.0
    spread = lambda v, n: jnp.broadcast_to(v, (n, width))
    down = lambda v: jnp.sum(v, axis=0, keepdims=True)
    total = jnp.zeros((sources, width), F32)
    for e in (0, 1):
        match = ids == (2 * host + e).astype(F32)
        member = jnp.sum(jnp.where(match, 1.0, 0.0), axis=1)
        gate = jnp.sum(jnp.where(match, gates, 0.0), axis=1)
        before = jnp.dot(member.astype(BF), upper, preferred_element_type=F32)
        order = jnp.where(member > 0.0, before + 1.0, 0.0)
        gate_ref[e] = gate
        if e == 0:
            late = jnp.where(row8 < 4, row8 + 17, -1).astype(F32)
        else:
            late = jnp.where(row8 < 4, -1, row8 + 13).astype(F32)
        for p in range(pairs):
            a, b = order[2 * p : 2 * p + 1], order[2 * p + 1 : 2 * p + 2]
            ga, gb = gate[2 * p : 2 * p + 1], gate[2 * p + 1 : 2 * p + 2]
            hot = jnp.concatenate(
                [
                    jnp.where(spread(a, 16) == row16, 1.0, 0.0),
                    jnp.where(spread(b, 16) == row16, 1.0, 0.0),
                    jnp.where(spread(a, 8) == late, 1.0, 0.0),
                    jnp.where(spread(b, 8) == late, 1.0, 0.0),
                ],
                axis=0,
            )
            weight = jnp.concatenate(
                [spread(ga, 16), spread(gb, 16), spread(ga, 8), spread(gb, 8)], axis=0
            )
            hot_ref[0, e, 48 * p : 48 * p + 48, :] = hot.astype(BF)
            gcol_ref[e, 48 * p : 48 * p + 48, :] = jnp.sum(hot * weight, axis=1, keepdims=True)
        pre = jnp.dot(xe_ref[0, e], w_ref[e, :, 0 : 2 * ff], preferred_element_type=F32)
        hidden_grad = jnp.dot(dye_ref[e], w_ref[e, :, 2 * ff :], preferred_element_type=F32)
        pre_gate, pre_up = pre[:, 0:ff], pre[:, ff:]
        sigma = jax.nn.sigmoid(pre_gate)
        active = pre_gate * sigma
        hidden = (active * pre_up).astype(BF).astype(F32)
        gg = jnp.sum(hidden_grad * hidden, axis=1, keepdims=True).astype(BF).astype(F32)
        gcol = gcol_ref[e]
        scaled = hidden_grad * gcol
        gu_ref[0, e, :, 0:ff] = (
            scaled * pre_up * sigma * (1.0 + pre_gate * (1.0 - sigma))
        ).astype(BF)
        gu_ref[0, e, :, ff:] = (scaled * active).astype(BF)
        add_ref[0, e] = gcol * gg
        for p in range(pairs):
            hit = hot_ref[0, e, 48 * p : 48 * p + 48, :].astype(F32) * gg[48 * p : 48 * p + 48]
            gg_ref[e, 2 * p : 2 * p + 1, :] = down(hit[0:16]) + down(hit[32:40])
            gg_ref[e, 2 * p + 1 : 2 * p + 2, :] = down(hit[16:32]) + down(hit[40:48])
        total = total + gate * gg_ref[e]
    total = total.astype(BF)
    for h in range(HOSTS):
        share_ref[h] = total


def forward(host, blocks, weights):
    _, model, triple = weights.shape
    double = triple // 3 * 2
    return pl.pallas_call(
        forward_kernel,
        grid=(HALVES,),
        out_shape=(
            compact_shape(model, BF), compact_shape(TOKENS, BF), compact_shape(double, BF),
            compact_shape(1, F32), dense_shape(), dense_shape(),
            jax.ShapeDtypeStruct((HOSTS, HOSTS, TOKENS), BF),
        ),
        in_specs=[
            smem(),
            pl.BlockSpec((SOURCES, BLOCK, 128), lambda i: (i, 0, 0)),
            pl.BlockSpec(weights.shape, lambda i: (0, 0, 0)),
        ],
        out_specs=(
            compact_spec(model), compact_spec(TOKENS), compact_spec(double),
            compact_spec(1), dense_spec(), dense_spec(),
            pl.BlockSpec((HOSTS, SOURCES, TOKENS), lambda i: (0, i, 0)),
        ),
        scratch_shapes=[
            pltpu.VMEM((2, COMPACT, model), BF),
            pltpu.VMEM((SOURCES, 8, TOKENS), F32),
            pltpu.VMEM((SOURCES, 8, TOKENS), F32),
            pltpu.VMEM((2, COMPACT, 1), F32),
        ],
        compiler_params=params(56),
        cost_estimate=cost(4 * HALVES * COMPACT * model * triple, 20_000_000),
        name="forward",
    )(host, blocks, weights)


def backward_kernel(host_ref, gu_ref, add_ref, rw_ref, w_ref, out_ref, re_ref):
    experts = rw_ref.shape[0]
    mine = lax.broadcasted_iota(jnp.int32, (8, experts), 0) + 2 * host_ref[0]
    pick = jnp.where(lax.broadcasted_iota(jnp.int32, (8, experts), 1) == mine, 1.0, 0.0)
    router = jnp.dot(pick.astype(BF), rw_ref[...], preferred_element_type=F32)
    for e in (0, 1):
        row = lax.dot_general(
            gu_ref[0, e], w_ref[e], (((1,), (1,)), ((), ())), preferred_element_type=F32
        )
        re_ref[e] = (row + add_ref[0, e] * router[e : e + 1]).astype(BF)
    for p in range(COMPACT // 48):
        r0 = re_ref[0, 48 * p : 48 * p + 48, :].astype(F32)
        r1 = re_ref[1, 48 * p : 48 * p + 48, :].astype(F32)
        out_ref[80 * p : 80 * p + 80, :] = jnp.concatenate(
            [
                r0[0:16], r1[0:16], r0[32:40] + r1[32:40],
                r0[16:32], r1[16:32], r0[40:48] + r1[40:48],
            ],
            axis=0,
        ).astype(BF)


def backward(host, gu, add, rw_t, weights):
    double = gu.shape[3]
    model = weights.shape[1]
    return pl.pallas_call(
        backward_kernel,
        grid=(HALVES,),
        out_shape=jax.ShapeDtypeStruct((ROWS, model), BF),
        in_specs=[
            smem(), compact_spec(double), compact_spec(1),
            pl.BlockSpec(rw_t.shape, lambda i: (0, 0)),
            pl.BlockSpec((2, model, double), lambda i: (0, 0, 0)),
        ],
        out_specs=pl.BlockSpec((ROWS // HALVES, model), lambda i: (i, 0)),
        scratch_shapes=[pltpu.VMEM((2, COMPACT, model), BF)],
        compiler_params=params(56),
        cost_estimate=cost(4 * HALVES * COMPACT * model * double, 10_000_000),
        name="backward",
    )(host, gu, add, rw_t, weights)


def router_kernel(shares_ref, gg_ref, gate_ref, hot_hbm, xe_hbm, part_ref, sum_ref, hot_ref, xe_ref, sems):
    copies = [
        pltpu.make_async_copy(hot_hbm, hot_ref, sems.at[0]),
        pltpu.make_async_copy(xe_hbm, xe_ref, sems.at[1]),
    ]
    for copy in copies:
        copy.start()
    total = shares_ref[0].astype(F32)
    for h in range(1, HOSTS):
        total = total + shares_ref[h].astype(F32)
    sum_ref[...] = total
    halves, _, compact, model = xe_ref.shape
    sources = HOSTS // halves
    source = lax.broadcasted_iota(jnp.int32, (sources, compact), 0)
    slot = lax.broadcasted_iota(jnp.int32, (sources, compact), 1) - 48 * (source >> 1)
    even = ((slot >= 0) & (slot < 16)) | ((slot >= 32) & (slot < 40))
    odd = ((slot >= 16) & (slot < 32)) | ((slot >= 40) & (slot < 48))
    own = ((source & 1) == 0) & even | ((source & 1) == 1) & odd
    for copy in copies:
        copy.wait()
    for e in (0, 1):
        logit = (gate_ref[e] * (gg_ref[e] - total)).astype(BF)
        part = jnp.zeros((8, model), F32)
        for i in range(halves):
            near = lax.dot_general(
                logit[sources * i : sources * i + sources], hot_ref[i, e],
                (((1,), (1,)), ((), ())), preferred_element_type=F32,
            )
            line = jnp.sum(jnp.where(own, near, 0.0), axis=0, keepdims=True)
            line = jnp.concatenate([line, jnp.zeros((7, compact), F32)], axis=0).astype(BF)
            part = part + jnp.dot(line, xe_ref[i, e], preferred_element_type=F32)
        part_ref[e : e + 1, :] = part[0:1]


def router_part(shares, gg, gate, hot, xe):
    return pl.pallas_call(
        router_kernel,
        out_shape=(
            jax.ShapeDtypeStruct((2, xe.shape[3]), F32),
            jax.ShapeDtypeStruct((HOSTS, gg.shape[2]), F32),
        ),
        in_specs=[vmem()] * 3 + [pl.BlockSpec(memory_space=pl.ANY)] * 2,
        out_specs=(vmem(), vmem()),
        scratch_shapes=[
            pltpu.VMEM(hot.shape, BF), pltpu.VMEM(xe.shape, BF), pltpu.SemaphoreType.DMA((2,)),
        ],
        compiler_params=params(16),
        cost_estimate=cost(64 * xe.size, 4_000_000),
        name="router_part",
    )(shares, gg, gate, hot, xe)


def lookup_kernel(ids_ref, gates_ref, expand_ref, rank_ref, hot_ref, dense_ref):
    tokens, top = ids_ref.shape
    experts = expand_ref.shape[0]
    column = lax.broadcasted_iota(jnp.int32, (tokens, experts), 1)
    member = jnp.zeros((tokens, experts), F32)
    dense = jnp.zeros((tokens, experts), F32)
    for k in range(top):
        match = ids_ref[:, k : k + 1] == column
        member += jnp.where(match, 1.0, 0.0)
        dense += jnp.where(match, gates_ref[:, k : k + 1], 0.0)
    before = jnp.dot(strict(tokens, tokens, False), member.astype(BF), preferred_element_type=F32)
    order = jnp.where(member > 0.0, before + 1.0, 0.0).astype(BF)
    wide = jnp.dot(order, expand_ref[...], preferred_element_type=F32)
    hot_ref[...] = jnp.where(wide == rank_ref[...], 1.0, 0.0).astype(BF)
    dense_ref[...] = dense


def lookup(ids, gates):
    slot = np.arange(ROWS)
    expert = 2 * (slot // SLOTS) + WHICH[slot % SLOTS]
    expand = (np.arange(2 * HOSTS)[:, None] == expert[None, :]).astype(np.float32)
    rank = (RANK[slot % SLOTS] + 1.0).astype(np.float32)[None, :]
    return pl.pallas_call(
        lookup_kernel,
        out_shape=(
            jax.ShapeDtypeStruct((ids.shape[0], ROWS), BF),
            jax.ShapeDtypeStruct((ids.shape[0], 2 * HOSTS), F32),
        ),
        in_specs=[vmem()] * 4,
        out_specs=(vmem(), vmem()),
        compiler_params=params(56),
        name="lookup",
    )(ids, gates, jnp.asarray(expand, BF), jnp.asarray(rank))


def combine_kernel(host_ref, hot_ref, dense_ref, sum_ref, rw_ref, rows_ref, out_ref):
    tokens = hot_ref.shape[0]
    own = jnp.broadcast_to(sum_ref[pl.ds(host_ref[0], 1), :], (tokens, tokens))
    diagonal = lax.broadcasted_iota(jnp.int32, (tokens, tokens), 0) == lax.broadcasted_iota(
        jnp.int32, (tokens, tokens), 1
    )
    own = jnp.sum(jnp.where(diagonal, own, 0.0), axis=1, keepdims=True)
    lost = jnp.dot((dense_ref[...] * own).astype(BF), rw_ref[...], preferred_element_type=F32)
    out = jnp.dot(hot_ref[...], rows_ref[...], preferred_element_type=F32)
    out_ref[...] = (out - lost).astype(BF)


def combine(host, hot, dense, sums, rw_t, rows):
    return pl.pallas_call(
        combine_kernel,
        out_shape=jax.ShapeDtypeStruct((hot.shape[0], rows.shape[1]), BF),
        in_specs=[smem()] + [vmem()] * 5,
        out_specs=vmem(),
        compiler_params=params(20),
        name="combine",
    )(host, hot, dense, sums, rw_t, rows)


def layout_kernel(columns_ref, out_ref):
    hosts, both = columns_ref.shape
    part = both // 2
    turned = columns_ref[...].T
    row = lax.broadcasted_iota(jnp.int32, (hosts, 2 * hosts), 0)
    column = lax.broadcasted_iota(jnp.int32, (hosts, 2 * hosts), 1)
    out = jnp.zeros(out_ref.shape, F32)
    for e in (0, 1):
        out = out + jnp.dot(
            turned[part * e : part * e + part],
            jnp.where(column == 2 * row + e, 1.0, 0.0),
            precision=lax.Precision.HIGHEST,
            preferred_element_type=F32,
        )
    out_ref[...] = out


def layout(columns):
    hosts, both = columns.shape
    return pl.pallas_call(
        layout_kernel,
        out_shape=jax.ShapeDtypeStruct((both // 2, 2 * hosts), F32),
        in_specs=[vmem()],
        out_specs=vmem(),
        compiler_params=params(16),
        name="layout",
    )(columns)


def exchange(rows):
    return lax.all_to_all(rows, "expert", split_axis=0, concat_axis=0, tiled=True)


def body(tokens, upstream, expert_ids, gates, expert_weights, router_weight):
    per_host, _, part, ff = expert_weights.shape
    host = lax.axis_index("expert").astype(jnp.int32)
    group = lax.axis_index("dp").astype(jnp.int32)
    host_arr = host.reshape(1)
    ids_t = expert_ids.T
    shard = expert_weights.transpose(0, 2, 1, 3).reshape(per_host, part, 3 * ff)
    weights = lax.all_gather(shard, "dp", axis=1, tiled=True)
    blocks = exchange(dispatch(ids_t, gates.T, tokens, upstream))
    places, dense = lookup(expert_ids, gates)
    blocks, places, dense = lax.optimization_barrier((blocks, places, dense))
    rw_t = router_weight.T
    xe, hot, gu, add, gg, gate, share = forward(host_arr, blocks, weights)
    shares = exchange(share)
    rows = backward(host_arr, gu, add, rw_t, weights)
    piece, sums = router_part(shares, gg, gate, hot, xe)
    back = exchange(rows)
    side = math.isqrt(lax.axis_size("dp"))
    near = [[side * h + l for l in range(side)] for h in range(side)]
    far = [[side * h + l for h in range(side)] for l in range(side)]
    column = lax.psum(piece, "dp", axis_index_groups=near)
    column = lax.psum(column, "dp", axis_index_groups=far)
    column = lax.dynamic_slice_in_dim(column, part * group, part, 1)
    spread = jnp.broadcast_to(column.reshape(1, 1, -1), (HOSTS, 1, per_host * part))
    spread, back = lax.optimization_barrier((spread, back))
    columns = exchange(spread).reshape(HOSTS, per_host * part)
    router_grad = layout(columns)
    token_grad = combine(host_arr, places, dense, sums, rw_t, back)
    return (token_grad, router_grad)


def solution(mesh):
    in_specs = (
        P(("dp", "expert"), None),
        P(("dp", "expert"), None),
        P(("dp", "expert"), None),
        P(("dp", "expert"), None),
        P("expert", None, "dp", None),
        P(),
    )
    out_specs = (P(("dp", "expert"), None), P("dp", None))
    return jax.shard_map(body, mesh=mesh, in_specs=in_specs, out_specs=out_specs, check_vma=False)
```
